32 devices in a mesh: dom: 1, expert: 8 (over z, y), dp: 4 (over x, core).
Axes of the slice: x: 2, y: 2, z: 4, core: 2. Of those that a mesh axis runs over, the one named last changes fastest.
Arguments:
- tokens: bfloat16 [1024, 1024], P(('dom', 'expert', 'dp')), may hold values from -6 to 6
- cotangent: bfloat16 [1024, 1024], P(('dom', 'expert', 'dp')), may hold values from -1.5 to 1.5
- expert_ids: int32 [1024, 8], P(('dom', 'expert', 'dp')), may hold values from 0 to 15, all different within a row; in each aligned block of 32 rows (0 to 31, 32 to 63, ...) at most 32 rows name the same one
- gate_probs: bfloat16 [1024, 8], P(('dom', 'expert', 'dp')), may hold values from 0.019897461 to 0.25
- gate_half: bfloat16 [32, 512, 384], P(('dom', 'expert', 'dp')), may hold values from -0.1875 to 0.1875
- up_half: bfloat16 [32, 512, 384], P(('dom', 'expert', 'dp')), may hold values from -0.1875 to 0.1875
- down_half: bfloat16 [32, 384, 512], P(('dom', 'expert', 'dp')), may hold values from -0.3125 to 0.3125
Outputs:
- grad_tokens: bfloat16 [1024, 1024], P(('dom', 'expert', 'dp'))
- grad_gates: bfloat16 [1024, 8], P(('dom', 'expert', 'dp'))
- grad_gate_half: bfloat16 [32, 512, 384], P(('dom', 'expert', 'dp'))
- grad_up_half: bfloat16 [32, 512, 384], P(('dom', 'expert', 'dp'))
- grad_down_half: bfloat16 [32, 384, 512], P(('dom', 'expert', 'dp'))
The draws below stay inside these ranges and needn't reach their ends.
Inputs may be any that keep to these rules, and one draw needn't show every extreme that they name: `expert_ids`: each row names 8 different experts. In each aligned block of 32 rows (the rows of one device) no expert is named by more than 32 rows, a bound that some block reaches.
All inputs are finite; a program needn't handle non-finite values.
Results may differ from the reference program's by a relative error of at most 0.0064.
Values may be sent and summed in bfloat16 or wider, within the bound.
No kernel may reach another device: no remote copies, remote signals or barrier semaphores. Data moves between devices by JAX's collectives and lax.ppermute only.
A program may use at most 64 MiB of HBM per device.

```python
import math
import jax
import jax.numpy as jnp
import numpy as np
from jax import lax

D = 1024
F = 384
TOP = 8
TOK_DEV = 32
EXPERTS = 16
TOKENS = 1024
MOST = 32


def block_levels(rng, extent, split, least, high):
    gain = 1.0
    for position, blocks in split:
        draws = jax.random.uniform(jax.random.fold_in(jax.random.fold_in(rng, 6), position), (blocks,), jnp.float32, least / len(split), high / len(split))
        gain = gain * jnp.repeat(jnp.exp(draws), extent[position] // blocks).reshape((-1,) + (1,) * (len(extent) - 1 - position))
    return gain


def routed_block(rng, own, number, rows, number_of, top, limit, lean):
    order = jax.random.permutation(rng, number_of)
    crowded, usual = load_shares(number_of, rows * top, limit, lean, True), load_shares(number_of, rows * top, limit, lean, False)
    places = jnp.arange(number_of)

    def named(lengths, rotation):
        used = int((lengths > 0).sum())
        fixed = max(1, used // 4)
        shifted = fixed + (places - fixed + rotation * (used - fixed)) % max(1, number_of - fixed)
        return jnp.zeros((number_of,), jnp.int32).at[order[jnp.where(places < fixed, places, shifted)]].set(jnp.asarray(lengths, jnp.int32))

    lengths = jnp.where(number % 4 == 0, named(crowded, number // 4), named(usual, number - number // 4 - 1))
    mixed = jax.random.permutation(jax.random.fold_in(own, 3), number_of)
    donor, receiver = mixed[0:number_of // 2 * 2:2], mixed[1:number_of // 2 * 2:2]
    margin = jnp.minimum(lengths[donor] - 1, limit - lengths[receiver]) // 2
    margin = jnp.where((donor == order[0]) | (receiver == order[0]) | (lengths[receiver] == 0), 0, jnp.maximum(margin, 0))
    shifted = jax.random.randint(jax.random.fold_in(own, 4), (number_of // 2,), 0, 1 << 20) % (margin + 1)
    lengths = lengths.at[donor].add(-shifted).at[receiver].add(shifted)
    labels = jnp.searchsorted(jnp.cumsum(lengths), jnp.arange(rows * top), side="right").astype(jnp.int32)
    listing = labels.reshape(top, rows).T
    listing = listing[jax.random.permutation(jax.random.fold_in(own, 1), rows)]
    rotation = jax.random.randint(jax.random.fold_in(own, 2), (rows, 1), 0, top)
    return jnp.take_along_axis(listing, (jnp.arange(top)[None, :] + rotation) % top, axis=1)


def load_shares(amount, total, reach, skew, full):
    portions = [(1 << 20) // math.isqrt(standing ** skew) + 1 for standing in range(1, amount + 1)]
    largest = reach if full else min(reach, max(-(-total // amount), total * portions[0] // sum(portions)))
    least = 1 if total - largest >= amount - 1 else 0
    given, rest = [largest] + [least] * (amount - 1), total - largest - least * (amount - 1)
    while rest > 0:
        candidates = [i for i in range(1, amount) if given[i] < largest] or [i for i in range(1, amount) if given[i] < reach]
        mass, remaining = sum([portions[i] for i in candidates]), rest
        for i in candidates:
            more = min(reach - given[i], max(1, remaining * portions[i] // mass), rest)
            given[i] = given[i] + more
            rest = rest - more
    return np.array(given)


def centred(own_key, shape, scale, reach, split=(), kind=jnp.bfloat16):
    loudness = block_levels(own_key, shape, split, -0.22, 0.18) if split else 1.0
    drawn = jax.random.normal(own_key, shape, jnp.float32) * scale * loudness
    return jnp.minimum(jnp.maximum(drawn, -reach), reach).astype(kind)


def setup_inputs(seed: int = 0, part: int = 0) -> dict:
    streams_of = jax.random.split(jax.random.key(seed), 8)
    part_splits = jax.random.split(jax.random.fold_in(streams_of[7], part), 8)
    tokens = centred(part_splits[0], (TOKENS, D), 1.0, 6.0, ((0, 32),))
    cotangent = centred(part_splits[1], (TOKENS, D), 0.25, 1.5, ((0, 32),))
    expert_ids_keys = jax.random.split(jax.random.fold_in(part_splits[2], 1), TOKENS // TOK_DEV)
    expert_ids_turns = jax.random.permutation(jax.random.fold_in(part_splits[2], 3), TOKENS // TOK_DEV)
    expert_ids = jax.vmap(lambda own, number: routed_block(jax.random.fold_in(part_splits[2], 2), own, number, TOK_DEV, EXPERTS, TOP, MOST, 2))(expert_ids_keys, expert_ids_turns).reshape((TOKENS, TOP))
    gate_probs = jnp.clip(0.019897461 + 0.23010254 * jax.random.uniform(part_splits[3], (TOKENS, TOP), jnp.float32) ** block_levels(part_splits[3], (TOKENS, TOP), ((0, 32),), -0.2, 0.2), 0.019897461, 0.25).astype(jnp.bfloat16)
    gate_half = centred(part_splits[4], (2 * EXPERTS, D // 2, F), D ** -0.5, 0.1875, ((0, 32),))
    up_half = centred(part_splits[5], (2 * EXPERTS, D // 2, F), D ** -0.5, 0.1875, ((0, 32),))
    down_half = centred(part_splits[6], (2 * EXPERTS, F, D // 2), F ** -0.5, 0.3125, ((0, 32),))
    return dict(tokens=tokens, cotangent=cotangent, expert_ids=expert_ids, gate_probs=gate_probs, gate_half=gate_half, up_half=up_half, down_half=down_half)


def silu_parts(pre_gate):
    sigmoid_part = jax.nn.sigmoid(pre_gate)
    active = pre_gate * sigmoid_part
    slope_term = sigmoid_part * (1.0 + pre_gate * (1.0 - sigmoid_part))
    return active, slope_term


def expert_pass(expert_rows, expert_dys, expert_gates, gate_w, up_w, down_w):
    pre_gate = jnp.dot(expert_rows, gate_w, preferred_element_type=jnp.float32)
    pre_up = jnp.dot(expert_rows, up_w, preferred_element_type=jnp.float32)
    active, slope_term = silu_parts(pre_gate)
    hidden = (active * pre_up).astype(jnp.bfloat16)
    expert_out = jnp.dot(hidden, down_w, preferred_element_type=jnp.float32)
    gate_grads = jnp.sum(expert_dys.astype(jnp.float32) * expert_out, axis=1).astype(jnp.bfloat16)
    scaled = (expert_gates.astype(jnp.float32)[:, None] * expert_dys.astype(jnp.float32)).astype(jnp.bfloat16)
    grad_hidden = jnp.dot(scaled, down_w.T, preferred_element_type=jnp.float32)
    grad_up = (grad_hidden * active).astype(jnp.bfloat16)
    grad_gate = (grad_hidden * pre_up * slope_term).astype(jnp.bfloat16)
    row_grad = (jnp.dot(grad_gate, gate_w.T, preferred_element_type=jnp.float32)
                + jnp.dot(grad_up, up_w.T, preferred_element_type=jnp.float32)).astype(jnp.bfloat16)
    grad_gate_w = jnp.dot(expert_rows.T, grad_gate, preferred_element_type=jnp.float32)
    grad_up_w = jnp.dot(expert_rows.T, grad_up, preferred_element_type=jnp.float32)
    grad_down_w = jnp.dot(hidden.T, scaled, preferred_element_type=jnp.float32)
    return row_grad, gate_grads, grad_gate_w, grad_up_w, grad_down_w


def reference(tokens, cotangent, expert_ids, gate_probs, gate_half, up_half, down_half):
    blocks = TOKENS // TOK_DEV
    per_block = TOK_DEV * TOP
    gate_full = gate_half.reshape(EXPERTS, D, F)
    up_full = up_half.reshape(EXPERTS, D, F)
    down_full = down_half.reshape(EXPERTS, 2, F, D // 2).transpose(0, 2, 1, 3).reshape(EXPERTS, F, D)
    ids_block = expert_ids.reshape(blocks, per_block)
    onehot = (ids_block[:, :, None] == jnp.arange(EXPERTS, dtype=jnp.int32)[None, None, :]).astype(jnp.int32)
    rank_in = jnp.sum((jnp.cumsum(onehot, axis=1) - onehot) * onehot, axis=2).astype(jnp.int32)
    column = (jnp.arange(blocks, dtype=jnp.int32)[:, None] * MOST + rank_in).astype(jnp.int32)
    assignment = jnp.arange(blocks * per_block, dtype=jnp.int32).reshape(blocks, per_block)
    slot_table = jnp.full((EXPERTS, blocks * MOST), -1, jnp.int32).at[ids_block, column].set(assignment)
    flat_gates = gate_probs.reshape(-1)

    def one_expert(running, inputs):
        grad_acc, gate_acc = running
        slot_index, gate_w, up_w, down_w = inputs
        is_valid = slot_index >= 0
        safe_index = jnp.where(is_valid, slot_index, 0).astype(jnp.int32)
        token_index = (safe_index // TOP).astype(jnp.int32)
        expert_rows = jnp.where(is_valid[:, None], tokens[token_index], 0)
        expert_dys = jnp.where(is_valid[:, None], cotangent[token_index], 0)
        expert_gates = jnp.where(is_valid, flat_gates[safe_index], 0)
        row_grad, gate_grads, grad_gate_w, grad_up_w, grad_down_w = expert_pass(
            expert_rows, expert_dys, expert_gates, gate_w, up_w, down_w)
        grad_acc = grad_acc.at[token_index].add(jnp.where(is_valid[:, None], row_grad.astype(jnp.float32), 0.0))
        gate_acc = gate_acc.at[safe_index].add(jnp.where(is_valid, gate_grads.astype(jnp.float32), 0.0))
        return (grad_acc, gate_acc), (grad_gate_w.astype(jnp.bfloat16), grad_up_w.astype(jnp.bfloat16),
                                      grad_down_w.astype(jnp.bfloat16))

    initial = (jnp.zeros((TOKENS, D), jnp.float32), jnp.zeros((TOKENS * TOP,), jnp.float32))
    (grad_acc, gate_acc), (grad_gate_w, grad_up_w, grad_down_w) = lax.scan(
        one_expert, initial, (slot_table, gate_full, up_full, down_full))
    grad_tokens = grad_acc.astype(jnp.bfloat16)
    grad_gates = gate_acc.reshape(TOKENS, TOP).astype(jnp.bfloat16)
    grad_gate_half = grad_gate_w.reshape(2 * EXPERTS, D // 2, F)
    grad_up_half = grad_up_w.reshape(2 * EXPERTS, D // 2, F)
    grad_down_half = grad_down_w.reshape(EXPERTS, F, 2, D // 2).transpose(0, 2, 1, 3).reshape(2 * EXPERTS, F, D // 2)
    return (grad_tokens, grad_gates, grad_gate_half, grad_up_half, grad_down_half)
```

```python
import jax
import jax.numpy as jnp
from jax import lax
from jax.sharding import Mesh, PartitionSpec as P

CHIPS = ("expert", "chip")


def swap_core(x):
    return lax.ppermute(x, "core", [(0, 1), (1, 0)])


def body(tokens, cotangent, expert_ids, gate_probs, gate_half, up_half, down_half):
    f32, bf16 = jnp.float32, jnp.bfloat16
    chip_count = lax.axis_size("expert") * lax.axis_size("chip")
    tok_rows, feature_count = tokens.shape
    top_count = expert_ids.shape[1]
    half_width = feature_count // 2
    member = lax.axis_index("core")
    own_expert = lax.axis_index("expert") * lax.axis_size("chip") + lax.axis_index("chip")

    own_half = (gate_half[0], up_half[0], down_half[0])
    other_half = [swap_core(w) for w in own_half]
    is_lower = member == 0

    def join(own, other, axis):
        return jnp.concatenate(
            [jnp.where(is_lower, own, other), jnp.where(is_lower, other, own)], axis
        )

    gate_w, up_w, down_w = (
        join(own, other, axis) for own, other, axis in zip(own_half, other_half, (0, 0, 1))
    )

    experts = jnp.arange(chip_count, dtype=jnp.int32)
    named = expert_ids[:, :, None] == experts
    weight = jnp.sum(jnp.where(named, gate_probs.astype(f32)[:, :, None], 0.0), axis=1)
    lanes = -(-chip_count // 128) * 128
    weight = jnp.pad(weight, ((0, 0), (0, lanes - chip_count))).astype(bf16)

    rows = lax.all_gather(tokens, CHIPS, axis=0, tiled=True)
    dys_weight = lax.all_gather(
        jnp.concatenate([cotangent, weight], 1), CHIPS, axis=0, tiled=True
    )
    dys = dys_weight[:, :feature_count]
    is_own = jnp.arange(lanes, dtype=jnp.int32) == own_expert
    gates = jnp.sum(
        jnp.where(is_own, dys_weight[:, feature_count:].astype(f32), 0.0), 1, keepdims=True
    )

    pre_gate = jnp.dot(rows, gate_w, preferred_element_type=f32)
    pre_up = jnp.dot(rows, up_w, preferred_element_type=f32)
    sig = jax.nn.sigmoid(pre_gate)
    active = pre_gate * sig
    slope = sig * (1.0 + pre_gate * (1.0 - sig))
    hidden = active * pre_up
    back = lax.dot_general(dys, down_w, (((1,), (1,)), ((), ())), preferred_element_type=f32)
    gate_grads = jnp.sum(hidden * back, 1, keepdims=True)
    back = back * gates
    grad_up = (back * active).astype(bf16)
    grad_gate = (back * pre_up * slope).astype(bf16)
    row_grad = (
        lax.dot_general(grad_gate, gate_w, (((1,), (1,)), ((), ())), preferred_element_type=f32)
        + lax.dot_general(grad_up, up_w, (((1,), (1,)), ((), ())), preferred_element_type=f32)
    ).astype(bf16)
    hidden = (hidden * gates).astype(bf16)

    gate_cols = jnp.where(is_own, gate_grads, 0.0).astype(bf16)
    summed = lax.psum_scatter(
        jnp.concatenate([row_grad, gate_cols], 1), CHIPS, scatter_dimension=0, tiled=True
    )
    grad_tokens = summed[:, :feature_count]
    grad_gates = jnp.sum(
        jnp.where(named, summed[:, None, feature_count : feature_count + chip_count], 0), 2
    ).astype(bf16)

    across = (((0,), (0,)), ((), ()))
    grad_gate_w = lax.dot_general(rows, grad_gate, across, preferred_element_type=f32)
    grad_up_w = lax.dot_general(rows, grad_up, across, preferred_element_type=f32)
    grad_down_w = lax.dot_general(hidden, dys, across, preferred_element_type=f32)

    def settle(whole, axis):
        give = lax.dynamic_slice_in_dim(whole, (1 - member) * half_width, half_width, axis)
        keep = lax.dynamic_slice_in_dim(whole, member * half_width, half_width, axis)
        return (keep + swap_core(give.astype(bf16)).astype(f32)).astype(bf16)[None]

    return (
        grad_tokens,
        grad_gates,
        settle(grad_gate_w, 0),
        settle(grad_up_w, 0),
        settle(grad_down_w, 1),
    )


def solution(mesh):
    shape = mesh.shape
    devices = mesh.devices.reshape(shape["dom"], shape["expert"], shape["dp"] // 2, 2)
    fine = Mesh(devices, ("dom", "expert", "chip", "core"))
    every = ("dom", "expert", "chip", "core")
    flat, cube = P(every, None), P(every, None, None)
    return jax.shard_map(
        body,
        mesh=fine,
        in_specs=(flat, flat, flat, flat, cube, cube, cube),
        out_specs=(flat, flat, cube, cube, cube),
        check_vma=False,
    )
```

```python
import jax
import jax.numpy as jnp
from jax import lax
from jax.sharding import Mesh, PartitionSpec as P

DEVICES = ("expert", "chip", "core")


def swap_core(x):
    return lax.ppermute(x, "core", [(0, 1), (1, 0)])


def doubling_pairs(chip_count):
    bits = []
    bit = chip_count // 2
    while bit:
        bits.append(bit)
        bit //= 2
    orders = (bits[:-2] + bits[-2:][::-1], bits)
    return [
        [
            (2 * chip + core, 2 * (chip ^ orders[core][step]) + core)
            for chip in range(chip_count)
            for core in range(2)
        ]
        for step in range(len(bits))
    ]


def gather(block, steps):
    for pairs in steps:
        block = jnp.concatenate([block, lax.ppermute(block, DEVICES, pairs)], 0)
    return block


def scatter_sum(block, steps):
    for pairs in reversed(steps):
        half = block.shape[0] // 2
        given = lax.ppermute(block[half:], DEVICES, pairs)
        block = (block[:half].astype(jnp.float32) + given.astype(jnp.float32)).astype(block.dtype)
    return block


def body(tokens, cotangent, expert_ids, gate_probs, gate_half, up_half, down_half):
    f32, bf16 = jnp.float32, jnp.bfloat16
    chip_count = lax.axis_size("expert") * lax.axis_size("chip")
    tok_rows, feature_count = tokens.shape
    half_width = feature_count // 2
    is_lower = lax.axis_index("core") == 0
    own_expert = lax.axis_index("expert") * lax.axis_size("chip") + lax.axis_index("chip")
    steps = doubling_pairs(chip_count)

    def own_first(rows):
        return jnp.where(is_lower, rows, jnp.roll(rows, half_width, 1))

    gate_w, up_w, down_w = (
        jnp.concatenate([w[0], swap_core(w[0])], axis)
        for w, axis in ((gate_half, 0), (up_half, 0), (down_half, 1))
    )

    experts = jnp.arange(chip_count, dtype=jnp.int32)
    named = expert_ids[:, :, None] == experts
    weight = jnp.sum(jnp.where(named, gate_probs.astype(f32)[:, :, None], 0.0), axis=1)
    lanes = -(-chip_count // 128) * 128
    weight = jnp.pad(weight, ((0, 0), (0, lanes - chip_count))).astype(bf16)

    rows = gather(own_first(tokens), steps)
    dys_weight = gather(jnp.concatenate([own_first(cotangent), weight], 1), steps)
    dys = dys_weight[:, :feature_count]
    is_own = jnp.arange(lanes, dtype=jnp.int32) == own_expert
    gates = jnp.sum(
        jnp.where(is_own, dys_weight[:, feature_count:].astype(f32), 0.0), 1, keepdims=True
    )

    pre_gate = jnp.dot(rows, gate_w, preferred_element_type=f32)
    pre_up = jnp.dot(rows, up_w, preferred_element_type=f32)
    sig = jax.nn.sigmoid(pre_gate)
    active = pre_gate * sig
    slope = sig * (1.0 + pre_gate * (1.0 - sig))
    hidden = active * pre_up
    last = (((1,), (1,)), ((), ()))
    back = lax.dot_general(dys, down_w, last, preferred_element_type=f32)
    gate_grads = jnp.sum(hidden * back, 1, keepdims=True)
    back = back * gates
    grad_up = (back * active).astype(bf16)
    grad_gate = (back * pre_up * slope).astype(bf16)
    row_grad = (
        lax.dot_general(grad_gate, gate_w, last, preferred_element_type=f32)
        + lax.dot_general(grad_up, up_w, last, preferred_element_type=f32)
    ).astype(bf16)
    hidden = (hidden * gates).astype(bf16)

    gate_cols = jnp.where(is_own, gate_grads, 0.0).astype(bf16)
    summed = scatter_sum(jnp.concatenate([row_grad, gate_cols], 1), steps)
    grad_tokens = own_first(summed[:, :feature_count])
    grad_gates = jnp.sum(
        jnp.where(named, summed[:, None, feature_count : feature_count + chip_count], 0), 2
    ).astype(bf16)

    across = (((0,), (0,)), ((), ()))
    grad_gate_w = lax.dot_general(rows, grad_gate, across, preferred_element_type=f32)
    grad_up_w = lax.dot_general(rows, grad_up, across, preferred_element_type=f32)
    grad_down_w = lax.dot_general(hidden, dys, across, preferred_element_type=f32)

    def settle(whole, axis):
        keep, give = jnp.split(whole, 2, axis)
        return (keep + swap_core(give.astype(bf16)).astype(f32)).astype(bf16)[None]

    return (
        grad_tokens,
        grad_gates,
        settle(grad_gate_w, 0),
        settle(grad_up_w, 0),
        settle(grad_down_w, 1),
    )


def solution(mesh):
    shape = mesh.shape
    devices = mesh.devices.reshape(shape["dom"], shape["expert"], shape["dp"] // 2, 2)
    fine = Mesh(devices, ("dom", "expert", "chip", "core"))
    every = ("dom", "expert", "chip", "core")
    flat, cube = P(every, None), P(every, None, None)
    return jax.shard_map(
        body,
        mesh=fine,
        in_specs=(flat, flat, flat, flat, cube, cube, cube),
        out_specs=(flat, flat, cube, cube, cube),
        check_vma=False,
    )
```

```python
import jax
import jax.numpy as jnp
from jax import lax
from jax.experimental import pallas as pl
from jax.experimental.pallas import tpu as pltpu
from jax.sharding import Mesh, PartitionSpec as P

DEVICES = ("expert", "chip", "core")
F32, BF16 = jnp.float32, jnp.bfloat16
NN = (((1,), (0,)), ((), ()))
NT = (((1,), (1,)), ((), ()))
TN = (((0,), (0,)), ((), ()))
CHUNK = 256


def dot(a, b, dims):
    return lax.dot_general(a, b, dims, preferred_element_type=F32)


def swap_core(x):
    return lax.ppermute(x, "core", [(0, 1), (1, 0)])


def for_chunks(rows, step):
    if rows <= CHUNK:
        step(pl.ds(0, rows))
    else:

        @pl.loop(0, rows // CHUNK)
        def _(i):
            step(pl.ds(pl.multiple_of(i * CHUNK, CHUNK), CHUNK))


def own_other(place_ref, half):
    member = place_ref[0]
    own = pl.ds(pl.multiple_of(member * half, half), half)
    other = pl.ds(pl.multiple_of((1 - member) * half, half), half)
    return own, other


def forward_kernel(place, rows, gate_own, gate_other, up_own, up_other, active, slope_up, hidden):
    own, other = own_other(place, gate_own.shape[0])

    def step(at):
        mine, rest = rows[at, own], rows[at, other]
        pre_gate = dot(mine, gate_own[...], NN) + dot(rest, gate_other[...], NN)
        pre_up = dot(mine, up_own[...], NN) + dot(rest, up_other[...], NN)
        sig = jax.nn.sigmoid(pre_gate)
        act = pre_gate * sig
        active[at, :] = act
        slope_up[at, :] = pre_up * (sig * (1.0 + pre_gate * (1.0 - sig)))
        hidden[at, :] = act * pre_up

    for_chunks(rows.shape[0], step)


def backward_kernel(
    place, dys, active, slope_up, hidden,
    gate_own, gate_other, up_own, up_other, down_own, down_other,
    row_own, row_other, grads, scaled_hidden,
):
    half, width = gate_own.shape
    lanes = dys.shape[1] - 2 * half
    own, other = own_other(place, half)

    def step(at):
        back = dot(dys[at, own], down_own[...], NT) + dot(dys[at, other], down_other[...], NT)
        lane = lax.broadcasted_iota(jnp.int32, (back.shape[0], lanes), 1)
        is_own = lane == place[1]
        gates = jnp.where(is_own, dys[at, pl.ds(2 * half, lanes)].astype(F32), 0.0)
        gates = jnp.sum(gates, 1, keepdims=True)
        hid = hidden[at, :]
        gate_grads = jnp.sum(hid * back, 1, keepdims=True)
        back = back * gates
        grad_gate = (back * slope_up[at, :]).astype(BF16)
        grad_up = (back * active[at, :]).astype(BF16)
        grads[at, pl.ds(0, width)] = grad_gate
        grads[at, pl.ds(width, width)] = grad_up
        scaled_hidden[at, :] = (hid * gates).astype(BF16)
        row_own[at, :] = (
            dot(grad_gate, gate_own[...], NT) + dot(grad_up, up_own[...], NT)
        ).astype(BF16)
        row_other[at, pl.ds(0, half)] = (
            dot(grad_gate, gate_other[...], NT) + dot(grad_up, up_other[...], NT)
        ).astype(BF16)
        row_other[at, pl.ds(half, lanes)] = jnp.where(is_own, gate_grads, 0.0).astype(BF16)

    for_chunks(dys.shape[0], step)


def weight_kernel(
    place, rows_a, rows_b, dys_a, dys_b, grads_a, grads_b, hidden_a, hidden_b,
    keep_in, keep_down, give_in, give_down,
):
    half = keep_in.shape[0]
    count = rows_a.shape[0]
    own, other = own_other(place, half)

    def products(at, cols):
        into = dot(rows_a[at, cols], grads_a[at, :], TN) + dot(rows_b[at, cols], grads_b[at, :], TN)
        down = dot(hidden_a[at, :], dys_a[at, cols], TN) + dot(hidden_b[at, :], dys_b[at, cols], TN)
        return into, down

    if count <= CHUNK:
        at = pl.ds(0, count)
        into, down = products(at, other)
        give_in[...] = into.astype(BF16)
        give_down[...] = down.astype(BF16)
        into, down = products(at, own)
        keep_in[...] = into
        keep_down[...] = down
    else:
        for cols, give in ((other, True), (own, False)):
            keep_in[...] = jnp.zeros_like(keep_in)
            keep_down[...] = jnp.zeros_like(keep_down)

            @pl.loop(0, count // CHUNK)
            def _(i):
                into, down = products(pl.ds(pl.multiple_of(i * CHUNK, CHUNK), CHUNK), cols)
                keep_in[...] += into
                keep_down[...] += down

            if give:
                give_in[...] = keep_in[...].astype(BF16)
                give_down[...] = keep_down[...].astype(BF16)


def call(kernel, outs, flops, place, *args):
    small = max(x.shape[0] for x in args) <= 2 * CHUNK
    if small:
        args = [pltpu.with_memory_space_constraint(x, pltpu.VMEM) for x in args]
        out_shape = [pltpu.VMEM(s, d) for s, d in outs]
    else:
        out_shape = [jax.ShapeDtypeStruct(s, d) for s, d in outs]
    moved = sum(x.size * x.dtype.itemsize for x in args)
    return pl.pallas_call(
        kernel,
        out_shape=out_shape,
        in_specs=[pl.BlockSpec(memory_space=pltpu.SMEM)]
        + [pl.BlockSpec(memory_space=pltpu.VMEM)] * len(args),
        out_specs=[pl.BlockSpec(memory_space=pltpu.VMEM)] * len(outs),
        compiler_params=pltpu.CompilerParams(vmem_limit_bytes=56 * 2**20),
        cost_estimate=pl.CostEstimate(flops=flops, bytes_accessed=moved, transcendentals=0),
    )(place, *args)


def chip_bits(chip_count):
    bits = []
    bit = chip_count // 2
    while bit:
        bits.append(bit)
        bit //= 2
    return (bits[:-2] + bits[-2:][::-1], bits)


def body(tokens, cotangent, expert_ids, gate_probs, gate_half, up_half, down_half):
    chip_count = lax.axis_size("expert") * lax.axis_size("chip")
    tok_rows, feature_count = tokens.shape
    half = feature_count // 2
    width = gate_half.shape[2]
    member = lax.axis_index("core")
    own_expert = lax.axis_index("expert") * lax.axis_size("chip") + lax.axis_index("chip")
    place = jnp.stack([member, own_expert]).astype(jnp.int32)
    is_lower = member == 0
    orders = chip_bits(chip_count)
    far = len(orders[0]) - 2
    pairs = [
        [
            (2 * chip + core, 2 * (chip ^ orders[core][step]) + core)
            for chip in range(chip_count)
            for core in range(2)
        ]
        for step in range(far + 2)
    ]

    def exchange(x, step):
        return lax.ppermute(x, DEVICES, pairs[step])

    rows = tokens
    for step in range(far + 1):
        rows = jnp.concatenate([rows, exchange(rows, step)], 0)
    rows_a, rows_b = rows, exchange(rows, far + 1)

    experts = jnp.arange(chip_count, dtype=jnp.int32)
    named = expert_ids[:, :, None] == experts
    weight = jnp.sum(jnp.where(named, gate_probs.astype(F32)[:, :, None], 0.0), axis=1)
    lanes = -(-chip_count // 128) * 128
    weight = jnp.pad(weight, ((0, 0), (0, lanes - chip_count))).astype(BF16)
    dys = jnp.concatenate([cotangent, weight], 1)
    dys = jnp.stack([dys, exchange(dys, far)], 0)
    for step in range(far):
        dys = jnp.concatenate([dys, exchange(dys, step)], 1)
    dys_a = dys.reshape(-1, feature_count + lanes)
    dys_b = exchange(dys_a, far + 1)

    gate_own, up_own, down_own = gate_half[0], up_half[0], down_half[0]
    gate_other, up_other, down_other = swap_core(gate_own), swap_core(up_own), swap_core(down_own)

    count = rows_a.shape[0]
    unit = 2 * count * feature_count * width

    def forward(rows):
        return call(
            forward_kernel, [((count, width), F32)] * 3, 2 * unit,
            place, rows, gate_own, gate_other, up_own, up_other,
        )

    def backward(dys, forward_outs):
        return call(
            backward_kernel,
            [
                ((count, half), BF16),
                ((count, half + lanes), BF16),
                ((count, 2 * width), BF16),
                ((count, width), BF16),
            ],
            3 * unit,
            place, dys, *forward_outs,
            gate_own, gate_other, up_own, up_other, down_own, down_other,
        )

    mid_a, mid_b = forward(rows_a), forward(rows_b)
    own_a, other_a, grads_a, hidden_a = backward(dys_a, mid_a)
    own_b, other_b, grads_b, hidden_b = backward(dys_b, mid_b)

    def add(x, y):
        return (x.astype(F32) + y.astype(F32)).astype(BF16)

    own, other = add(own_a, exchange(own_b, far + 1)), add(other_a, exchange(other_b, far + 1))
    for step in reversed(range(far + 1)):
        middle = own.shape[0] // 2
        own = add(own[:middle], exchange(own[middle:], step))
        other = add(other[:middle], exchange(other[middle:], step))

    lower = jnp.where(is_lower, own, other[:, :half])
    upper = jnp.where(is_lower, other[:, :half], own)
    grad_tokens = jnp.concatenate([lower, upper], 1)
    gate_cols = other[:, None, half : half + chip_count]
    grad_gates = jnp.sum(jnp.where(named, gate_cols, 0), 2).astype(BF16)

    keep_in, keep_down, give_in, give_down = call(
        weight_kernel,
        [
            ((half, 2 * width), F32),
            ((width, half), F32),
            ((half, 2 * width), BF16),
            ((width, half), BF16),
        ],
        6 * unit,
        place, rows_a, rows_b, dys_a, dys_b, grads_a, grads_b, hidden_a, hidden_b,
    )
    got_in, got_down = swap_core(give_in), swap_core(give_down)
    grad_in = (keep_in + got_in.astype(F32)).astype(BF16)
    grad_down = (keep_down + got_down.astype(F32)).astype(BF16)
    return (
        grad_tokens,
        grad_gates,
        grad_in[None, :, :width],
        grad_in[None, :, width:],
        grad_down[None],
    )


def solution(mesh):
    shape = mesh.shape
    devices = mesh.devices.reshape(shape["dom"], shape["expert"], shape["dp"] // 2, 2)
    fine = Mesh(devices, ("dom", "expert", "chip", "core"))
    every = ("dom", "expert", "chip", "core")
    flat, cube = P(every, None), P(every, None, None)
    return jax.shard_map(
        body,
        mesh=fine,
        in_specs=(flat, flat, flat, flat, cube, cube, cube),
        out_specs=(flat, flat, cube, cube, cube),
        check_vma=False,
    )
```

```python
import jax
import jax.numpy as jnp
from jax import lax
from jax.experimental import pallas as pl
from jax.experimental.pallas import tpu as pltpu
from jax.sharding import Mesh, PartitionSpec as P

DEVICES = ("expert", "chip", "core")
F32, BF16 = jnp.float32, jnp.bfloat16
NN = (((1,), (0,)), ((), ()))
NT = (((1,), (1,)), ((), ()))
TN = (((0,), (0,)), ((), ()))
CHUNK = 256


def dot(a, b, dims):
    return lax.dot_general(a, b, dims, preferred_element_type=F32)


def swap_core(x):
    return lax.ppermute(x, "core", [(0, 1), (1, 0)])


def for_chunks(rows, step):
    if rows <= CHUNK:
        step(pl.ds(0, rows))
    else:

        @pl.loop(0, rows // CHUNK)
        def _(i):
            step(pl.ds(pl.multiple_of(i * CHUNK, CHUNK), CHUNK))


def own_other(place_ref, half):
    member = place_ref[0]
    own = pl.ds(pl.multiple_of(member * half, half), half)
    other = pl.ds(pl.multiple_of((1 - member) * half, half), half)
    return own, other


def prepare_kernel(tokens, cotangent, ids, probs, rows, dys):
    features = tokens.shape[1]
    rows[0] = tokens[...]
    dys[0, :, pl.ds(0, features)] = cotangent[...]
    lanes = dys.shape[2] - features
    lane = lax.broadcasted_iota(jnp.int32, (tokens.shape[0], lanes), 1)
    names, given = ids[...], probs[...].astype(F32)
    weight = jnp.zeros(lane.shape, F32)
    for k in range(ids.shape[1]):
        weight = jnp.where(names[:, k : k + 1] == lane, given[:, k : k + 1], weight)
    dys[0, :, pl.ds(features, lanes)] = weight.astype(BF16)


def stack_kernel(first, second, out):
    out[0] = first[0]
    out[1] = second[0]


def join_kernel(first, second, out):
    rows = first.shape[1]
    out[:, pl.ds(0, rows), :] = first[...]
    out[:, pl.ds(rows, rows), :] = second[...]


def split_kernel(kept, got, keep, give):
    rows = keep.shape[0]
    upper, lower = pl.ds(0, rows), pl.ds(rows, rows)
    give[...] = (kept[lower, :].astype(F32) + got[lower, :].astype(F32)).astype(BF16)
    keep[...] = kept[upper, :].astype(F32) + got[upper, :].astype(F32)


def finish_kernel(place, own_kept, own_got, other_kept, other_got, ids, grad_tokens, grad_gates):
    half = own_kept.shape[1]
    own, other = own_other(place, half)
    left = pl.ds(0, half)
    grad_tokens[:, own] = (own_kept[...].astype(F32) + own_got[...].astype(F32)).astype(BF16)
    grad_tokens[:, other] = (
        other_kept[:, left].astype(F32) + other_got[:, left].astype(F32)
    ).astype(BF16)
    right = pl.ds(half, other_kept.shape[1] - half)
    gates = other_kept[:, right].astype(F32) + other_got[:, right].astype(F32)
    lane = lax.broadcasted_iota(jnp.int32, gates.shape, 1)
    names = ids[...]
    column = lax.broadcasted_iota(jnp.int32, names.shape, 1)
    out = jnp.zeros(names.shape, F32)
    for k in range(names.shape[1]):
        picked = jnp.sum(jnp.where(names[:, k : k + 1] == lane, gates, 0.0), 1, keepdims=True)
        out = jnp.where(column == k, picked, out)
    grad_gates[...] = out.astype(BF16)


def forward_kernel(place, rows, gate_own, gate_other, up_own, up_other, active, slope_up, hidden):
    own, other = own_other(place, gate_own.shape[0])

    def step(at):
        mine, rest = rows[at, own], rows[at, other]
        pre_gate = dot(mine, gate_own[...], NN) + dot(rest, gate_other[...], NN)
        pre_up = dot(mine, up_own[...], NN) + dot(rest, up_other[...], NN)
        sig = jax.nn.sigmoid(pre_gate)
        act = pre_gate * sig
        active[at, :] = act
        slope_up[at, :] = pre_up * (sig * (1.0 + pre_gate * (1.0 - sig)))
        hidden[at, :] = act * pre_up

    for_chunks(rows.shape[0], step)


def backward_kernel(
    place, dys, active, slope_up, hidden,
    gate_own, gate_other, up_own, up_other, down_own, down_other,
    row_own, row_other, grads, scaled_hidden,
):
    half, width = gate_own.shape
    lanes = dys.shape[1] - 2 * half
    own, other = own_other(place, half)

    def step(at):
        back = dot(dys[at, own], down_own[...], NT) + dot(dys[at, other], down_other[...], NT)
        lane = lax.broadcasted_iota(jnp.int32, (back.shape[0], lanes), 1)
        is_own = lane == place[1]
        gates = jnp.where(is_own, dys[at, pl.ds(2 * half, lanes)].astype(F32), 0.0)
        gates = jnp.sum(gates, 1, keepdims=True)
        hid = hidden[at, :]
        gate_grads = jnp.sum(hid * back, 1, keepdims=True)
        back = back * gates
        grad_gate = (back * slope_up[at, :]).astype(BF16)
        grad_up = (back * active[at, :]).astype(BF16)
        grads[at, pl.ds(0, width)] = grad_gate
        grads[at, pl.ds(width, width)] = grad_up
        scaled_hidden[at, :] = (hid * gates).astype(BF16)
        row_own[at, :] = (
            dot(grad_gate, gate_own[...], NT) + dot(grad_up, up_own[...], NT)
        ).astype(BF16)
        row_other[at, pl.ds(0, half)] = (
            dot(grad_gate, gate_other[...], NT) + dot(grad_up, up_other[...], NT)
        ).astype(BF16)
        row_other[at, pl.ds(half, lanes)] = jnp.where(is_own, gate_grads, 0.0).astype(BF16)

    for_chunks(dys.shape[0], step)


def weight_kernel(
    place, rows_a, rows_b, dys_a, dys_b, grads_a, grads_b, hidden_a, hidden_b,
    keep_in, keep_down, give_gate, give_up, give_down,
):
    half, width = give_gate.shape
    left, right = pl.ds(0, width), pl.ds(width, width)
    count = rows_a.shape[0]
    own, other = own_other(place, half)

    def products(at, cols):
        into = dot(rows_a[at, cols], grads_a[at, :], TN) + dot(rows_b[at, cols], grads_b[at, :], TN)
        down = dot(hidden_a[at, :], dys_a[at, cols], TN) + dot(hidden_b[at, :], dys_b[at, cols], TN)
        return into, down

    if count <= CHUNK:
        at = pl.ds(0, count)
        into, down = products(at, other)
        give_gate[...] = into[:, :width].astype(BF16)
        give_up[...] = into[:, width:].astype(BF16)
        give_down[...] = down.astype(BF16)
        into, down = products(at, own)
        keep_in[...] = into
        keep_down[...] = down
    else:
        for cols, give in ((other, True), (own, False)):
            keep_in[...] = jnp.zeros_like(keep_in)
            keep_down[...] = jnp.zeros_like(keep_down)

            @pl.loop(0, count // CHUNK)
            def _(i):
                into, down = products(pl.ds(pl.multiple_of(i * CHUNK, CHUNK), CHUNK), cols)
                keep_in[...] += into
                keep_down[...] += down

            if give:
                give_gate[...] = keep_in[:, left].astype(BF16)
                give_up[...] = keep_in[:, right].astype(BF16)
                give_down[...] = keep_down[...].astype(BF16)


def settle_kernel(keep_in, keep_down, got_gate, got_up, got_down, gate, up, down, done):
    width = gate.shape[1]
    left, right = pl.ds(0, width), pl.ds(width, width)
    gate[...] = (keep_in[:, left] + got_gate[...].astype(F32)).astype(BF16)
    up[...] = (keep_in[:, right] + got_up[...].astype(F32)).astype(BF16)
    down[...] = (keep_down[...] + got_down[...].astype(F32)).astype(BF16)
    done[...] = jnp.zeros_like(done)


def call(kernel, outs, flops, place, *args, after=(), small=True, arrives=0, leaves=0):
    used = len(args)
    limit = 10 * 2**20 if small else 56 * 2**20
    if small:
        args = [
            pltpu.with_memory_space_constraint(x, pltpu.VMEM) if i < used - arrives else x
            for i, x in enumerate(args)
        ]
    out_shape = [
        pltpu.VMEM(s, d) if small and i >= leaves else jax.ShapeDtypeStruct(s, d)
        for i, (s, d) in enumerate(outs)
    ]

    scalars = () if place is None else (place,)
    read = len(scalars) + used

    def run(*refs):
        kernel(*refs[:read], *refs[read + len(after) :])

    moved = sum(x.size * x.dtype.itemsize for x in args)
    vmem = pl.BlockSpec(memory_space=pltpu.VMEM)
    return pl.pallas_call(
        run,
        out_shape=out_shape,
        in_specs=[pl.BlockSpec(memory_space=pltpu.SMEM)] * len(scalars)
        + [vmem] * used
        + [pl.BlockSpec(memory_space=pl.ANY)] * len(after),
        out_specs=[vmem] * len(outs),
        compiler_params=pltpu.CompilerParams(vmem_limit_bytes=limit),
        cost_estimate=pl.CostEstimate(flops=flops, bytes_accessed=moved, transcendentals=0),
        name=kernel.__name__,
    )(*scalars, *args, *after)


def chip_bits(chip_count):
    bits = []
    bit = chip_count // 2
    while bit:
        bits.append(bit)
        bit //= 2
    return (bits[:-2] + bits[-2:][::-1], bits)


def body(tokens, cotangent, expert_ids, gate_probs, gate_half, up_half, down_half):
    chip_count = lax.axis_size("expert") * lax.axis_size("chip")
    tok_rows, features = tokens.shape
    half = features // 2
    width = gate_half.shape[2]
    lanes = -(-chip_count // 128) * 128
    count = tok_rows * chip_count // 2
    small = count <= CHUNK
    member = lax.axis_index("core")
    own_expert = lax.axis_index("expert") * lax.axis_size("chip") + lax.axis_index("chip")
    place = jnp.stack([member, own_expert]).astype(jnp.int32)
    orders = chip_bits(chip_count)
    far = len(orders[0]) - 2
    pairs = [
        [
            (2 * chip + core, 2 * (chip ^ orders[core][step]) + core)
            for chip in range(chip_count)
            for core in range(2)
        ]
        for step in range(far + 2)
    ]

    def exchange(x, step):
        return lax.ppermute(x, DEVICES, pairs[step])

    def stack(first, second):
        shape = (2,) + first.shape[1:]
        return call(stack_kernel, [(shape, BF16)], 0, None, first, second)[0]

    def join(first, second):
        outer, rows, cols = first.shape
        shape = (outer, 2 * rows, cols)
        fits = small or outer * rows < count
        return call(join_kernel, [(shape, BF16)], 0, None, first, second, small=fits)[0]

    rows, dys = call(
        prepare_kernel,
        [((1, tok_rows, features), BF16), ((1, tok_rows, features + lanes), BF16)], 0,
        None, tokens, cotangent, expert_ids, gate_probs, arrives=4,
    )

    near = exchange(dys, far)
    for step in range(far + 1):
        rows = join(rows, exchange(rows, step))
        dys = join(dys, near) if step else stack(dys, near)
        if step < far:
            near = exchange(dys, step)
    rows_a, rows_b = rows[0], exchange(rows[0], far + 1)
    dys_a = dys.reshape(count, features + lanes)
    dys_b = exchange(dys_a, far + 1)

    gate_own, up_own, down_own = gate_half[0], up_half[0], down_half[0]
    gate_other, up_other, down_other = swap_core(gate_own), swap_core(up_own), swap_core(down_own)
    unit = 2 * count * features * width

    def forward(rows, after=()):
        return call(
            forward_kernel, [((count, width), F32)] * 3, 20 * unit,
            place, rows, gate_own, gate_other, up_own, up_other, after=after, small=small,
        )

    def backward(dys, forward_outs, after=()):
        return call(
            backward_kernel,
            [
                ((count, half), BF16),
                ((count, half + lanes), BF16),
                ((count, 2 * width), BF16),
                ((count, width), BF16),
            ],
            3 * unit,
            place, dys, *forward_outs,
            gate_own, gate_other, up_own, up_other, down_own, down_other, after=after, small=small,
        )

    mid_a = forward(rows_a)
    own_a, other_a, grads_a, hidden_a = backward(dys_a, mid_a)
    mid_b = forward(rows_b, after=(own_a,))
    own_b, other_b, grads_b, hidden_b = backward(dys_b, mid_b)

    got_own, got_other = exchange(own_b, far + 1), exchange(other_b, far + 1)
    keep_in, keep_down, *gives = call(
        weight_kernel,
        [
            ((half, 2 * width), F32),
            ((width, half), F32),
            ((half, width), BF16),
            ((half, width), BF16),
            ((width, half), BF16),
        ],
        6 * unit,
        place, rows_a, rows_b, dys_a, dys_b, grads_a, grads_b, hidden_a, hidden_b, small=small,
    )
    gots = [swap_core(give) for give in gives]

    def split(kept, got, after=()):
        rows, cols = kept.shape
        shape = (rows // 2, cols)
        return call(
            split_kernel, [(shape, F32), (shape, BF16)], 0,
            None, kept, got, after=after, small=small,
        )

    own, other = own_a, other_a
    for step in reversed(range(far + 1)):
        after = ()
        if step == 0:
            grad_gate, grad_up, grad_down, *after = call(
                settle_kernel,
                [
                    ((half, width), BF16),
                    ((half, width), BF16),
                    ((width, half), BF16),
                    ((8, 128), F32),
                ],
                0,
                None, keep_in, keep_down, *gots, small=small, leaves=3,
            )
        other, give_other = split(other, got_other, after)
        got_other = exchange(give_other, step)
        own, give_own = split(own, got_own)
        got_own = exchange(give_own, step)
    grad_tokens, grad_gates = call(
        finish_kernel,
        [((tok_rows, features), BF16), (expert_ids.shape, BF16)], 0,
        place, own, got_own, other, got_other, expert_ids, arrives=1, leaves=2,
    )
    return grad_tokens, grad_gates, grad_gate[None], grad_up[None], grad_down[None]


def solution(mesh):
    shape = mesh.shape
    devices = mesh.devices.reshape(shape["dom"], shape["expert"], shape["dp"] // 2, 2)
    fine = Mesh(devices, ("dom", "expert", "chip", "core"))
    every = ("dom", "expert", "chip", "core")
    flat, cube = P(every, None), P(every, None, None)
    return jax.shard_map(
        body,
        mesh=fine,
        in_specs=(flat, flat, flat, flat, cube, cube, cube),
        out_specs=(flat, flat, cube, cube, cube),
        check_vma=False,
    )
```

```python
import jax
import jax.numpy as jnp
from jax import lax
from jax.experimental import pallas as pl
from jax.experimental.pallas import tpu as pltpu
from jax.sharding import Mesh, PartitionSpec as P

DEVICES = ("expert", "chip", "core")
F32, BF16 = jnp.float32, jnp.bfloat16
NN = (((1,), (0,)), ((), ()))
NT = (((1,), (1,)), ((), ()))
TN = (((0,), (0,)), ((), ()))
CHUNK = 128


def dot(a, b, dims):
    return lax.dot_general(a, b, dims, preferred_element_type=F32)


def swap_core(x):
    return lax.ppermute(x, "core", [(0, 1), (1, 0)])


def for_chunks(rows, step):
    if rows <= CHUNK:
        step(pl.ds(0, rows))
    else:

        @pl.loop(0, rows // CHUNK)
        def _(i):
            step(pl.ds(pl.multiple_of(i * CHUNK, CHUNK), CHUNK))


def own_other(place_ref, half, start=0):
    member = place_ref[0]
    own = pl.ds(pl.multiple_of(start + member * half, half), half)
    other = pl.ds(pl.multiple_of(start + (1 - member) * half, half), half)
    return own, other


def prepare_kernel(tokens, cotangent, ids, probs, out, ids_here, probs_here, sems):
    features = tokens.shape[1]
    lanes = out.shape[1] - 2 * features
    copies = [
        pltpu.make_async_copy(source, target, sems.at[i])
        for i, (source, target) in enumerate(
            (
                (ids, ids_here),
                (probs, probs_here),
                (tokens, out.at[:, pl.ds(0, features)]),
                (cotangent, out.at[:, pl.ds(features, features)]),
            )
        )
    ]
    for copy in copies:
        copy.start()
    copies[0].wait()
    copies[1].wait()
    names, given = ids_here[...], probs_here[...].astype(F32)
    expert = lax.broadcasted_iota(jnp.int32, (lanes, names.shape[1]), 0)
    weight = jnp.zeros(expert.shape, F32)
    for k in range(names.shape[0]):
        weight = jnp.where(names[k : k + 1, :] == expert, given[k : k + 1, :], weight)
    turned = dot(weight.astype(BF16), unit_matrix(lanes), TN)
    out[:, pl.ds(2 * features, lanes)] = turned.astype(BF16)
    copies[2].wait()
    copies[3].wait()


def unit_matrix(size):
    row = lax.broadcasted_iota(jnp.int32, (size, size), 0)
    column = lax.broadcasted_iota(jnp.int32, (size, size), 1)
    return jnp.where(row == column, 1.0, 0.0).astype(BF16)


def join_kernel(first, second, out):
    rows = first.shape[0]
    out[pl.ds(0, rows), :] = first[...]
    out[pl.ds(rows, rows), :] = second[...]


def split_kernel(kept, got, keep, give):
    rows = keep.shape[0]
    upper, lower = pl.ds(0, rows), pl.ds(rows, rows)
    give[...] = (kept[lower, :].astype(F32) + got[lower, :].astype(F32)).astype(BF16)
    keep[...] = kept[upper, :].astype(F32) + got[upper, :].astype(F32)


def add_kernel(kept, got, total):
    total[...] = (kept[...] + got[...].astype(F32)).astype(total.dtype)


def pass_kernel(source, out):
    out[...] = source[...]


def expert_kernel(
    place, first, second, gate_own, gate_other, up_own, up_other, down_own, down_other,
    keep, give, grads, scaled_hidden,
):
    half, width = gate_own.shape
    features = 2 * half
    lanes = first.shape[1] - 2 * features
    own, other = own_other(place, half)
    dys_own, dys_other = own_other(place, half, features)

    def step(at):
        count = at.size

        def take(cols):
            return jnp.concatenate([first[at, cols], second[at, cols]], 0)

        mine, rest = take(own), take(other)
        pre_gate = dot(mine, gate_own[...], NN) + dot(rest, gate_other[...], NN)
        pre_up = dot(mine, up_own[...], NN) + dot(rest, up_other[...], NN)
        back = dot(take(dys_own), down_own[...], NT) + dot(take(dys_other), down_other[...], NT)
        sig = jax.nn.sigmoid(pre_gate)
        active = pre_gate * sig
        slope = sig * (1.0 + pre_gate * (1.0 - sig))
        hidden = active * pre_up
        lane = lax.broadcasted_iota(jnp.int32, (2 * count, lanes), 1)
        is_own = lane == place[1]
        gates = jnp.where(is_own, take(pl.ds(2 * features, lanes)).astype(F32), 0.0)
        gates = jnp.sum(gates, 1, keepdims=True)
        gate_grads = jnp.sum(hidden * back, 1, keepdims=True)
        back = back * gates
        grad_gate = (back * pre_up * slope).astype(BF16)
        grad_up = (back * active).astype(BF16)
        scaled = (hidden * gates).astype(BF16)
        pieces = (
            dot(grad_gate, gate_own[...], NT) + dot(grad_up, up_own[...], NT),
            dot(grad_gate, gate_other[...], NT) + dot(grad_up, up_other[...], NT),
            jnp.where(is_own, gate_grads, 0.0),
        )
        begin = 0
        for piece in pieces:
            cols = pl.ds(begin, piece.shape[1])
            give[at, cols] = piece[count:].astype(BF16)
            keep[at, cols] = piece[:count].astype(BF16)
            begin += piece.shape[1]
        for i in range(2):
            part = slice(i * count, (i + 1) * count)
            grads[i, at, pl.ds(0, width)] = grad_gate[part]
            grads[i, at, pl.ds(width, width)] = grad_up[part]
            scaled_hidden[i, at, :] = scaled[part]

    for_chunks(first.shape[0], step)


def weight_kernel(place, *refs):
    keep_in, keep_down, give_gate, give_up, give_down = refs[-5:]
    pieces = [refs[i : i + 4] for i in range(0, len(refs) - 5, 4)]
    half, width = give_gate.shape
    count = pieces[0][0].shape[0]
    own, other = own_other(place, half)
    dys_own, dys_other = own_other(place, half, 2 * half)
    left, right = pl.ds(0, width), pl.ds(width, width)
    parts = [(p[i], p[2].at[i], p[3].at[i]) for p in pieces for i in range(2)]

    def products(parts, at, cols, dys_cols):
        def gathered(values):
            return values[0] if len(values) == 1 else jnp.concatenate(values, 0)

        rows = gathered([p[0][at, cols] for p in parts])
        dys = gathered([p[0][at, dys_cols] for p in parts])
        grads = gathered([p[1][at, :] for p in parts])
        hidden = gathered([p[2][at, :] for p in parts])
        return dot(rows, grads, TN), dot(hidden, dys, TN)

    def hand_over(into, down):
        give_gate[...] = into[:, left.start : left.start + width].astype(BF16)
        give_up[...] = into[:, width : 2 * width].astype(BF16)
        give_down[...] = down.astype(BF16)

    if count <= CHUNK:
        at = pl.ds(0, count)
        hand_over(*products(parts, at, other, dys_other))
        keep_in[...], keep_down[...] = products(parts, at, own, dys_own)
    else:
        for cols, dys_cols, is_given in ((other, dys_other, True), (own, dys_own, False)):
            keep_in[...] = jnp.zeros_like(keep_in)
            keep_down[...] = jnp.zeros_like(keep_down)

            @pl.loop(0, count // CHUNK)
            def _(i):
                at = pl.ds(pl.multiple_of(i * CHUNK, CHUNK), CHUNK)
                into, down = products(parts, at, cols, dys_cols)
                keep_in[...] += into
                keep_down[...] += down

            if is_given:
                hand_over(keep_in[...], keep_down[...])


def settle_kernel(keep_in, keep_down, got_gate, got_up, got_down, gate, up, down):
    width = gate.shape[1]
    left, right = pl.ds(0, width), pl.ds(width, width)
    gate[...] = (keep_in[:, left] + got_gate[...].astype(F32)).astype(BF16)
    up[...] = (keep_in[:, right] + got_up[...].astype(F32)).astype(BF16)
    down[...] = (keep_down[...] + got_down[...].astype(F32)).astype(BF16)


def finish_kernel(place, *refs):
    ids, grad_tokens, grad_gates, done = refs[-4:]
    done[...] = jnp.zeros_like(done)
    total = refs[0][...].astype(F32)
    for part in refs[1:-4]:
        total = total + part[...].astype(F32)
    half = grad_tokens.shape[1] // 2
    lanes = total.shape[1] - 2 * half
    own, other = own_other(place, half)
    grad_tokens[:, own] = total[:, :half].astype(BF16)
    grad_tokens[:, other] = total[:, half : 2 * half].astype(BF16)
    gates = dot(unit_matrix(lanes), total[:, 2 * half :].astype(BF16), NT)
    names = ids[...]
    expert = lax.broadcasted_iota(jnp.int32, gates.shape, 0)
    row = lax.broadcasted_iota(jnp.int32, names.shape, 0)
    out = jnp.zeros(names.shape, F32)
    for k in range(names.shape[0]):
        picked = jnp.sum(jnp.where(names[k : k + 1, :] == expert, gates, 0.0), 0, keepdims=True)
        out = jnp.where(row == k, picked, out)
    grad_gates[...] = out.astype(BF16)


def call(kernel, outs, place, *args, after=(), small=True, arrives=0, leaves=0, flops=0):
    used = len(args)
    limit = 10 * 2**20 if small else 56 * 2**20
    if small:
        args = [
            pltpu.with_memory_space_constraint(x, pltpu.VMEM) if i < used - arrives else x
            for i, x in enumerate(args)
        ]
    out_shape = [
        pltpu.VMEM(s, d) if small and i >= leaves else jax.ShapeDtypeStruct(s, d)
        for i, (s, d) in enumerate(outs)
    ]

    scalars = () if place is None else (place,)
    read = len(scalars) + used

    def run(*refs):
        kernel(*refs[:read], *refs[read + len(after) :])

    vmem = pl.BlockSpec(memory_space=pltpu.VMEM)
    return pl.pallas_call(
        run,
        out_shape=out_shape,
        in_specs=[pl.BlockSpec(memory_space=pltpu.SMEM)] * len(scalars)
        + [vmem] * used
        + [pl.BlockSpec(memory_space=pl.ANY)] * len(after),
        out_specs=[vmem] * len(outs),
        compiler_params=pltpu.CompilerParams(vmem_limit_bytes=limit),
        cost_estimate=pl.CostEstimate(flops=flops, bytes_accessed=0, transcendentals=0),
        name=kernel.__name__,
    )(*scalars, *args, *after)


def chip_bits(chip_count):
    bits = []
    bit = chip_count // 2
    while bit:
        bits.append(bit)
        bit //= 2
    return (bits[:-2] + bits[-2:][::-1], bits)


def body(tokens, cotangent, expert_ids, gate_probs, gate_half, up_half, down_half):
    chip_count = lax.axis_size("expert") * lax.axis_size("chip")
    tok_rows, features = tokens.shape
    half = features // 2
    width = gate_half.shape[2]
    lanes = -(-chip_count // 128) * 128
    member = lax.axis_index("core")
    own_expert = lax.axis_index("expert") * lax.axis_size("chip") + lax.axis_index("chip")
    place = jnp.stack([member, own_expert]).astype(jnp.int32)
    bits = chip_bits(chip_count)
    far = len(bits[0]) - 4
    small = far == 0

    def exchange(x, offsets):
        pairs = [
            (2 * chip + core, 2 * (chip ^ offsets[core]) + core)
            for chip in range(chip_count)
            for core in range(2)
        ]
        return lax.ppermute(x, DEVICES, pairs)

    steps = list(zip(*bits))
    near_a, near_b = steps[-2:]
    up_two, up_one = steps[far][0], steps[far + 1][0]

    before = []

    def run(kernel, outs, place, *args, **kwargs):
        results = call(kernel, outs, place, *args, after=tuple(before), small=small, **kwargs)
        before[:] = results[-1:]
        return results

    hbm = pl.BlockSpec(memory_space=pltpu.HBM)
    arguments = (tokens, cotangent, expert_ids.T, gate_probs.T)
    block = pl.pallas_call(
        prepare_kernel,
        out_shape=pltpu.VMEM((tok_rows, 2 * features + lanes), BF16),
        in_specs=[hbm] * 4,
        out_specs=pl.BlockSpec(memory_space=pltpu.VMEM),
        scratch_shapes=[
            pltpu.VMEM(expert_ids.shape[::-1], jnp.int32),
            pltpu.VMEM(gate_probs.shape[::-1], BF16),
            pltpu.SemaphoreType.DMA((4,)),
        ],
        name="prepare_kernel",
    )(*(pltpu.with_memory_space_constraint(x, pltpu.HBM) for x in arguments))

    for step in steps[:far]:
        block = jnp.concatenate([block, exchange(block, step)], 0)

    offsets = (0, up_one, up_two, up_one ^ up_two)
    sources = [block] + [exchange(block, (offset, offset)) for offset in offsets[1:]]
    count = 2 * block.shape[0]
    half_shape = (count // 2, features + lanes)
    full_shape = (count, features + lanes)

    gate_own, up_own, down_own = gate_half[0], up_half[0], down_half[0]
    gate_other, up_other, down_other = swap_core(gate_own), swap_core(up_own), swap_core(down_own)
    weights = (gate_own, gate_other, up_own, up_other, down_own, down_other)

    second_blocks = {}
    first, second, kept, got, saved = {}, {}, {}, {}, {}
    returned = {}

    def send(i, ordered=True):
        if ordered:
            (sources[i],) = run(pass_kernel, [(sources[i].shape, BF16)], None, sources[i])
        second_blocks[i] = exchange(sources[i], near_a)

    def join(i):
        shape = (count, 2 * features + lanes)
        (first[i],) = run(join_kernel, [(shape, BF16)], None, sources[i], second_blocks[i])
        second[i] = exchange(first[i], near_b)

    def expert(i):
        kept[i], give, grads, hidden = run(
            expert_kernel,
            [
                (full_shape, BF16),
                (full_shape, BF16),
                ((2, count, 2 * width), BF16),
                ((2, count, width), BF16),
            ],
            place, first[i], second[i], *weights,
        )
        got[i] = exchange(give, near_b)
        saved[i] = (first[i], second[i], grads, hidden)

    def split(i):
        kept[i], give = run(
            split_kernel, [(half_shape, F32), (half_shape, BF16)], None, kept[i], got[i]
        )
        got[i] = exchange(give, near_a)

    def add(i):
        (give,) = run(add_kernel, [(half_shape, BF16)], None, kept[i], got[i])
        returned[i] = exchange(give, (offsets[i], offsets[i]))

    def collect(total, part):
        return run(add_kernel, [(half_shape, F32)], None, total, part)[0]

    send(0, ordered=False)
    send(1, ordered=False)
    join(0)
    join(1)
    send(2)
    expert(0)
    join(2)
    send(3)
    expert(1)
    join(3)
    split(0)
    expert(2)
    split(1)
    total = collect(kept[0], got[0])
    expert(3)
    add(1)
    split(2)
    split(3)
    add(2)
    total = collect(total, returned[1])
    add(3)
    keep_in, keep_down, *gives = run(
        weight_kernel,
        [
            ((half, 2 * width), F32),
            ((width, half), F32),
            ((half, width), BF16),
            ((half, width), BF16),
            ((width, half), BF16),
        ],
        place, *saved[0], *saved[1], *saved[2], *saved[3],
    )
    gots = [swap_core(give) for give in gives]
    total = collect(total, returned[2])

    parts = (total, returned[3])
    if far:
        total = total + returned[3].astype(F32)
        for step in reversed(steps[:far]):
            middle = total.shape[0] // 2
            total = total[:middle] + exchange(total[middle:].astype(BF16), step).astype(F32)
        parts = (total,)
    grad_tokens, grad_gates, _ = run(
        finish_kernel,
        [((tok_rows, features), BF16), (expert_ids.shape[::-1], BF16), ((8, 128), F32)],
        place, *parts, expert_ids.T, arrives=1, leaves=2, flops=6 * 10**9,
    )
    grad_gate, grad_up, grad_down = run(
        settle_kernel,
        [((half, width), BF16), ((half, width), BF16), ((width, half), BF16)],
        None, keep_in, keep_down, *gots, leaves=3,
    )
    return grad_tokens, grad_gates.T, grad_gate[None], grad_up[None], grad_down[None]


def solution(mesh):
    shape = mesh.shape
    devices = mesh.devices.reshape(shape["dom"], shape["expert"], shape["dp"] // 2, 2)
    fine = Mesh(devices, ("dom", "expert", "chip", "core"))
    every = ("dom", "expert", "chip", "core")
    flat, cube = P(every, None), P(every, None, None)
    return jax.shard_map(
        body,
        mesh=fine,
        in_specs=(flat, flat, flat, flat, cube, cube, cube),
        out_specs=(flat, flat, cube, cube, cube),
        check_vma=False,
    )
```

```python
import jax
import jax.numpy as jnp
from jax import lax
from jax.experimental import pallas as pl
from jax.experimental.pallas import tpu as pltpu
from jax.sharding import Mesh, PartitionSpec as P

DEVICES = ("expert", "chip", "core")
F32, BF16 = jnp.float32, jnp.bfloat16
NN = (((1,), (0,)), ((), ()))
NT = (((1,), (1,)), ((), ()))
TN = (((0,), (0,)), ((), ()))
CHUNK = 128


def dot(a, b, dims):
    return lax.dot_general(a, b, dims, preferred_element_type=F32)


def swap_core(x):
    return lax.ppermute(x, "core", [(0, 1), (1, 0)])


def for_chunks(rows, step):
    if rows <= CHUNK:
        step(pl.ds(0, rows))
    else:

        @pl.loop(0, rows // CHUNK)
        def _(i):
            step(pl.ds(pl.multiple_of(i * CHUNK, CHUNK), CHUNK))


def own_other(place_ref, half, start=0):
    member = place_ref[0]
    own = pl.ds(pl.multiple_of(start + member * half, half), half)
    other = pl.ds(pl.multiple_of(start + (1 - member) * half, half), half)
    return own, other


def prepare_kernel(tokens, cotangent, ids, probs, out, ids_here, probs_here, sems):
    features = tokens.shape[1]
    lanes = out.shape[1] - 2 * features
    copies = [
        pltpu.make_async_copy(source, target, sems.at[i])
        for i, (source, target) in enumerate(
            (
                (ids, ids_here),
                (probs, probs_here),
                (tokens, out.at[:, pl.ds(0, features)]),
                (cotangent, out.at[:, pl.ds(features, features)]),
            )
        )
    ]
    for copy in copies:
        copy.start()
    copies[0].wait()
    copies[1].wait()
    names, given = ids_here[...], probs_here[...].astype(F32)
    expert = lax.broadcasted_iota(jnp.int32, (lanes, names.shape[1]), 0)
    weight = jnp.zeros(expert.shape, F32)
    for k in range(names.shape[0]):
        weight = jnp.where(names[k : k + 1, :] == expert, given[k : k + 1, :], weight)
    turned = dot(weight.astype(BF16), unit_matrix(lanes), TN)
    out[:, pl.ds(2 * features, lanes)] = turned.astype(BF16)
    copies[2].wait()
    copies[3].wait()


def unit_matrix(size):
    row = lax.broadcasted_iota(jnp.int32, (size, size), 0)
    column = lax.broadcasted_iota(jnp.int32, (size, size), 1)
    return jnp.where(row == column, 1.0, 0.0).astype(BF16)


def join_kernel(first, second, out):
    rows = first.shape[0]
    out[pl.ds(0, rows), :] = first[...]
    out[pl.ds(rows, rows), :] = second[...]


def split_kernel(kept, got, keep, give):
    rows = keep.shape[0]
    upper, lower = pl.ds(0, rows), pl.ds(rows, rows)
    give[...] = (kept[lower, :].astype(F32) + got[lower, :].astype(F32)).astype(give.dtype)
    keep[...] = (kept[upper, :].astype(F32) + got[upper, :].astype(F32)).astype(keep.dtype)


def add_kernel(kept, got, total):
    total[...] = (kept[...] + got[...].astype(F32)).astype(total.dtype)


def pass_kernel(source, out):
    out[...] = source[...]


def expert_kernel(
    place, block, gate_own, gate_other, up_own, up_other, down_own, down_other,
    row_grads, grads, scaled_hidden,
):
    half, width = gate_own.shape
    features = 2 * half
    lanes = block.shape[1] - 2 * features
    own, other = own_other(place, half)
    dys_own, dys_other = own_other(place, half, features)

    def step(at):
        mine, rest = block[at, own], block[at, other]
        pre_gate = dot(mine, gate_own[...], NN) + dot(rest, gate_other[...], NN)
        pre_up = dot(mine, up_own[...], NN) + dot(rest, up_other[...], NN)
        back = dot(block[at, dys_own], down_own[...], NT)
        back = back + dot(block[at, dys_other], down_other[...], NT)
        sig = jax.nn.sigmoid(pre_gate)
        active = pre_gate * sig
        slope = sig * (1.0 + pre_gate * (1.0 - sig))
        hidden = active * pre_up
        lane = lax.broadcasted_iota(jnp.int32, (back.shape[0], lanes), 1)
        is_own = lane == place[1]
        gates = jnp.where(is_own, block[at, pl.ds(2 * features, lanes)].astype(F32), 0.0)
        gates = jnp.sum(gates, 1, keepdims=True)
        gate_grads = jnp.sum(hidden * back, 1, keepdims=True)
        back = back * gates
        grad_gate = (back * pre_up * slope).astype(BF16)
        grad_up = (back * active).astype(BF16)
        row_grads[at, pl.ds(0, half)] = (
            dot(grad_gate, gate_own[...], NT) + dot(grad_up, up_own[...], NT)
        ).astype(BF16)
        row_grads[at, pl.ds(half, half)] = (
            dot(grad_gate, gate_other[...], NT) + dot(grad_up, up_other[...], NT)
        ).astype(BF16)
        row_grads[at, pl.ds(features, lanes)] = jnp.where(is_own, gate_grads, 0.0).astype(BF16)
        grads[at, pl.ds(0, width)] = grad_gate
        grads[at, pl.ds(width, width)] = grad_up
        scaled_hidden[at, :] = (hidden * gates).astype(BF16)

    for_chunks(block.shape[0], step)


def weight_kernel(place, *refs):
    keep_in, keep_down, give_gate, give_up, give_down = refs[-5:]
    parts = [refs[i : i + 3] for i in range(0, len(refs) - 5, 3)]
    half, width = give_gate.shape
    count = parts[0][0].shape[0]
    own, other = own_other(place, half)
    dys_own, dys_other = own_other(place, half, 2 * half)
    left, right = pl.ds(0, width), pl.ds(width, width)

    def products(parts, at, cols, dys_cols):
        rows = jnp.concatenate([p[0][at, cols] for p in parts], 0)
        dys = jnp.concatenate([p[0][at, dys_cols] for p in parts], 0)
        grads = jnp.concatenate([p[1][at, :] for p in parts], 0)
        hidden = jnp.concatenate([p[2][at, :] for p in parts], 0)
        return dot(rows, grads, TN), dot(hidden, dys, TN)

    def hand_over(into, down):
        give_gate[...] = into[:, left.start : left.start + width].astype(BF16)
        give_up[...] = into[:, width : 2 * width].astype(BF16)
        give_down[...] = down.astype(BF16)

    if count <= CHUNK:
        at = pl.ds(0, count)
        hand_over(*products(parts, at, other, dys_other))
        keep_in[...], keep_down[...] = products(parts, at, own, dys_own)
    else:
        for cols, dys_cols, is_given in ((other, dys_other, True), (own, dys_own, False)):
            keep_in[...] = jnp.zeros_like(keep_in)
            keep_down[...] = jnp.zeros_like(keep_down)

            @pl.loop(0, count // CHUNK)
            def _(i):
                at = pl.ds(pl.multiple_of(i * CHUNK, CHUNK), CHUNK)
                into, down = products(parts, at, cols, dys_cols)
                keep_in[...] += into
                keep_down[...] += down

            if is_given:
                hand_over(keep_in[...], keep_down[...])


def settle_kernel(keep_in, keep_down, got_gate, got_up, got_down, gate, up, down):
    width = gate.shape[1]
    left, right = pl.ds(0, width), pl.ds(width, width)
    gate[...] = (keep_in[:, left] + got_gate[...].astype(F32)).astype(BF16)
    up[...] = (keep_in[:, right] + got_up[...].astype(F32)).astype(BF16)
    down[...] = (keep_down[...] + got_down[...].astype(F32)).astype(BF16)


def finish_kernel(place, *refs):
    ids, grad_tokens, grad_gates, done = refs[-4:]
    done[...] = jnp.zeros_like(done)
    total = refs[0][...].astype(F32)
    for part in refs[1:-4]:
        total = total + part[...].astype(F32)
    half = grad_tokens.shape[1] // 2
    lanes = total.shape[1] - 2 * half
    own, other = own_other(place, half)
    grad_tokens[:, own] = total[:, :half].astype(BF16)
    grad_tokens[:, other] = total[:, half : 2 * half].astype(BF16)
    gates = dot(unit_matrix(lanes), total[:, 2 * half :].astype(BF16), NT)
    names = ids[...]
    expert = lax.broadcasted_iota(jnp.int32, gates.shape, 0)
    row = lax.broadcasted_iota(jnp.int32, names.shape, 0)
    out = jnp.zeros(names.shape, F32)
    for k in range(names.shape[0]):
        picked = jnp.sum(jnp.where(names[k : k + 1, :] == expert, gates, 0.0), 0, keepdims=True)
        out = jnp.where(row == k, picked, out)
    grad_gates[...] = out.astype(BF16)


def call(kernel, outs, place, *args, after=(), small=True, arrives=0, leaves=0, flops=0, limit=2):
    used = len(args)
    limit = (limit if small else 56) * 2**20
    if small:
        args = [
            pltpu.with_memory_space_constraint(x, pltpu.VMEM) if i < used - arrives else x
            for i, x in enumerate(args)
        ]
    out_shape = [
        pltpu.VMEM(s, d) if small and i >= leaves else jax.ShapeDtypeStruct(s, d)
        for i, (s, d) in enumerate(outs)
    ]

    scalars = () if place is None else (place,)
    read = len(scalars) + used

    def run(*refs):
        kernel(*refs[:read], *refs[read + len(after) :])

    vmem = pl.BlockSpec(memory_space=pltpu.VMEM)
    return pl.pallas_call(
        run,
        out_shape=out_shape,
        in_specs=[pl.BlockSpec(memory_space=pltpu.SMEM)] * len(scalars)
        + [vmem] * used
        + [pl.BlockSpec(memory_space=pl.ANY)] * len(after),
        out_specs=[vmem] * len(outs),
        compiler_params=pltpu.CompilerParams(vmem_limit_bytes=limit),
        cost_estimate=pl.CostEstimate(flops=flops, bytes_accessed=0, transcendentals=0),
        name=kernel.__name__,
    )(*scalars, *args, *after)


def chip_bits(chip_count):
    bits = []
    bit = chip_count // 2
    while bit:
        bits.append(bit)
        bit //= 2
    return (bits[:-2] + bits[-2:][::-1], bits)


def body(tokens, cotangent, expert_ids, gate_probs, gate_half, up_half, down_half):
    chip_count = lax.axis_size("expert") * lax.axis_size("chip")
    tok_rows, features = tokens.shape
    half = features // 2
    width = gate_half.shape[2]
    lanes = -(-chip_count // 128) * 128
    member = lax.axis_index("core")
    own_expert = lax.axis_index("expert") * lax.axis_size("chip") + lax.axis_index("chip")
    place = jnp.stack([member, own_expert]).astype(jnp.int32)
    bits = chip_bits(chip_count)
    far = len(bits[0]) - 4
    small = far == 0

    def exchange(x, offsets):
        pairs = [
            (2 * chip + core, 2 * (chip ^ offsets[core]) + core)
            for chip in range(chip_count)
            for core in range(2)
        ]
        return lax.ppermute(x, DEVICES, pairs)

    steps = list(zip(*bits))
    near_a, near_b = steps[-2:]
    up_two, up_one = steps[far][0], steps[far + 1][0]

    before = []

    def run(kernel, outs, place, *args, **kwargs):
        results = call(kernel, outs, place, *args, after=tuple(before), small=small, **kwargs)
        before[:] = results[-1:]
        return results

    hbm = pl.BlockSpec(memory_space=pltpu.HBM)
    arguments = (tokens, cotangent, expert_ids.T, gate_probs.T)
    block = pl.pallas_call(
        prepare_kernel,
        out_shape=pltpu.VMEM((tok_rows, 2 * features + lanes), BF16),
        in_specs=[hbm] * 4,
        out_specs=pl.BlockSpec(memory_space=pltpu.VMEM),
        scratch_shapes=[
            pltpu.VMEM(expert_ids.shape[::-1], jnp.int32),
            pltpu.VMEM(gate_probs.shape[::-1], BF16),
            pltpu.SemaphoreType.DMA((4,)),
        ],
        name="prepare_kernel",
    )(*(pltpu.with_memory_space_constraint(x, pltpu.HBM) for x in arguments))

    for step in steps[:far]:
        block = jnp.concatenate([block, exchange(block, step)], 0)

    offsets = (up_two, up_one, up_one ^ up_two)
    rows = block.shape[0]
    columns = features + lanes

    gate_own, up_own, down_own = gate_half[0], up_half[0], down_half[0]
    gate_other, up_other, down_other = swap_core(gate_own), swap_core(up_own), swap_core(down_own)
    weights = (gate_own, gate_other, up_own, up_other, down_own, down_other)
    saved = []

    def at_offset(x, i):
        return exchange(x, (offsets[i], offsets[i]))

    def join(first, second):
        shape = (2 * first.shape[0], first.shape[1])
        return run(join_kernel, [(shape, BF16)], None, first, second)[0]

    def after_all(x, *others):
        before.extend(others)
        return run(pass_kernel, [(x.shape, BF16)], None, x)[0]

    def expert(block):
        count = block.shape[0]
        row_grads, grads, hidden = run(
            expert_kernel,
            [((count, columns), BF16), ((count, 2 * width), BF16), ((count, width), BF16)],
            place, block, *weights, limit=6, flops=6 * 10**9,
        )
        saved.extend([block, grads, hidden])
        return row_grads

    def split(kept, got, types):
        shape = (kept.shape[0] // 2, columns)
        return run(split_kernel, [(shape, t) for t in types], None, kept, got)

    def collect(total, part):
        return run(add_kernel, [(total.shape, F32)], None, total, part)[0]

    near_0 = join(block, at_offset(block, 0))
    near_1 = at_offset(near_0, 1)
    first_0 = join(near_0, exchange(near_0, near_a))
    second_0 = exchange(first_0, near_b)
    near_1 = after_all(near_1)
    got_near = exchange(near_1, near_a)
    kept_0 = expert(first_0)
    first_1 = join(near_1, got_near)
    second_1 = exchange(first_1, near_b)
    give_0 = expert(second_0)
    kept_1 = expert(first_1)
    got_0 = exchange(after_all(give_0, second_1), near_b)
    got_1 = exchange(expert(second_1), near_b)

    kept_0, give = split(kept_0, got_0, (F32, BF16))
    got_0 = exchange(give, near_a)
    kept_1, give = split(kept_1, got_1, (F32, BF16))
    got_1 = exchange(give, near_a)
    total, give = split(kept_0, got_0, (F32, BF16))
    back_two = at_offset(give, 0)
    give_one, give_both = split(kept_1, got_1, (BF16, BF16))
    back_one, back_both = at_offset(give_one, 1), at_offset(give_both, 2)
    keep_in, keep_down, *gives = run(
        weight_kernel,
        [
            ((half, 2 * width), F32),
            ((width, half), F32),
            ((half, width), BF16),
            ((half, width), BF16),
            ((width, half), BF16),
        ],
        place, *saved, limit=10,
    )
    gots = [swap_core(give) for give in gives]
    total = collect(total, back_two)
    total = collect(total, back_one)

    parts = (total, back_both)
    if far:
        total = total + back_both.astype(F32)
        for step in reversed(steps[:far]):
            middle = total.shape[0] // 2
            total = total[:middle] + exchange(total[middle:].astype(BF16), step).astype(F32)
        parts = (total,)
    grad_tokens, grad_gates, _ = run(
        finish_kernel,
        [((tok_rows, features), BF16), (expert_ids.shape[::-1], BF16), ((8, 128), F32)],
        place, *parts, expert_ids.T, arrives=1, leaves=2, flops=6 * 10**9,
    )
    grad_gate, grad_up, grad_down = run(
        settle_kernel,
        [((half, width), BF16), ((half, width), BF16), ((width, half), BF16)],
        None, keep_in, keep_down, *gots, leaves=3, limit=6,
    )
    return grad_tokens, grad_gates.T, grad_gate[None], grad_up[None], grad_down[None]


def solution(mesh):
    shape = mesh.shape
    devices = mesh.devices.reshape(shape["dom"], shape["expert"], shape["dp"] // 2, 2)
    fine = Mesh(devices, ("dom", "expert", "chip", "core"))
    every = ("dom", "expert", "chip", "core")
    flat, cube = P(every, None), P(every, None, None)
    return jax.shard_map(
        body,
        mesh=fine,
        in_specs=(flat, flat, flat, flat, cube, cube, cube),
        out_specs=(flat, flat, cube, cube, cube),
        check_vma=False,
    )
```

```python
import jax
import jax.numpy as jnp
from jax import lax
from jax.experimental import pallas as pl
from jax.experimental.pallas import tpu as pltpu
from jax.sharding import Mesh, PartitionSpec as P

DEVICES = ("expert", "chip", "core")
F32, BF16 = jnp.float32, jnp.bfloat16
NN = (((1,), (0,)), ((), ()))
NT = (((1,), (1,)), ((), ()))
TN = (((0,), (0,)), ((), ()))
CHUNK = 128


def dot(a, b, dims):
    return lax.dot_general(a, b, dims, preferred_element_type=F32)


def swap_core(x):
    return lax.ppermute(x, "core", [(0, 1), (1, 0)])


def for_chunks(rows, step, chunk):
    if rows <= chunk:
        step(pl.ds(0, rows))
    else:

        @pl.loop(0, rows // chunk)
        def _(i):
            step(pl.ds(pl.multiple_of(i * chunk, chunk), chunk))


def own_other(place_ref, half, start=0):
    member = place_ref[0]
    own = pl.ds(pl.multiple_of(start + member * half, half), half)
    other = pl.ds(pl.multiple_of(start + (1 - member) * half, half), half)
    return own, other


def prepare_kernel(tokens, cotangent, ids, probs, out, ids_here, probs_here, sems):
    features = tokens.shape[1]
    lanes = out.shape[1] - 2 * features
    copies = [
        pltpu.make_async_copy(source, target, sems.at[i])
        for i, (source, target) in enumerate(
            (
                (ids, ids_here),
                (probs, probs_here),
                (tokens, out.at[:, pl.ds(0, features)]),
                (cotangent, out.at[:, pl.ds(features, features)]),
            )
        )
    ]
    for copy in copies:
        copy.start()
    copies[0].wait()
    copies[1].wait()
    names, given = ids_here[...], probs_here[...].astype(F32)
    expert = lax.broadcasted_iota(jnp.int32, (lanes, names.shape[1]), 0)
    weight = jnp.zeros(expert.shape, F32)
    for k in range(names.shape[0]):
        weight = jnp.where(names[k : k + 1, :] == expert, given[k : k + 1, :], weight)
    turned = dot(weight.astype(BF16), unit_matrix(lanes), TN)
    out[:, pl.ds(2 * features, lanes)] = turned.astype(BF16)
    copies[2].wait()
    copies[3].wait()


def unit_matrix(size):
    row = lax.broadcasted_iota(jnp.int32, (size, size), 0)
    column = lax.broadcasted_iota(jnp.int32, (size, size), 1)
    return jnp.where(row == column, 1.0, 0.0).astype(BF16)


def join_kernel(first, second, out):
    rows = first.shape[0]
    out[pl.ds(0, rows), :] = first[...]
    out[pl.ds(rows, rows), :] = second[...]


def split_kernel(kept, got, keep, give):
    rows = keep.shape[0]
    upper, lower = pl.ds(0, rows), pl.ds(rows, rows)
    give[...] = (kept[lower, :].astype(F32) + got[lower, :].astype(F32)).astype(give.dtype)
    keep[...] = (kept[upper, :].astype(F32) + got[upper, :].astype(F32)).astype(keep.dtype)


def add_kernel(kept, got, total):
    total[...] = (kept[...] + got[...].astype(F32)).astype(total.dtype)


def pass_kernel(source, out):
    out[...] = source[...]


def expert_kernel(place, *refs):
    blocks, refs = refs[:-9], refs[-9:]
    gate_own, gate_other, up_own, up_other, down_own, down_other = refs[:6]
    row_grads, grads, scaled_hidden = refs[6:]
    half, width = gate_own.shape
    features = 2 * half
    number, count = len(blocks), blocks[0].shape[0]
    lanes = blocks[0].shape[1] - 2 * features
    own, other = own_other(place, half)
    dys_own, dys_other = own_other(place, half, features)

    def step(at):
        def take(cols):
            return jnp.concatenate([block[at, cols] for block in blocks], 0)

        mine, rest = take(own), take(other)
        pre_gate = dot(mine, gate_own[...], NN) + dot(rest, gate_other[...], NN)
        pre_up = dot(mine, up_own[...], NN) + dot(rest, up_other[...], NN)
        back = dot(take(dys_own), down_own[...], NT) + dot(take(dys_other), down_other[...], NT)
        sig = jax.nn.sigmoid(pre_gate)
        active = pre_gate * sig
        slope = sig * (1.0 + pre_gate * (1.0 - sig))
        hidden = active * pre_up
        lane = lax.broadcasted_iota(jnp.int32, (back.shape[0], lanes), 1)
        is_own = lane == place[1]
        gates = jnp.where(is_own, take(pl.ds(2 * features, lanes)).astype(F32), 0.0)
        gates = jnp.sum(gates, 1, keepdims=True)
        gate_grads = jnp.sum(hidden * back, 1, keepdims=True)
        back = back * gates
        grad_gate = (back * pre_up * slope).astype(BF16)
        grad_up = (back * active).astype(BF16)
        scaled = (hidden * gates).astype(BF16)
        pieces = (
            dot(grad_gate, gate_own[...], NT) + dot(grad_up, up_own[...], NT),
            dot(grad_gate, gate_other[...], NT) + dot(grad_up, up_other[...], NT),
            jnp.where(is_own, gate_grads, 0.0),
        )
        middle = count // 2
        for i in range(number):
            part = slice(i * at.size, (i + 1) * at.size)
            grads[i, at, pl.ds(0, width)] = grad_gate[part]
            grads[i, at, pl.ds(width, width)] = grad_up[part]
            scaled_hidden[i, at, :] = scaled[part]
            begin = 0
            for piece in pieces:
                cols = pl.ds(begin, piece.shape[1])
                begin += piece.shape[1]
                rows = piece[part].astype(BF16)
                if at.size == count:
                    row_grads[pl.ds(i * middle, middle), cols] = rows[:middle]
                    row_grads[pl.ds((number + i) * middle, middle), cols] = rows[middle:]
                else:
                    place_at = at.start + at.start // middle * (number - 1) * middle + i * middle
                    row_grads[pl.ds(pl.multiple_of(place_at, at.size), at.size), cols] = rows

    for_chunks(count, step, CHUNK // number)


def weight_kernel(numbers, place, *refs):
    keep_in, keep_down, give_gate, give_up, give_down = refs[-5:]
    parts, begin = [], 0
    for number in numbers:
        grads, hidden = refs[begin + number : begin + number + 2]
        parts += [(refs[begin + i], grads.at[i], hidden.at[i]) for i in range(number)]
        begin += number + 2
    half, width = give_gate.shape
    own, other = own_other(place, half)
    dys_own, dys_other = own_other(place, half, 2 * half)
    steps = max(1, min(p[0].shape[0] for p in parts) // CHUNK)

    def products(i, cols, dys_cols):
        def gather(which, cols):
            values = []
            for part in parts:
                size = part[0].shape[0] // steps
                start = i * size
                at = pl.ds(start if steps == 1 else pl.multiple_of(start, size), size)
                values.append(part[which][at, cols])
            return jnp.concatenate(values, 0)

        into = dot(gather(0, cols), gather(1, pl.ds(0, 2 * width)), TN)
        return into, dot(gather(2, pl.ds(0, width)), gather(0, dys_cols), TN)

    def hand_over(into, down):
        give_gate[...] = into[:, :width].astype(BF16)
        give_up[...] = into[:, width:].astype(BF16)
        give_down[...] = down.astype(BF16)

    if steps == 1:
        hand_over(*products(0, other, dys_other))
        keep_in[...], keep_down[...] = products(0, own, dys_own)
    else:
        for cols, dys_cols, is_given in ((other, dys_other, True), (own, dys_own, False)):
            keep_in[...] = jnp.zeros_like(keep_in)
            keep_down[...] = jnp.zeros_like(keep_down)

            @pl.loop(0, steps)
            def _(i):
                into, down = products(i, cols, dys_cols)
                keep_in[...] += into
                keep_down[...] += down

            if is_given:
                hand_over(keep_in[...], keep_down[...])


def settle_kernel(keep_in, keep_down, got_gate, got_up, got_down, gate, up, down, done):
    width = gate.shape[1]
    left, right = pl.ds(0, width), pl.ds(width, width)
    gate[...] = (keep_in[:, left] + got_gate[...].astype(F32)).astype(BF16)
    up[...] = (keep_in[:, right] + got_up[...].astype(F32)).astype(BF16)
    down[...] = (keep_down[...] + got_down[...].astype(F32)).astype(BF16)
    done[...] = jnp.zeros_like(done)


def finish_kernel(place, *refs):
    ids, grad_tokens, grad_gates = refs[-3:]
    total = refs[0][...].astype(F32)
    for part in refs[1:-3]:
        total = total + part[...].astype(F32)
    half = grad_tokens.shape[1] // 2
    lanes = total.shape[1] - 2 * half
    own, other = own_other(place, half)
    grad_tokens[:, own] = total[:, :half].astype(BF16)
    grad_tokens[:, other] = total[:, half : 2 * half].astype(BF16)
    gates = dot(unit_matrix(lanes), total[:, 2 * half :].astype(BF16), NT)
    names = ids[...]
    expert = lax.broadcasted_iota(jnp.int32, gates.shape, 0)
    row = lax.broadcasted_iota(jnp.int32, names.shape, 0)
    out = jnp.zeros(names.shape, F32)
    for k in range(names.shape[0]):
        picked = jnp.sum(jnp.where(names[k : k + 1, :] == expert, gates, 0.0), 0, keepdims=True)
        out = jnp.where(row == k, picked, out)
    grad_gates[...] = out.astype(BF16)


def call(kernel, outs, place, *args, after=(), small=True, arrives=0, leaves=0, flops=0, limit=2):
    used = len(args)
    limit = (limit if small else 56) * 2**20
    if small:
        args = [
            pltpu.with_memory_space_constraint(x, pltpu.VMEM) if i < used - arrives else x
            for i, x in enumerate(args)
        ]
    out_shape = [
        pltpu.VMEM(s, d) if small and i >= leaves else jax.ShapeDtypeStruct(s, d)
        for i, (s, d) in enumerate(outs)
    ]

    scalars = () if place is None else (place,)
    read = len(scalars) + used

    def run(*refs):
        kernel(*refs[:read], *refs[read + len(after) :])

    vmem = pl.BlockSpec(memory_space=pltpu.VMEM)
    return pl.pallas_call(
        run,
        out_shape=out_shape,
        in_specs=[pl.BlockSpec(memory_space=pltpu.SMEM)] * len(scalars)
        + [vmem] * used
        + [pl.BlockSpec(memory_space=pl.ANY)] * len(after),
        out_specs=[vmem] * len(outs),
        compiler_params=pltpu.CompilerParams(vmem_limit_bytes=limit),
        cost_estimate=pl.CostEstimate(flops=flops, bytes_accessed=0, transcendentals=0),
        name=kernel.__name__.replace("<lambda>", "weight_kernel"),
    )(*scalars, *args, *after)


def chip_bits(chip_count):
    bits = []
    bit = chip_count // 2
    while bit:
        bits.append(bit)
        bit //= 2
    return (bits[:-2] + bits[-2:][::-1], bits)


def body(tokens, cotangent, expert_ids, gate_probs, gate_half, up_half, down_half):
    chip_count = lax.axis_size("expert") * lax.axis_size("chip")
    tok_rows, features = tokens.shape
    half = features // 2
    width = gate_half.shape[2]
    lanes = -(-chip_count // 128) * 128
    member = lax.axis_index("core")
    own_expert = lax.axis_index("expert") * lax.axis_size("chip") + lax.axis_index("chip")
    place = jnp.stack([member, own_expert]).astype(jnp.int32)
    bits = chip_bits(chip_count)
    far = len(bits[0]) - 4
    small = far == 0

    def exchange(x, offsets):
        pairs = [
            (2 * chip + core, 2 * (chip ^ offsets[core]) + core)
            for chip in range(chip_count)
            for core in range(2)
        ]
        return lax.ppermute(x, DEVICES, pairs)

    steps = list(zip(*bits))
    near_a, near_b = steps[-2:]
    up_two, up_one = steps[far][0], steps[far + 1][0]

    before = []

    def run(kernel, outs, place, *args, **kwargs):
        results = call(kernel, outs, place, *args, after=tuple(before), small=small, **kwargs)
        before[:] = results[-1:]
        return results

    hbm = pl.BlockSpec(memory_space=pltpu.HBM)
    arguments = (tokens, cotangent, expert_ids.T, gate_probs.T)
    block = pl.pallas_call(
        prepare_kernel,
        out_shape=pltpu.VMEM((tok_rows, 2 * features + lanes), BF16),
        in_specs=[hbm] * 4,
        out_specs=pl.BlockSpec(memory_space=pltpu.VMEM),
        scratch_shapes=[
            pltpu.VMEM(expert_ids.shape[::-1], jnp.int32),
            pltpu.VMEM(gate_probs.shape[::-1], BF16),
            pltpu.SemaphoreType.DMA((4,)),
        ],
        name="prepare_kernel",
    )(*(pltpu.with_memory_space_constraint(x, pltpu.HBM) for x in arguments))

    for step in steps[:far]:
        block = jnp.concatenate([block, exchange(block, step)], 0)

    offsets = (up_two, up_one, up_one ^ up_two)
    rows = block.shape[0]
    columns = features + lanes

    gate_own, up_own, down_own = gate_half[0], up_half[0], down_half[0]
    gate_other, up_other, down_other = swap_core(gate_own), swap_core(up_own), swap_core(down_own)
    weights = (gate_own, gate_other, up_own, up_other, down_own, down_other)
    numbers, saved = [], []

    def at_offset(x, i):
        return exchange(x, (offsets[i], offsets[i]))

    def join(first, second):
        shape = (2 * first.shape[0], first.shape[1])
        return run(join_kernel, [(shape, BF16)], None, first, second)[0]

    def after_all(x, *others):
        before.extend(others)
        return run(pass_kernel, [(x.shape, BF16)], None, x)[0]

    def expert(*blocks):
        number, count = len(blocks), blocks[0].shape[0]
        row_grads, grads, hidden = run(
            expert_kernel,
            [
                ((number * count, columns), BF16),
                ((number, count, 2 * width), BF16),
                ((number, count, width), BF16),
            ],
            place, *blocks, *weights, limit=6, flops=6 * 10**9,
        )
        numbers.append(number)
        saved.extend([*blocks, grads, hidden])
        return row_grads

    def split(kept, got, types):
        shape = (kept.shape[0] // 2, columns)
        return run(split_kernel, [(shape, t) for t in types], None, kept, got)

    def collect(total, part):
        return run(add_kernel, [(total.shape, F32)], None, total, part)[0]

    far_two = at_offset(block, 0)
    first_own = join(block, exchange(block, near_a))
    second_own = exchange(first_own, near_b)
    near_1 = at_offset(join(block, far_two), 1)
    second_own = after_all(second_own)
    first_two = join(far_two, exchange(far_two, near_a))
    second_two = exchange(first_two, near_b)
    near_1 = after_all(near_1)
    got_near = exchange(near_1, near_a)
    got_0 = exchange(expert(second_own, second_two), near_b)
    first_1 = join(near_1, got_near)
    second_1 = exchange(first_1, near_b)
    kept_0 = expert(first_own, first_two)
    kept_0, give = split(kept_0, got_0, (F32, BF16))
    got_0 = exchange(give, near_a)
    kept_1 = expert(first_1)
    got_1 = exchange(expert(second_1), near_b)
    total, give = split(kept_0, got_0, (F32, BF16))
    back_two = at_offset(give, 0)
    keep_in, keep_down, *gives = run(
        lambda *refs: weight_kernel(tuple(numbers), *refs),
        [
            ((half, 2 * width), F32),
            ((width, half), F32),
            ((half, width), BF16),
            ((half, width), BF16),
            ((width, half), BF16),
        ],
        place, *saved, limit=10,
    )
    gots = [swap_core(give) for give in gives]
    kept_1, give = split(kept_1, got_1, (F32, BF16))
    got_1 = exchange(give, near_a)
    total = collect(total, back_two)
    give_one, give_both = split(kept_1, got_1, (BF16, BF16))
    back_one, back_both = at_offset(give_one, 1), at_offset(give_both, 2)
    grad_gate, grad_up, grad_down, _ = run(
        settle_kernel,
        [((half, width), BF16), ((half, width), BF16), ((width, half), BF16), ((8, 128), F32)],
        None, keep_in, keep_down, *gots, leaves=3, limit=6,
    )
    total = collect(total, back_one)

    parts = (total, back_both)
    if far:
        total = total + back_both.astype(F32)
        for step in reversed(steps[:far]):
            middle = total.shape[0] // 2
            total = total[:middle] + exchange(total[middle:].astype(BF16), step).astype(F32)
        parts = (total,)
    grad_tokens, grad_gates = run(
        finish_kernel,
        [((tok_rows, features), BF16), (expert_ids.shape[::-1], BF16)],
        place, *parts, expert_ids.T, arrives=1, leaves=2,
    )
    return grad_tokens, grad_gates.T, grad_gate[None], grad_up[None], grad_down[None]


def solution(mesh):
    shape = mesh.shape
    devices = mesh.devices.reshape(shape["dom"], shape["expert"], shape["dp"] // 2, 2)
    fine = Mesh(devices, ("dom", "expert", "chip", "core"))
    every = ("dom", "expert", "chip", "core")
    flat, cube = P(every, None), P(every, None, None)
    return jax.shard_map(
        body,
        mesh=fine,
        in_specs=(flat, flat, flat, flat, cube, cube, cube),
        out_specs=(flat, flat, cube, cube, cube),
        check_vma=False,
    )
```

```python
import jax
import jax.numpy as jnp
from jax import lax
from jax.experimental import pallas as pl
from jax.experimental.pallas import tpu as pltpu
from jax.sharding import Mesh, PartitionSpec as P

DEVICES = ("expert", "chip", "core")
F32, BF16 = jnp.float32, jnp.bfloat16
NN = (((1,), (0,)), ((), ()))
NT = (((1,), (1,)), ((), ()))
TN = (((0,), (0,)), ((), ()))
CHUNK = 128


def dot(a, b, dims):
    return lax.dot_general(a, b, dims, preferred_element_type=F32)


def swap_core(x):
    return lax.ppermute(x, "core", [(0, 1), (1, 0)])


def for_chunks(rows, step, chunk):
    if rows <= chunk:
        step(pl.ds(0, rows))
    else:

        @pl.loop(0, rows // chunk)
        def _(i):
            step(pl.ds(pl.multiple_of(i * chunk, chunk), chunk))


def own_other(place_ref, half, start=0):
    member = place_ref[0]
    own = pl.ds(pl.multiple_of(start + member * half, half), half)
    other = pl.ds(pl.multiple_of(start + (1 - member) * half, half), half)
    return own, other


def prepare_kernel(tokens, cotangent, ids, probs, out, ids_here, probs_here, sems):
    features = tokens.shape[1]
    lanes = out.shape[1] - 2 * features
    copies = [
        pltpu.make_async_copy(source, target, sems.at[i])
        for i, (source, target) in enumerate(
            (
                (ids, ids_here),
                (probs, probs_here),
                (tokens, out.at[:, pl.ds(0, features)]),
                (cotangent, out.at[:, pl.ds(features, features)]),
            )
        )
    ]
    for copy in copies:
        copy.start()
    copies[0].wait()
    copies[1].wait()
    names, given = ids_here[...], probs_here[...].astype(F32)
    expert = lax.broadcasted_iota(jnp.int32, (lanes, names.shape[1]), 0)
    weight = jnp.zeros(expert.shape, F32)
    for k in range(names.shape[0]):
        weight = jnp.where(names[k : k + 1, :] == expert, given[k : k + 1, :], weight)
    turned = dot(weight.astype(BF16), unit_matrix(lanes), TN)
    out[:, pl.ds(2 * features, lanes)] = turned.astype(BF16)
    copies[2].wait()
    copies[3].wait()


def unit_matrix(size):
    row = lax.broadcasted_iota(jnp.int32, (size, size), 0)
    column = lax.broadcasted_iota(jnp.int32, (size, size), 1)
    return jnp.where(row == column, 1.0, 0.0).astype(BF16)


def join_kernel(first, second, out):
    rows = first.shape[0]
    out[pl.ds(0, rows), :] = first[...]
    out[pl.ds(rows, rows), :] = second[...]


def split_kernel(kept, got, keep, give):
    rows = keep.shape[0]
    upper, lower = pl.ds(0, rows), pl.ds(rows, rows)
    give[...] = (kept[lower, :].astype(F32) + got[lower, :].astype(F32)).astype(give.dtype)
    keep[...] = (kept[upper, :].astype(F32) + got[upper, :].astype(F32)).astype(keep.dtype)


def add_kernel(kept, got, total):
    total[...] = (kept[...] + got[...].astype(F32)).astype(total.dtype)


def pass_kernel(source, out):
    out[...] = source[...]


def expert_kernel(place, *refs):
    blocks, refs = refs[:-9], refs[-9:]
    gate_own, gate_other, up_own, up_other, down_own, down_other = refs[:6]
    row_grads, grads, scaled_hidden = refs[6:]
    half, width = gate_own.shape
    features = 2 * half
    number, count = len(blocks), blocks[0].shape[0]
    lanes = blocks[0].shape[1] - 2 * features
    own, other = own_other(place, half)
    dys_own, dys_other = own_other(place, half, features)

    def step(at):
        def take(cols):
            return jnp.concatenate([block[at, cols] for block in blocks], 0)

        mine, rest = take(own), take(other)
        pre_gate = dot(mine, gate_own[...], NN) + dot(rest, gate_other[...], NN)
        pre_up = dot(mine, up_own[...], NN) + dot(rest, up_other[...], NN)
        back = dot(take(dys_own), down_own[...], NT) + dot(take(dys_other), down_other[...], NT)
        sig = jax.nn.sigmoid(pre_gate)
        active = pre_gate * sig
        slope = sig * (1.0 + pre_gate * (1.0 - sig))
        hidden = active * pre_up
        lane = lax.broadcasted_iota(jnp.int32, (back.shape[0], lanes), 1)
        is_own = lane == place[1]
        gates = jnp.where(is_own, take(pl.ds(2 * features, lanes)).astype(F32), 0.0)
        gates = jnp.sum(gates, 1, keepdims=True)
        gate_grads = jnp.sum(hidden * back, 1, keepdims=True)
        back = back * gates
        grad_gate = (back * pre_up * slope).astype(BF16)
        grad_up = (back * active).astype(BF16)
        scaled = (hidden * gates).astype(BF16)
        middle = count // 2

        def put(rows, cols):
            for i in range(number):
                part = rows[i * at.size : (i + 1) * at.size]
                if at.size == count:
                    row_grads[pl.ds(i * middle, middle), cols] = part[:middle]
                    row_grads[pl.ds((number + i) * middle, middle), cols] = part[middle:]
                else:
                    start = at.start + at.start // middle * (number - 1) * middle + i * middle
                    row_grads[pl.ds(pl.multiple_of(start, at.size), at.size), cols] = part

        to_own = dot(grad_gate, gate_own[...], NT) + dot(grad_up, up_own[...], NT)
        put(to_own.astype(BF16), pl.ds(0, half))
        to_other = dot(grad_gate, gate_other[...], NT) + dot(grad_up, up_other[...], NT)
        put(to_other.astype(BF16), pl.ds(half, half))
        put(jnp.where(is_own, gate_grads, 0.0).astype(BF16), pl.ds(features, lanes))
        for i in range(number):
            part = slice(i * at.size, (i + 1) * at.size)
            grads[i, at, pl.ds(0, width)] = grad_gate[part]
            grads[i, at, pl.ds(width, width)] = grad_up[part]
            scaled_hidden[i, at, :] = scaled[part]

    for_chunks(count, step, CHUNK // number)


def weight_kernel(numbers, place, *refs):
    keep_in, keep_down, give_gate, give_up, give_down = refs[-5:]
    parts, begin = [], 0
    for number in numbers:
        grads, hidden = refs[begin + number : begin + number + 2]
        parts += [(refs[begin + i], grads.at[i], hidden.at[i]) for i in range(number)]
        begin += number + 2
    half, width = give_gate.shape
    own, other = own_other(place, half)
    dys_own, dys_other = own_other(place, half, 2 * half)
    steps = max(1, min(p[0].shape[0] for p in parts) // CHUNK)

    def products(i, cols, dys_cols):
        def gather(which, cols):
            values = []
            for part in parts:
                size = part[0].shape[0] // steps
                start = i * size
                at = pl.ds(start if steps == 1 else pl.multiple_of(start, size), size)
                values.append(part[which][at, cols])
            return jnp.concatenate(values, 0)

        into = dot(gather(0, cols), gather(1, pl.ds(0, 2 * width)), TN)
        return into, dot(gather(2, pl.ds(0, width)), gather(0, dys_cols), TN)

    def hand_over(into, down):
        give_gate[...] = into[:, :width].astype(BF16)
        give_up[...] = into[:, width:].astype(BF16)
        give_down[...] = down.astype(BF16)

    if steps == 1:
        hand_over(*products(0, other, dys_other))
        keep_in[...], keep_down[...] = products(0, own, dys_own)
    else:
        for cols, dys_cols, is_given in ((other, dys_other, True), (own, dys_own, False)):
            keep_in[...] = jnp.zeros_like(keep_in)
            keep_down[...] = jnp.zeros_like(keep_down)

            @pl.loop(0, steps)
            def _(i):
                into, down = products(i, cols, dys_cols)
                keep_in[...] += into
                keep_down[...] += down

            if is_given:
                hand_over(keep_in[...], keep_down[...])


def settle_kernel(keep_in, keep_down, got_gate, got_up, got_down, gate, up, down, done):
    width = gate.shape[1]
    left, right = pl.ds(0, width), pl.ds(width, width)
    gate[...] = (keep_in[:, left] + got_gate[...].astype(F32)).astype(BF16)
    up[...] = (keep_in[:, right] + got_up[...].astype(F32)).astype(BF16)
    down[...] = (keep_down[...] + got_down[...].astype(F32)).astype(BF16)
    done[...] = jnp.zeros_like(done)


def finish_kernel(place, *refs):
    ids, grad_tokens, grad_gates = refs[-3:]
    total = refs[0][...].astype(F32)
    for part in refs[1:-3]:
        total = total + part[...].astype(F32)
    half = grad_tokens.shape[1] // 2
    lanes = total.shape[1] - 2 * half
    own, other = own_other(place, half)
    grad_tokens[:, own] = total[:, :half].astype(BF16)
    grad_tokens[:, other] = total[:, half : 2 * half].astype(BF16)
    gates = dot(unit_matrix(lanes), total[:, 2 * half :].astype(BF16), NT)
    names = ids[...]
    expert = lax.broadcasted_iota(jnp.int32, gates.shape, 0)
    row = lax.broadcasted_iota(jnp.int32, names.shape, 0)
    out = jnp.zeros(names.shape, F32)
    for k in range(names.shape[0]):
        picked = jnp.sum(jnp.where(names[k : k + 1, :] == expert, gates, 0.0), 0, keepdims=True)
        out = jnp.where(row == k, picked, out)
    grad_gates[...] = out.astype(BF16)


def call(kernel, outs, place, *args, after=(), small=True, arrives=0, leaves=0, flops=0, limit=2):
    used = len(args)
    limit = (limit if small else 56) * 2**20
    if small:
        args = [
            pltpu.with_memory_space_constraint(x, pltpu.VMEM) if i < used - arrives else x
            for i, x in enumerate(args)
        ]
    out_shape = [
        pltpu.VMEM(s, d) if small and i >= leaves else jax.ShapeDtypeStruct(s, d)
        for i, (s, d) in enumerate(outs)
    ]

    scalars = () if place is None else (place,)
    read = len(scalars) + used

    def run(*refs):
        kernel(*refs[:read], *refs[read + len(after) :])

    vmem = pl.BlockSpec(memory_space=pltpu.VMEM)
    return pl.pallas_call(
        run,
        out_shape=out_shape,
        in_specs=[pl.BlockSpec(memory_space=pltpu.SMEM)] * len(scalars)
        + [vmem] * used
        + [pl.BlockSpec(memory_space=pl.ANY)] * len(after),
        out_specs=[vmem] * len(outs),
        compiler_params=pltpu.CompilerParams(vmem_limit_bytes=limit),
        cost_estimate=pl.CostEstimate(flops=flops, bytes_accessed=0, transcendentals=0),
        name=kernel.__name__.replace("<lambda>", "weight_kernel"),
    )(*scalars, *args, *after)


def chip_bits(chip_count):
    bits = []
    bit = chip_count // 2
    while bit:
        bits.append(bit)
        bit //= 2
    return (bits[:-2] + bits[-2:][::-1], bits)


def body(tokens, cotangent, expert_ids, gate_probs, gate_half, up_half, down_half):
    chip_count = lax.axis_size("expert") * lax.axis_size("chip")
    tok_rows, features = tokens.shape
    half = features // 2
    width = gate_half.shape[2]
    lanes = -(-chip_count // 128) * 128
    member = lax.axis_index("core")
    own_expert = lax.axis_index("expert") * lax.axis_size("chip") + lax.axis_index("chip")
    place = jnp.stack([member, own_expert]).astype(jnp.int32)
    bits = chip_bits(chip_count)
    far = len(bits[0]) - 4
    small = far == 0

    def exchange(x, offsets):
        pairs = [
            (2 * chip + core, 2 * (chip ^ offsets[core]) + core)
            for chip in range(chip_count)
            for core in range(2)
        ]
        return lax.ppermute(x, DEVICES, pairs)

    steps = list(zip(*bits))
    near_a, near_b = steps[-2:]
    up_two, up_one = steps[far][0], steps[far + 1][0]

    before = []

    def run(kernel, outs, place, *args, **kwargs):
        results = call(kernel, outs, place, *args, after=tuple(before), small=small, **kwargs)
        before[:] = results[-1:]
        return results

    hbm = pl.BlockSpec(memory_space=pltpu.HBM)
    arguments = (tokens, cotangent, expert_ids.T, gate_probs.T)
    block = pl.pallas_call(
        prepare_kernel,
        out_shape=pltpu.VMEM((tok_rows, 2 * features + lanes), BF16),
        in_specs=[hbm] * 4,
        out_specs=pl.BlockSpec(memory_space=pltpu.VMEM),
        scratch_shapes=[
            pltpu.VMEM(expert_ids.shape[::-1], jnp.int32),
            pltpu.VMEM(gate_probs.shape[::-1], BF16),
            pltpu.SemaphoreType.DMA((4,)),
        ],
        name="prepare_kernel",
    )(*(pltpu.with_memory_space_constraint(x, pltpu.HBM) for x in arguments))

    for step in steps[:far]:
        block = jnp.concatenate([block, exchange(block, step)], 0)

    offsets = (up_two, up_one, up_one ^ up_two)
    rows = block.shape[0]
    columns = features + lanes

    gate_own, up_own, down_own = gate_half[0], up_half[0], down_half[0]
    gate_other, up_other, down_other = swap_core(gate_own), swap_core(up_own), swap_core(down_own)
    weights = (gate_own, gate_other, up_own, up_other, down_own, down_other)
    numbers, saved = [], []

    def at_offset(x, i):
        return exchange(x, (offsets[i], offsets[i]))

    def join(first, second, flops=0):
        shape = (2 * first.shape[0], first.shape[1])
        return run(join_kernel, [(shape, BF16)], None, first, second, flops=flops)[0]

    def after_all(x, *others):
        before.extend(others)
        return run(pass_kernel, [(x.shape, BF16)], None, x)[0]

    def expert(*blocks):
        number, count = len(blocks), blocks[0].shape[0]
        row_grads, grads, hidden = run(
            expert_kernel,
            [
                ((number * count, columns), BF16),
                ((number, count, 2 * width), BF16),
                ((number, count, width), BF16),
            ],
            place, *blocks, *weights, limit=6, flops=6 * 10**9,
        )
        numbers.append(number)
        saved.extend([*blocks, grads, hidden])
        return row_grads

    def split(kept, got, types):
        shape = (kept.shape[0] // 2, columns)
        return run(split_kernel, [(shape, t) for t in types], None, kept, got)

    def collect(total, part):
        return run(add_kernel, [(total.shape, F32)], None, total, part)[0]

    far_two = at_offset(block, 0)
    first_own = join(block, exchange(block, near_a))
    second_own = exchange(first_own, near_b)
    near_1 = at_offset(join(block, far_two, flops=4 * 10**9), 1)
    second_own = after_all(second_own)
    first_two = join(far_two, exchange(far_two, near_a))
    second_two = exchange(first_two, near_b)
    near_1 = after_all(near_1)
    got_near = exchange(near_1, near_a)
    got_0 = exchange(expert(second_own, second_two), near_b)
    first_1 = join(near_1, got_near)
    second_1 = exchange(first_1, near_b)
    kept_0 = expert(first_own, first_two)
    kept_0, give = split(kept_0, got_0, (F32, BF16))
    got_0 = exchange(give, near_a)
    kept_1 = expert(first_1)
    got_1 = exchange(expert(second_1), near_b)
    total, give = split(kept_0, got_0, (F32, BF16))
    back_two = at_offset(give, 0)
    keep_in, keep_down, *gives = run(
        lambda *refs: weight_kernel(tuple(numbers), *refs),
        [
            ((half, 2 * width), F32),
            ((width, half), F32),
            ((half, width), BF16),
            ((half, width), BF16),
            ((width, half), BF16),
        ],
        place, *saved, limit=10, flops=6 * 10**9,
    )
    gots = [swap_core(give) for give in gives]
    kept_1, give = split(kept_1, got_1, (F32, BF16))
    got_1 = exchange(give, near_a)
    give_one, give_both = split(kept_1, got_1, (BF16, BF16))
    back_one, back_both = at_offset(give_one, 1), at_offset(give_both, 2)
    total = collect(total, back_two)
    grad_gate, grad_up, grad_down, _ = run(
        settle_kernel,
        [((half, width), BF16), ((half, width), BF16), ((width, half), BF16), ((8, 128), F32)],
        None, keep_in, keep_down, *gots, leaves=3, limit=6,
    )
    total = collect(total, back_one)

    parts = (total, back_both)
    if far:
        total = total + back_both.astype(F32)
        for step in reversed(steps[:far]):
            middle = total.shape[0] // 2
            total = total[:middle] + exchange(total[middle:].astype(BF16), step).astype(F32)
        parts = (total,)
    grad_tokens, grad_gates = run(
        finish_kernel,
        [((tok_rows, features), BF16), (expert_ids.shape[::-1], BF16)],
        place, *parts, expert_ids.T, arrives=1, leaves=2,
    )
    return grad_tokens, grad_gates.T, grad_gate[None], grad_up[None], grad_down[None]


def solution(mesh):
    shape = mesh.shape
    devices = mesh.devices.reshape(shape["dom"], shape["expert"], shape["dp"] // 2, 2)
    fine = Mesh(devices, ("dom", "expert", "chip", "core"))
    every = ("dom", "expert", "chip", "core")
    flat, cube = P(every, None), P(every, None, None)
    return jax.shard_map(
        body,
        mesh=fine,
        in_specs=(flat, flat, flat, flat, cube, cube, cube),
        out_specs=(flat, flat, cube, cube, cube),
        check_vma=False,
    )
```

```python
import jax
import jax.numpy as jnp
from jax import lax
from jax.experimental import pallas as pl
from jax.experimental.pallas import tpu as pltpu
from jax.sharding import Mesh, PartitionSpec as P

DEVICES = ("expert", "chip", "core")
F32, BF16 = jnp.float32, jnp.bfloat16
NN = (((1,), (0,)), ((), ()))
NT = (((1,), (1,)), ((), ()))
TN = (((0,), (0,)), ((), ()))
CHUNK = 128


def dot(a, b, dims):
    return lax.dot_general(a, b, dims, preferred_element_type=F32)


def swap_core(x):
    return lax.ppermute(x, "core", [(0, 1), (1, 0)])


def for_chunks(rows, step, chunk):
    if rows <= chunk:
        step(pl.ds(0, rows))
    else:

        @pl.loop(0, rows // chunk)
        def _(i):
            step(pl.ds(pl.multiple_of(i * chunk, chunk), chunk))


def own_other(place_ref, half, start=0):
    member = place_ref[0]
    own = pl.ds(pl.multiple_of(start + member * half, half), half)
    other = pl.ds(pl.multiple_of(start + (1 - member) * half, half), half)
    return own, other


def prepare_kernel(tokens, cotangent, ids, probs, out, ids_here, probs_here, sems):
    features = tokens.shape[1]
    lanes = out.shape[1] - 2 * features
    copies = [
        pltpu.make_async_copy(source, target, sems.at[i])
        for i, (source, target) in enumerate(
            (
                (ids, ids_here),
                (probs, probs_here),
                (tokens, out.at[:, pl.ds(0, features)]),
                (cotangent, out.at[:, pl.ds(features, features)]),
            )
        )
    ]
    for copy in copies:
        copy.start()
    copies[0].wait()
    copies[1].wait()
    names, given = ids_here[...], probs_here[...].astype(F32)
    expert = lax.broadcasted_iota(jnp.int32, (lanes, names.shape[1]), 0)
    weight = jnp.zeros(expert.shape, F32)
    for k in range(names.shape[0]):
        weight = jnp.where(names[k : k + 1, :] == expert, given[k : k + 1, :], weight)
    turned = dot(weight.astype(BF16), unit_matrix(lanes), TN)
    out[:, pl.ds(2 * features, lanes)] = turned.astype(BF16)
    copies[2].wait()
    copies[3].wait()


def unit_matrix(size):
    row = lax.broadcasted_iota(jnp.int32, (size, size), 0)
    column = lax.broadcasted_iota(jnp.int32, (size, size), 1)
    return jnp.where(row == column, 1.0, 0.0).astype(BF16)


def join_kernel(first, second, out):
    rows = first.shape[0]
    out[pl.ds(0, rows), :] = first[...]
    out[pl.ds(rows, rows), :] = second[...]


def split_kernel(kept, got, keep, give):
    rows = keep.shape[0]
    upper, lower = pl.ds(0, rows), pl.ds(rows, rows)
    give[...] = (kept[lower, :].astype(F32) + got[lower, :].astype(F32)).astype(give.dtype)
    keep[...] = (kept[upper, :].astype(F32) + got[upper, :].astype(F32)).astype(keep.dtype)


def add_kernel(kept, got, total):
    total[...] = (kept[...] + got[...].astype(F32)).astype(total.dtype)


def pass_kernel(source, out):
    out[...] = source[...]


def expert_kernel(place, *refs):
    blocks, refs = refs[:-9], refs[-9:]
    gate_own, gate_other, up_own, up_other, down_own, down_other = refs[:6]
    row_grads, grads, scaled_hidden = refs[6:]
    half, width = gate_own.shape
    features = 2 * half
    number, count = len(blocks), blocks[0].shape[0]
    lanes = blocks[0].shape[1] - 2 * features
    own, other = own_other(place, half)
    dys_own, dys_other = own_other(place, half, features)

    def step(at):
        def take(cols):
            return jnp.concatenate([block[at, cols] for block in blocks], 0)

        mine, rest = take(own), take(other)
        pre_gate = dot(mine, gate_own[...], NN) + dot(rest, gate_other[...], NN)
        pre_up = dot(mine, up_own[...], NN) + dot(rest, up_other[...], NN)
        back = dot(take(dys_own), down_own[...], NT) + dot(take(dys_other), down_other[...], NT)
        sig = jax.nn.sigmoid(pre_gate)
        active = pre_gate * sig
        slope = sig * (1.0 + pre_gate * (1.0 - sig))
        hidden = active * pre_up
        lane = lax.broadcasted_iota(jnp.int32, (back.shape[0], lanes), 1)
        is_own = lane == place[1]
        gates = jnp.where(is_own, take(pl.ds(2 * features, lanes)).astype(F32), 0.0)
        gates = jnp.sum(gates, 1, keepdims=True)
        gate_grads = jnp.sum(hidden * back, 1, keepdims=True)
        back = back * gates
        grad_gate = (back * pre_up * slope).astype(BF16)
        grad_up = (back * active).astype(BF16)
        scaled = (hidden * gates).astype(BF16)
        middle = count // 2

        def put(rows, cols):
            for i in range(number):
                part = rows[i * at.size : (i + 1) * at.size]
                if at.size == count:
                    row_grads[pl.ds(i * middle, middle), cols] = part[:middle]
                    row_grads[pl.ds((number + i) * middle, middle), cols] = part[middle:]
                else:
                    start = at.start + at.start // middle * (number - 1) * middle + i * middle
                    row_grads[pl.ds(pl.multiple_of(start, at.size), at.size), cols] = part

        to_own = dot(grad_gate, gate_own[...], NT) + dot(grad_up, up_own[...], NT)
        put(to_own.astype(BF16), pl.ds(0, half))
        to_other = dot(grad_gate, gate_other[...], NT) + dot(grad_up, up_other[...], NT)
        put(to_other.astype(BF16), pl.ds(half, half))
        put(jnp.where(is_own, gate_grads, 0.0).astype(BF16), pl.ds(features, lanes))
        for i in range(number):
            part = slice(i * at.size, (i + 1) * at.size)
            grads[i, at, pl.ds(0, width)] = grad_gate[part]
            grads[i, at, pl.ds(width, width)] = grad_up[part]
            scaled_hidden[i, at, :] = scaled[part]

    for_chunks(count, step, CHUNK // number)


def weight_kernel(numbers, place, *refs):
    keep_in, keep_down, give_gate, give_up, give_down = refs[-5:]
    parts, begin = [], 0
    for number in numbers:
        grads, hidden = refs[begin + number : begin + number + 2]
        parts += [(refs[begin + i], grads.at[i], hidden.at[i]) for i in range(number)]
        begin += number + 2
    half, width = give_gate.shape
    own, other = own_other(place, half)
    dys_own, dys_other = own_other(place, half, 2 * half)
    steps = max(1, min(p[0].shape[0] for p in parts) // CHUNK)

    def products(i, cols, dys_cols):
        def gather(which, cols):
            values = []
            for part in parts:
                size = part[0].shape[0] // steps
                start = i * size
                at = pl.ds(start if steps == 1 else pl.multiple_of(start, size), size)
                values.append(part[which][at, cols])
            return jnp.concatenate(values, 0)

        into = dot(gather(0, cols), gather(1, pl.ds(0, 2 * width)), TN)
        return into, dot(gather(2, pl.ds(0, width)), gather(0, dys_cols), TN)

    def hand_over(into, down):
        give_gate[...] = into[:, :width].astype(BF16)
        give_up[...] = into[:, width:].astype(BF16)
        give_down[...] = down.astype(BF16)

    if steps == 1:
        hand_over(*products(0, other, dys_other))
        keep_in[...], keep_down[...] = products(0, own, dys_own)
    else:
        for cols, dys_cols, is_given in ((other, dys_other, True), (own, dys_own, False)):
            keep_in[...] = jnp.zeros_like(keep_in)
            keep_down[...] = jnp.zeros_like(keep_down)

            @pl.loop(0, steps)
            def _(i):
                into, down = products(i, cols, dys_cols)
                keep_in[...] += into
                keep_down[...] += down

            if is_given:
                hand_over(keep_in[...], keep_down[...])


def settle_kernel(keep_in, keep_down, got_gate, got_up, got_down, gate, up, down, done):
    width = gate.shape[1]
    left, right = pl.ds(0, width), pl.ds(width, width)
    gate[...] = (keep_in[:, left] + got_gate[...].astype(F32)).astype(BF16)
    up[...] = (keep_in[:, right] + got_up[...].astype(F32)).astype(BF16)
    down[...] = (keep_down[...] + got_down[...].astype(F32)).astype(BF16)
    done[...] = jnp.zeros_like(done)


def finish_kernel(place, *refs):
    ids, grad_tokens, grad_gates = refs[-3:]
    total = refs[0][...].astype(F32)
    for part in refs[1:-3]:
        total = total + part[...].astype(F32)
    half = grad_tokens.shape[1] // 2
    lanes = total.shape[1] - 2 * half
    own, other = own_other(place, half)
    grad_tokens[:, own] = total[:, :half].astype(BF16)
    grad_tokens[:, other] = total[:, half : 2 * half].astype(BF16)
    gates = dot(unit_matrix(lanes), total[:, 2 * half :].astype(BF16), NT)
    names = ids[...]
    expert = lax.broadcasted_iota(jnp.int32, gates.shape, 0)
    row = lax.broadcasted_iota(jnp.int32, names.shape, 0)
    out = jnp.zeros(names.shape, F32)
    for k in range(names.shape[0]):
        picked = jnp.sum(jnp.where(names[k : k + 1, :] == expert, gates, 0.0), 0, keepdims=True)
        out = jnp.where(row == k, picked, out)
    grad_gates[...] = out.astype(BF16)


def call(kernel, outs, place, *args, after=(), small=True, arrives=0, leaves=0, flops=0, limit=2):
    used = len(args)
    limit = (limit if small else 56) * 2**20
    if small:
        args = [
            pltpu.with_memory_space_constraint(x, pltpu.VMEM) if i < used - arrives else x
            for i, x in enumerate(args)
        ]
    out_shape = [
        pltpu.VMEM(s, d) if small and i >= leaves else jax.ShapeDtypeStruct(s, d)
        for i, (s, d) in enumerate(outs)
    ]

    scalars = () if place is None else (place,)
    read = len(scalars) + used

    def run(*refs):
        kernel(*refs[:read], *refs[read + len(after) :])

    vmem = pl.BlockSpec(memory_space=pltpu.VMEM)
    return pl.pallas_call(
        run,
        out_shape=out_shape,
        in_specs=[pl.BlockSpec(memory_space=pltpu.SMEM)] * len(scalars)
        + [vmem] * used
        + [pl.BlockSpec(memory_space=pl.ANY)] * len(after),
        out_specs=[vmem] * len(outs),
        compiler_params=pltpu.CompilerParams(vmem_limit_bytes=limit),
        cost_estimate=pl.CostEstimate(flops=flops, bytes_accessed=0, transcendentals=0),
        name=kernel.__name__.replace("<lambda>", "weight_kernel"),
    )(*scalars, *args, *after)


def chip_bits(chip_count):
    bits = []
    bit = chip_count // 2
    while bit:
        bits.append(bit)
        bit //= 2
    return (bits[:-2] + bits[-2:][::-1], bits)


def body(tokens, cotangent, expert_ids, gate_probs, gate_half, up_half, down_half):
    chip_count = lax.axis_size("expert") * lax.axis_size("chip")
    tok_rows, features = tokens.shape
    half = features // 2
    width = gate_half.shape[2]
    lanes = -(-chip_count // 128) * 128
    member = lax.axis_index("core")
    own_expert = lax.axis_index("expert") * lax.axis_size("chip") + lax.axis_index("chip")
    place = jnp.stack([member, own_expert]).astype(jnp.int32)
    bits = chip_bits(chip_count)
    far = len(bits[0]) - 4
    small = far == 0

    def exchange(x, offsets):
        pairs = [
            (2 * chip + core, 2 * (chip ^ offsets[core]) + core)
            for chip in range(chip_count)
            for core in range(2)
        ]
        return lax.ppermute(x, DEVICES, pairs)

    steps = list(zip(*bits))
    near_a, near_b = steps[-2:]
    up_two, up_one = steps[far][0], steps[far + 1][0]

    before = []

    def run(kernel, outs, place, *args, **kwargs):
        results = call(kernel, outs, place, *args, after=tuple(before), small=small, **kwargs)
        before[:] = results[-1:]
        return results

    hbm = pl.BlockSpec(memory_space=pltpu.HBM)
    arguments = (tokens, cotangent, expert_ids.T, gate_probs.T)
    block = pl.pallas_call(
        prepare_kernel,
        out_shape=pltpu.VMEM((tok_rows, 2 * features + lanes), BF16),
        in_specs=[hbm] * 4,
        out_specs=pl.BlockSpec(memory_space=pltpu.VMEM),
        scratch_shapes=[
            pltpu.VMEM(expert_ids.shape[::-1], jnp.int32),
            pltpu.VMEM(gate_probs.shape[::-1], BF16),
            pltpu.SemaphoreType.DMA((4,)),
        ],
        name="prepare_kernel",
    )(*(pltpu.with_memory_space_constraint(x, pltpu.HBM) for x in arguments))

    for step in steps[:far]:
        block = jnp.concatenate([block, exchange(block, step)], 0)

    offsets = (up_two, up_one, up_one ^ up_two)
    rows = block.shape[0]
    columns = features + lanes

    gate_own, up_own, down_own = gate_half[0], up_half[0], down_half[0]
    gate_other, up_other, down_other = swap_core(gate_own), swap_core(up_own), swap_core(down_own)
    weights = [gate_own, gate_other, up_own, up_other, down_own, down_other]
    numbers, saved = [], []

    def at_offset(x, i):
        return exchange(x, (offsets[i], offsets[i]))

    def join(first, second, flops=0):
        shape = (2 * first.shape[0], first.shape[1])
        return run(join_kernel, [(shape, BF16)], None, first, second, flops=flops)[0]

    def after_all(x, *others):
        before.extend(others)
        return run(pass_kernel, [(x.shape, BF16)], None, x)[0]

    def expert(*blocks):
        number, count = len(blocks), blocks[0].shape[0]
        row_grads, grads, hidden = run(
            expert_kernel,
            [
                ((number * count, columns), BF16),
                ((number, count, 2 * width), BF16),
                ((number, count, width), BF16),
            ],
            place, *blocks, *weights, limit=6, flops=6 * 10**9,
        )
        numbers.append(number)
        saved.extend([*blocks, grads, hidden])
        return row_grads

    def split(kept, got, types):
        shape = (kept.shape[0] // 2, columns)
        return run(split_kernel, [(shape, t) for t in types], None, kept, got)

    def collect(total, part):
        return run(add_kernel, [(total.shape, F32)], None, total, part)[0]

    far_two = at_offset(block, 0)
    first_own = join(block, exchange(block, near_a))
    second_own = exchange(first_own, near_b)
    near_1 = at_offset(join(block, far_two, flops=4 * 10**9), 1)
    second_own = after_all(second_own)
    first_two = join(far_two, exchange(far_two, near_a))
    second_two = exchange(first_two, near_b)
    near_1 = after_all(near_1)
    got_near = exchange(near_1, near_a)
    weights[-1] = after_all(weights[-1])
    kept_0 = expert(first_own, first_two)
    first_1 = join(near_1, got_near)
    second_1 = exchange(first_1, near_b)
    give_0 = expert(second_own, second_two)
    kept_1 = expert(first_1)
    got_0 = exchange(after_all(give_0, second_1), near_b)
    got_1 = exchange(expert(second_1), near_b)
    kept_0, give = split(kept_0, got_0, (F32, BF16))
    got_0 = exchange(give, near_a)
    keep_in, keep_down, *gives = run(
        lambda *refs: weight_kernel(tuple(numbers), *refs),
        [
            ((half, 2 * width), F32),
            ((width, half), F32),
            ((half, width), BF16),
            ((half, width), BF16),
            ((width, half), BF16),
        ],
        place, *saved, limit=10, flops=6 * 10**9,
    )
    gots = [swap_core(give) for give in gives]
    kept_1, give = split(kept_1, got_1, (F32, BF16))
    got_1 = exchange(give, near_a)
    total, give = split(kept_0, got_0, (F32, BF16))
    back_two = at_offset(give, 0)
    give_one, give_both = split(kept_1, got_1, (BF16, BF16))
    back_one, back_both = at_offset(give_one, 1), at_offset(give_both, 2)
    grad_gate, grad_up, grad_down, _ = run(
        settle_kernel,
        [((half, width), BF16), ((half, width), BF16), ((width, half), BF16), ((8, 128), F32)],
        None, keep_in, keep_down, *gots, leaves=3, limit=6,
    )
    total = collect(total, back_two)
    total = collect(total, back_one)

    parts = (total, back_both)
    if far:
        total = total + back_both.astype(F32)
        for step in reversed(steps[:far]):
            middle = total.shape[0] // 2
            total = total[:middle] + exchange(total[middle:].astype(BF16), step).astype(F32)
        parts = (total,)
    grad_tokens, grad_gates = run(
        finish_kernel,
        [((tok_rows, features), BF16), (expert_ids.shape[::-1], BF16)],
        place, *parts, expert_ids.T, arrives=1, leaves=2,
    )
    return grad_tokens, grad_gates.T, grad_gate[None], grad_up[None], grad_down[None]


def solution(mesh):
    shape = mesh.shape
    devices = mesh.devices.reshape(shape["dom"], shape["expert"], shape["dp"] // 2, 2)
    fine = Mesh(devices, ("dom", "expert", "chip", "core"))
    every = ("dom", "expert", "chip", "core")
    flat, cube = P(every, None), P(every, None, None)
    return jax.shard_map(
        body,
        mesh=fine,
        in_specs=(flat, flat, flat, flat, cube, cube, cube),
        out_specs=(flat, flat, cube, cube, cube),
        check_vma=False,
    )
```

```python
import jax
import jax.numpy as jnp
from jax import lax
from jax.experimental import pallas as pl
from jax.experimental.pallas import tpu as pltpu
from jax.sharding import Mesh, PartitionSpec as P

DEVICES = ("expert", "chip", "core")
F32, BF16 = jnp.float32, jnp.bfloat16
NN = (((1,), (0,)), ((), ()))
NT = (((1,), (1,)), ((), ()))
TN = (((0,), (0,)), ((), ()))
CHUNK = 128


def dot(a, b, dims):
    return lax.dot_general(a, b, dims, preferred_element_type=F32)


def swap_core(x):
    return lax.ppermute(x, "core", [(0, 1), (1, 0)])


def for_chunks(rows, step, chunk):
    if rows <= chunk:
        step(pl.ds(0, rows))
    else:

        @pl.loop(0, rows // chunk)
        def _(i):
            step(pl.ds(pl.multiple_of(i * chunk, chunk), chunk))


def own_other(place_ref, half, start=0):
    member = place_ref[0]
    own = pl.ds(pl.multiple_of(start + member * half, half), half)
    other = pl.ds(pl.multiple_of(start + (1 - member) * half, half), half)
    return own, other


def prepare_kernel(tokens, cotangent, ids, probs, out, ids_here, probs_here, sems):
    features = tokens.shape[1]
    lanes = out.shape[1] - 2 * features
    copies = [
        pltpu.make_async_copy(source, target, sems.at[i])
        for i, (source, target) in enumerate(
            (
                (ids, ids_here),
                (probs, probs_here),
                (tokens, out.at[:, pl.ds(0, features)]),
                (cotangent, out.at[:, pl.ds(features, features)]),
            )
        )
    ]
    for copy in copies:
        copy.start()
    copies[0].wait()
    copies[1].wait()
    names, given = ids_here[...], probs_here[...].astype(F32)
    expert = lax.broadcasted_iota(jnp.int32, (lanes, names.shape[1]), 0)
    weight = jnp.zeros(expert.shape, F32)
    for k in range(names.shape[0]):
        weight = jnp.where(names[k : k + 1, :] == expert, given[k : k + 1, :], weight)
    turned = dot(weight.astype(BF16), unit_matrix(lanes), TN)
    out[:, pl.ds(2 * features, lanes)] = turned.astype(BF16)
    copies[2].wait()
    copies[3].wait()


def unit_matrix(size):
    row = lax.broadcasted_iota(jnp.int32, (size, size), 0)
    column = lax.broadcasted_iota(jnp.int32, (size, size), 1)
    return jnp.where(row == column, 1.0, 0.0).astype(BF16)


def join_kernel(first, second, out):
    rows = first.shape[0]
    out[pl.ds(0, rows), :] = first[...]
    out[pl.ds(rows, rows), :] = second[...]


def split_kernel(kept, got, keep, give):
    rows = keep.shape[0]
    upper, lower = pl.ds(0, rows), pl.ds(rows, rows)
    give[...] = (kept[lower, :].astype(F32) + got[lower, :].astype(F32)).astype(give.dtype)
    keep[...] = (kept[upper, :].astype(F32) + got[upper, :].astype(F32)).astype(keep.dtype)


def add_kernel(kept, got, total):
    total[...] = (kept[...] + got[...].astype(F32)).astype(total.dtype)


def pass_kernel(source, out):
    out[...] = source[...]


def expert_kernel(place, *refs):
    blocks, refs = refs[:-9], refs[-9:]
    gate_own, gate_other, up_own, up_other, down_own, down_other = refs[:6]
    row_grads, grads, scaled_hidden = refs[6:]
    half, width = gate_own.shape
    features = 2 * half
    number, count = len(blocks), blocks[0].shape[0]
    lanes = blocks[0].shape[1] - 2 * features
    own, other = own_other(place, half)
    dys_own, dys_other = own_other(place, half, features)

    def step(at):
        def take(cols):
            return jnp.concatenate([block[at, cols] for block in blocks], 0)

        mine, rest = take(own), take(other)
        pre_gate = dot(mine, gate_own[...], NN) + dot(rest, gate_other[...], NN)
        pre_up = dot(mine, up_own[...], NN) + dot(rest, up_other[...], NN)
        back = dot(take(dys_own), down_own[...], NT) + dot(take(dys_other), down_other[...], NT)
        sig = jax.nn.sigmoid(pre_gate)
        active = pre_gate * sig
        slope = sig * (1.0 + pre_gate * (1.0 - sig))
        hidden = active * pre_up
        lane = lax.broadcasted_iota(jnp.int32, (back.shape[0], lanes), 1)
        is_own = lane == place[1]
        gates = jnp.where(is_own, take(pl.ds(2 * features, lanes)).astype(F32), 0.0)
        gates = jnp.sum(gates, 1, keepdims=True)
        gate_grads = jnp.sum(hidden * back, 1, keepdims=True)
        back = back * gates
        grad_gate = (back * pre_up * slope).astype(BF16)
        grad_up = (back * active).astype(BF16)
        scaled = (hidden * gates).astype(BF16)
        middle = count // 2

        def put(rows, cols):
            for i in range(number):
                part = rows[i * at.size : (i + 1) * at.size]
                if at.size == count:
                    row_grads[pl.ds(i * middle, middle), cols] = part[:middle]
                    row_grads[pl.ds((number + i) * middle, middle), cols] = part[middle:]
                else:
                    start = at.start + at.start // middle * (number - 1) * middle + i * middle
                    row_grads[pl.ds(pl.multiple_of(start, at.size), at.size), cols] = part

        to_own = dot(grad_gate, gate_own[...], NT) + dot(grad_up, up_own[...], NT)
        put(to_own.astype(BF16), pl.ds(0, half))
        to_other = dot(grad_gate, gate_other[...], NT) + dot(grad_up, up_other[...], NT)
        put(to_other.astype(BF16), pl.ds(half, half))
        put(jnp.where(is_own, gate_grads, 0.0).astype(BF16), pl.ds(features, lanes))
        for i in range(number):
            part = slice(i * at.size, (i + 1) * at.size)
            grads[i, at, pl.ds(0, width)] = grad_gate[part]
            grads[i, at, pl.ds(width, width)] = grad_up[part]
            scaled_hidden[i, at, :] = scaled[part]

    for_chunks(count, step, CHUNK // number)


def weight_kernel(numbers, place, *refs):
    keep_in, keep_down, give_gate, give_up, give_down = refs[-5:]
    parts, begin = [], 0
    for number in numbers:
        grads, hidden = refs[begin + number : begin + number + 2]
        parts += [(refs[begin + i], grads.at[i], hidden.at[i]) for i in range(number)]
        begin += number + 2
    half, width = give_gate.shape
    own, other = own_other(place, half)
    dys_own, dys_other = own_other(place, half, 2 * half)
    steps = max(1, min(p[0].shape[0] for p in parts) // CHUNK)

    def products(i, cols, dys_cols):
        def gather(which, cols):
            values = []
            for part in parts:
                size = part[0].shape[0] // steps
                start = i * size
                at = pl.ds(start if steps == 1 else pl.multiple_of(start, size), size)
                values.append(part[which][at, cols])
            return jnp.concatenate(values, 0)

        into = dot(gather(0, cols), gather(1, pl.ds(0, 2 * width)), TN)
        return into, dot(gather(2, pl.ds(0, width)), gather(0, dys_cols), TN)

    def hand_over(into, down):
        give_gate[...] = into[:, :width].astype(BF16)
        give_up[...] = into[:, width:].astype(BF16)
        give_down[...] = down.astype(BF16)

    if steps == 1:
        hand_over(*products(0, other, dys_other))
        keep_in[...], keep_down[...] = products(0, own, dys_own)
    else:
        for cols, dys_cols, is_given in ((other, dys_other, True), (own, dys_own, False)):
            keep_in[...] = jnp.zeros_like(keep_in)
            keep_down[...] = jnp.zeros_like(keep_down)

            @pl.loop(0, steps)
            def _(i):
                into, down = products(i, cols, dys_cols)
                keep_in[...] += into
                keep_down[...] += down

            if is_given:
                hand_over(keep_in[...], keep_down[...])


def settle_kernel(keep_in, keep_down, got_gate, got_up, got_down, gate, up, down, done):
    width = gate.shape[1]
    left, right = pl.ds(0, width), pl.ds(width, width)
    gate[...] = (keep_in[:, left] + got_gate[...].astype(F32)).astype(BF16)
    up[...] = (keep_in[:, right] + got_up[...].astype(F32)).astype(BF16)
    down[...] = (keep_down[...] + got_down[...].astype(F32)).astype(BF16)
    done[...] = jnp.zeros_like(done)


def finish_kernel(place, *refs):
    ids, grad_tokens, grad_gates = refs[-3:]
    total = refs[0][...].astype(F32)
    for part in refs[1:-3]:
        total = total + part[...].astype(F32)
    half = grad_tokens.shape[1] // 2
    lanes = total.shape[1] - 2 * half
    own, other = own_other(place, half)
    grad_tokens[:, own] = total[:, :half].astype(BF16)
    grad_tokens[:, other] = total[:, half : 2 * half].astype(BF16)
    gates = dot(unit_matrix(lanes), total[:, 2 * half :].astype(BF16), NT)
    names = ids[...]
    expert = lax.broadcasted_iota(jnp.int32, gates.shape, 0)
    row = lax.broadcasted_iota(jnp.int32, names.shape, 0)
    out = jnp.zeros(names.shape, F32)
    for k in range(names.shape[0]):
        picked = jnp.sum(jnp.where(names[k : k + 1, :] == expert, gates, 0.0), 0, keepdims=True)
        out = jnp.where(row == k, picked, out)
    grad_gates[...] = out.astype(BF16)


def call(kernel, outs, place, *args, after=(), small=True, arrives=0, leaves=0, flops=0, limit=2):
    used = len(args)
    limit = (limit if small else 56) * 2**20
    if small:
        args = [
            pltpu.with_memory_space_constraint(x, pltpu.VMEM) if i < used - arrives else x
            for i, x in enumerate(args)
        ]
    out_shape = [
        pltpu.VMEM(s, d) if small and i >= leaves else jax.ShapeDtypeStruct(s, d)
        for i, (s, d) in enumerate(outs)
    ]

    scalars = () if place is None else (place,)
    read = len(scalars) + used

    def run(*refs):
        kernel(*refs[:read], *refs[read + len(after) :])

    vmem = pl.BlockSpec(memory_space=pltpu.VMEM)
    return pl.pallas_call(
        run,
        out_shape=out_shape,
        in_specs=[pl.BlockSpec(memory_space=pltpu.SMEM)] * len(scalars)
        + [vmem] * used
        + [pl.BlockSpec(memory_space=pl.ANY)] * len(after),
        out_specs=[vmem] * len(outs),
        compiler_params=pltpu.CompilerParams(vmem_limit_bytes=limit),
        cost_estimate=pl.CostEstimate(flops=flops, bytes_accessed=0, transcendentals=0),
        name=kernel.__name__.replace("<lambda>", "weight_kernel"),
    )(*scalars, *args, *after)


def chip_bits(chip_count):
    bits = []
    bit = chip_count // 2
    while bit:
        bits.append(bit)
        bit //= 2
    return (bits[:-2] + bits[-2:][::-1], bits)


def body(tokens, cotangent, expert_ids, gate_probs, gate_half, up_half, down_half):
    chip_count = lax.axis_size("expert") * lax.axis_size("chip")
    tok_rows, features = tokens.shape
    half = features // 2
    width = gate_half.shape[2]
    lanes = -(-chip_count // 128) * 128
    member = lax.axis_index("core")
    own_expert = lax.axis_index("expert") * lax.axis_size("chip") + lax.axis_index("chip")
    place = jnp.stack([member, own_expert]).astype(jnp.int32)
    bits = chip_bits(chip_count)
    far = len(bits[0]) - 4
    small = far == 0

    def exchange(x, offsets):
        pairs = [
            (2 * chip + core, 2 * (chip ^ offsets[core]) + core)
            for chip in range(chip_count)
            for core in range(2)
        ]
        return lax.ppermute(x, DEVICES, pairs)

    steps = list(zip(*bits))
    near_a, near_b = steps[-2:]
    up_two, up_one = steps[far][0], steps[far + 1][0]

    before = []

    def run(kernel, outs, place, *args, **kwargs):
        results = call(kernel, outs, place, *args, after=tuple(before), small=small, **kwargs)
        before[:] = results[-1:]
        return results

    hbm = pl.BlockSpec(memory_space=pltpu.HBM)
    arguments = (tokens, cotangent, expert_ids.T, gate_probs.T)
    block = pl.pallas_call(
        prepare_kernel,
        out_shape=pltpu.VMEM((tok_rows, 2 * features + lanes), BF16),
        in_specs=[hbm] * 4,
        out_specs=pl.BlockSpec(memory_space=pltpu.VMEM),
        scratch_shapes=[
            pltpu.VMEM(expert_ids.shape[::-1], jnp.int32),
            pltpu.VMEM(gate_probs.shape[::-1], BF16),
            pltpu.SemaphoreType.DMA((4,)),
        ],
        name="prepare_kernel",
    )(*(pltpu.with_memory_space_constraint(x, pltpu.HBM) for x in arguments))

    for step in steps[:far]:
        block = jnp.concatenate([block, exchange(block, step)], 0)

    offsets = (up_two, up_one, up_one ^ up_two)
    rows = block.shape[0]
    columns = features + lanes

    gate_own, up_own, down_own = gate_half[0], up_half[0], down_half[0]
    gate_other, up_other, down_other = swap_core(gate_own), swap_core(up_own), swap_core(down_own)
    weights = [gate_own, gate_other, up_own, up_other, down_own, down_other]
    numbers, saved = [], []

    def at_offset(x, i):
        return exchange(x, (offsets[i], offsets[i]))

    def join(first, second, flops=0):
        shape = (2 * first.shape[0], first.shape[1])
        return run(join_kernel, [(shape, BF16)], None, first, second, flops=flops)[0]

    def after_all(x, *others):
        before.extend(others)
        return run(pass_kernel, [(x.shape, BF16)], None, x)[0]

    def expert(*blocks):
        number, count = len(blocks), blocks[0].shape[0]
        row_grads, grads, hidden = run(
            expert_kernel,
            [
                ((number * count, columns), BF16),
                ((number, count, 2 * width), BF16),
                ((number, count, width), BF16),
            ],
            place, *blocks, *weights, limit=6, flops=6 * 10**9,
        )
        numbers.append(number)
        saved.extend([*blocks, grads, hidden])
        return row_grads

    def split(kept, got, types, flops=0):
        shape = (kept.shape[0] // 2, columns)
        return run(split_kernel, [(shape, t) for t in types], None, kept, got, flops=flops)

    def collect(total, part):
        return run(add_kernel, [(total.shape, F32)], None, total, part)[0]

    far_two = at_offset(block, 0)
    first_own = join(block, exchange(block, near_a))
    second_own = exchange(first_own, near_b)
    near_1 = at_offset(join(block, far_two, flops=4 * 10**9), 1)
    second_own = after_all(second_own)
    first_two = join(far_two, exchange(far_two, near_a))
    second_two = exchange(first_two, near_b)
    near_1 = after_all(near_1)
    got_near = exchange(near_1, near_a)
    weights[-1] = after_all(weights[-1])
    kept_0 = expert(first_own, first_two)
    first_1 = join(near_1, got_near)
    second_1 = exchange(first_1, near_b)
    give_0 = expert(second_own, second_two)
    kept_1 = expert(first_1)
    got_0 = exchange(after_all(give_0, second_1), near_b)
    got_1 = exchange(expert(second_1), near_b)
    kept_0, give = split(kept_0, got_0, (F32, BF16))
    got_0 = exchange(give, near_a)
    kept_1, give = split(kept_1, got_1, (F32, BF16))
    got_1 = exchange(give, near_a)
    total, give = split(kept_0, got_0, (F32, BF16))
    back_two = at_offset(give, 0)
    keep_in, keep_down, *gives = run(
        lambda *refs: weight_kernel(tuple(numbers), *refs),
        [
            ((half, 2 * width), F32),
            ((width, half), F32),
            ((half, width), BF16),
            ((half, width), BF16),
            ((width, half), BF16),
        ],
        place, *saved, limit=10, flops=6 * 10**9,
    )
    gots = [swap_core(give) for give in gives]
    give_one, give_both = split(kept_1, got_1, (BF16, BF16), flops=6 * 10**9)
    back_one, back_both = at_offset(give_one, 1), at_offset(give_both, 2)
    grad_gate, grad_up, grad_down, _ = run(
        settle_kernel,
        [((half, width), BF16), ((half, width), BF16), ((width, half), BF16), ((8, 128), F32)],
        None, keep_in, keep_down, *gots, leaves=3, limit=6,
    )
    total = collect(total, back_two)
    total = collect(total, back_one)

    parts = (total, back_both)
    if far:
        total = total + back_both.astype(F32)
        for step in reversed(steps[:far]):
            middle = total.shape[0] // 2
            total = total[:middle] + exchange(total[middle:].astype(BF16), step).astype(F32)
        parts = (total,)
    grad_tokens, grad_gates = run(
        finish_kernel,
        [((tok_rows, features), BF16), (expert_ids.shape[::-1], BF16)],
        place, *parts, expert_ids.T, arrives=1, leaves=2,
    )
    return grad_tokens, grad_gates.T, grad_gate[None], grad_up[None], grad_down[None]


def solution(mesh):
    shape = mesh.shape
    devices = mesh.devices.reshape(shape["dom"], shape["expert"], shape["dp"] // 2, 2)
    fine = Mesh(devices, ("dom", "expert", "chip", "core"))
    every = ("dom", "expert", "chip", "core")
    flat, cube = P(every, None), P(every, None, None)
    return jax.shard_map(
        body,
        mesh=fine,
        in_specs=(flat, flat, flat, flat, cube, cube, cube),
        out_specs=(flat, flat, cube, cube, cube),
        check_vma=False,
    )
```

```python
import jax
import jax.numpy as jnp
from jax import lax
from jax.experimental import pallas as pl
from jax.experimental.pallas import tpu as pltpu
from jax.sharding import Mesh, PartitionSpec as P

DEVICES = ("expert", "chip", "core")
F32, BF16 = jnp.float32, jnp.bfloat16
NN = (((1,), (0,)), ((), ()))
NT = (((1,), (1,)), ((), ()))
TN = (((0,), (0,)), ((), ()))
CHUNK = 128


def dot(a, b, dims):
    return lax.dot_general(a, b, dims, preferred_element_type=F32)


def swap_core(x):
    return lax.ppermute(x, "core", [(0, 1), (1, 0)])


def for_chunks(rows, step, chunk):
    if rows <= chunk:
        step(pl.ds(0, rows))
    else:

        @pl.loop(0, rows // chunk)
        def _(i):
            step(pl.ds(pl.multiple_of(i * chunk, chunk), chunk))


def own_other(place_ref, half, start=0):
    member = place_ref[0]
    own = pl.ds(pl.multiple_of(start + member * half, half), half)
    other = pl.ds(pl.multiple_of(start + (1 - member) * half, half), half)
    return own, other


def prepare_kernel(tokens, cotangent, ids, probs, out, ids_here, probs_here, sems):
    features = tokens.shape[1]
    lanes = out.shape[1] - 2 * features
    copies = [
        pltpu.make_async_copy(source, target, sems.at[i])
        for i, (source, target) in enumerate(
            (
                (ids, ids_here),
                (probs, probs_here),
                (tokens, out.at[:, pl.ds(0, features)]),
                (cotangent, out.at[:, pl.ds(features, features)]),
            )
        )
    ]
    for copy in copies:
        copy.start()
    copies[0].wait()
    copies[1].wait()
    names, given = ids_here[...], probs_here[...].astype(F32)
    expert = lax.broadcasted_iota(jnp.int32, (lanes, names.shape[1]), 0)
    weight = jnp.zeros(expert.shape, F32)
    for k in range(names.shape[0]):
        weight = jnp.where(names[k : k + 1, :] == expert, given[k : k + 1, :], weight)
    turned = dot(weight.astype(BF16), unit_matrix(lanes), TN)
    out[:, pl.ds(2 * features, lanes)] = turned.astype(BF16)
    copies[2].wait()
    copies[3].wait()


def unit_matrix(size):
    row = lax.broadcasted_iota(jnp.int32, (size, size), 0)
    column = lax.broadcasted_iota(jnp.int32, (size, size), 1)
    return jnp.where(row == column, 1.0, 0.0).astype(BF16)


def join_kernel(first, second, out):
    rows = first.shape[0]
    out[pl.ds(0, rows), :] = first[...]
    out[pl.ds(rows, rows), :] = second[...]


def split_kernel(kept, got, keep, give):
    rows = keep.shape[0]
    upper, lower = pl.ds(0, rows), pl.ds(rows, rows)
    give[...] = (kept[lower, :].astype(F32) + got[lower, :].astype(F32)).astype(give.dtype)
    keep[...] = (kept[upper, :].astype(F32) + got[upper, :].astype(F32)).astype(keep.dtype)


def add_kernel(kept, got, total):
    total[...] = (kept[...] + got[...].astype(F32)).astype(total.dtype)


def pass_kernel(source, out):
    out[...] = source[...]


def expert_kernel(place, *refs):
    blocks, refs = refs[:-9], refs[-9:]
    gate_own, gate_other, up_own, up_other, down_own, down_other = refs[:6]
    row_grads, grads, scaled_hidden = refs[6:]
    half, width = gate_own.shape
    features = 2 * half
    number, count = len(blocks), blocks[0].shape[0]
    lanes = blocks[0].shape[1] - 2 * features
    own, other = own_other(place, half)
    dys_own, dys_other = own_other(place, half, features)

    def step(at):
        def take(cols):
            return jnp.concatenate([block[at, cols] for block in blocks], 0)

        mine, rest = take(own), take(other)
        pre_gate = dot(mine, gate_own[...], NN) + dot(rest, gate_other[...], NN)
        pre_up = dot(mine, up_own[...], NN) + dot(rest, up_other[...], NN)
        back = dot(take(dys_own), down_own[...], NT) + dot(take(dys_other), down_other[...], NT)
        sig = jax.nn.sigmoid(pre_gate)
        active = pre_gate * sig
        slope = sig * (1.0 + pre_gate * (1.0 - sig))
        hidden = active * pre_up
        lane = lax.broadcasted_iota(jnp.int32, (back.shape[0], lanes), 1)
        is_own = lane == place[1]
        gates = jnp.where(is_own, take(pl.ds(2 * features, lanes)).astype(F32), 0.0)
        gates = jnp.sum(gates, 1, keepdims=True)
        gate_grads = jnp.sum(hidden * back, 1, keepdims=True)
        back = back * gates
        grad_gate = (back * pre_up * slope).astype(BF16)
        grad_up = (back * active).astype(BF16)
        scaled = (hidden * gates).astype(BF16)
        middle = count // 2

        def put(rows, cols):
            for i in range(number):
                part = rows[i * at.size : (i + 1) * at.size]
                if at.size == count:
                    row_grads[pl.ds(i * middle, middle), cols] = part[:middle]
                    row_grads[pl.ds((number + i) * middle, middle), cols] = part[middle:]
                else:
                    start = at.start + at.start // middle * (number - 1) * middle + i * middle
                    row_grads[pl.ds(pl.multiple_of(start, at.size), at.size), cols] = part

        to_own = dot(grad_gate, gate_own[...], NT) + dot(grad_up, up_own[...], NT)
        put(to_own.astype(BF16), pl.ds(0, half))
        to_other = dot(grad_gate, gate_other[...], NT) + dot(grad_up, up_other[...], NT)
        put(to_other.astype(BF16), pl.ds(half, half))
        put(jnp.where(is_own, gate_grads, 0.0).astype(BF16), pl.ds(features, lanes))
        for i in range(number):
            part = slice(i * at.size, (i + 1) * at.size)
            grads[i, at, pl.ds(0, width)] = grad_gate[part]
            grads[i, at, pl.ds(width, width)] = grad_up[part]
            scaled_hidden[i, at, :] = scaled[part]

    for_chunks(count, step, CHUNK // number)


def weight_kernel(numbers, place, *refs):
    keep_in, keep_down, give_gate, give_up, give_down = refs[-5:]
    parts, begin = [], 0
    for number in numbers:
        grads, hidden = refs[begin + number : begin + number + 2]
        parts += [(refs[begin + i], grads.at[i], hidden.at[i]) for i in range(number)]
        begin += number + 2
    half, width = give_gate.shape
    own, other = own_other(place, half)
    dys_own, dys_other = own_other(place, half, 2 * half)
    steps = max(1, min(p[0].shape[0] for p in parts) // CHUNK)

    def products(i, cols, dys_cols):
        def gather(which, cols):
            values = []
            for part in parts:
                size = part[0].shape[0] // steps
                start = i * size
                at = pl.ds(start if steps == 1 else pl.multiple_of(start, size), size)
                values.append(part[which][at, cols])
            return jnp.concatenate(values, 0)

        into = dot(gather(0, cols), gather(1, pl.ds(0, 2 * width)), TN)
        return into, dot(gather(2, pl.ds(0, width)), gather(0, dys_cols), TN)

    def hand_over(into, down):
        give_gate[...] = into[:, :width].astype(BF16)
        give_up[...] = into[:, width:].astype(BF16)
        give_down[...] = down.astype(BF16)

    if steps == 1:
        hand_over(*products(0, other, dys_other))
        keep_in[...], keep_down[...] = products(0, own, dys_own)
    else:
        for cols, dys_cols, is_given in ((other, dys_other, True), (own, dys_own, False)):
            keep_in[...] = jnp.zeros_like(keep_in)
            keep_down[...] = jnp.zeros_like(keep_down)

            @pl.loop(0, steps)
            def _(i):
                into, down = products(i, cols, dys_cols)
                keep_in[...] += into
                keep_down[...] += down

            if is_given:
                hand_over(keep_in[...], keep_down[...])


def settle_kernel(keep_in, keep_down, got_gate, got_up, got_down, gate, up, down, done):
    width = gate.shape[1]
    left, right = pl.ds(0, width), pl.ds(width, width)
    gate[...] = (keep_in[:, left] + got_gate[...].astype(F32)).astype(BF16)
    up[...] = (keep_in[:, right] + got_up[...].astype(F32)).astype(BF16)
    down[...] = (keep_down[...] + got_down[...].astype(F32)).astype(BF16)
    done[...] = jnp.zeros_like(done)


def finish_kernel(place, *refs):
    ids, grad_tokens, grad_gates = refs[-3:]
    total = refs[0][...].astype(F32)
    for part in refs[1:-3]:
        total = total + part[...].astype(F32)
    half = grad_tokens.shape[1] // 2
    lanes = total.shape[1] - 2 * half
    own, other = own_other(place, half)
    grad_tokens[:, own] = total[:, :half].astype(BF16)
    grad_tokens[:, other] = total[:, half : 2 * half].astype(BF16)
    gates = dot(unit_matrix(lanes), total[:, 2 * half :].astype(BF16), NT)
    names = ids[...]
    expert = lax.broadcasted_iota(jnp.int32, gates.shape, 0)
    row = lax.broadcasted_iota(jnp.int32, names.shape, 0)
    out = jnp.zeros(names.shape, F32)
    for k in range(names.shape[0]):
        picked = jnp.sum(jnp.where(names[k : k + 1, :] == expert, gates, 0.0), 0, keepdims=True)
        out = jnp.where(row == k, picked, out)
    grad_gates[...] = out.astype(BF16)


def call(kernel, outs, place, *args, after=(), small=True, arrives=0, leaves=0, flops=0, limit=2):
    used = len(args)
    limit = (limit if small else 56) * 2**20
    if small:
        args = [
            pltpu.with_memory_space_constraint(x, pltpu.VMEM) if i < used - arrives else x
            for i, x in enumerate(args)
        ]
    out_shape = [
        pltpu.VMEM(s, d) if small and i >= leaves else jax.ShapeDtypeStruct(s, d)
        for i, (s, d) in enumerate(outs)
    ]

    scalars = () if place is None else (place,)
    read = len(scalars) + used

    def run(*refs):
        kernel(*refs[:read], *refs[read + len(after) :])

    vmem = pl.BlockSpec(memory_space=pltpu.VMEM)
    return pl.pallas_call(
        run,
        out_shape=out_shape,
        in_specs=[pl.BlockSpec(memory_space=pltpu.SMEM)] * len(scalars)
        + [vmem] * used
        + [pl.BlockSpec(memory_space=pl.ANY)] * len(after),
        out_specs=[vmem] * len(outs),
        compiler_params=pltpu.CompilerParams(vmem_limit_bytes=limit),
        cost_estimate=pl.CostEstimate(flops=flops, bytes_accessed=0, transcendentals=0),
        name=kernel.__name__.replace("<lambda>", "weight_kernel"),
    )(*scalars, *args, *after)


def chip_bits(chip_count):
    bits = []
    bit = chip_count // 2
    while bit:
        bits.append(bit)
        bit //= 2
    return (bits[:-2] + bits[-2:][::-1], bits)


def body(tokens, cotangent, expert_ids, gate_probs, gate_half, up_half, down_half):
    chip_count = lax.axis_size("expert") * lax.axis_size("chip")
    tok_rows, features = tokens.shape
    half = features // 2
    width = gate_half.shape[2]
    lanes = -(-chip_count // 128) * 128
    member = lax.axis_index("core")
    own_expert = lax.axis_index("expert") * lax.axis_size("chip") + lax.axis_index("chip")
    place = jnp.stack([member, own_expert]).astype(jnp.int32)
    bits = chip_bits(chip_count)
    far = len(bits[0]) - 4
    small = far == 0

    def exchange(x, offsets):
        pairs = [
            (2 * chip + core, 2 * (chip ^ offsets[core]) + core)
            for chip in range(chip_count)
            for core in range(2)
        ]
        return lax.ppermute(x, DEVICES, pairs)

    steps = list(zip(*bits))
    near_a, near_b = steps[-2:]
    up_two, up_one = steps[far][0], steps[far + 1][0]

    before = []

    def run(kernel, outs, place, *args, **kwargs):
        results = call(kernel, outs, place, *args, after=tuple(before), small=small, **kwargs)
        before[:] = results[-1:]
        return results

    hbm = pl.BlockSpec(memory_space=pltpu.HBM)
    arguments = (tokens, cotangent, expert_ids.T, gate_probs.T)
    block = pl.pallas_call(
        prepare_kernel,
        out_shape=pltpu.VMEM((tok_rows, 2 * features + lanes), BF16),
        in_specs=[hbm] * 4,
        out_specs=pl.BlockSpec(memory_space=pltpu.VMEM),
        scratch_shapes=[
            pltpu.VMEM(expert_ids.shape[::-1], jnp.int32),
            pltpu.VMEM(gate_probs.shape[::-1], BF16),
            pltpu.SemaphoreType.DMA((4,)),
        ],
        name="prepare_kernel",
    )(*(pltpu.with_memory_space_constraint(x, pltpu.HBM) for x in arguments))

    for step in steps[:far]:
        block = jnp.concatenate([block, exchange(block, step)], 0)

    offsets = (up_two, up_one, up_one ^ up_two)
    rows = block.shape[0]
    columns = features + lanes

    gate_own, up_own, down_own = gate_half[0], up_half[0], down_half[0]
    gate_other, up_other, down_other = swap_core(gate_own), swap_core(up_own), swap_core(down_own)
    weights = [gate_own, gate_other, up_own, up_other, down_own, down_other]
    numbers, saved = [], []

    def at_offset(x, i):
        return exchange(x, (offsets[i], offsets[i]))

    def join(first, second, flops=0):
        shape = (2 * first.shape[0], first.shape[1])
        return run(join_kernel, [(shape, BF16)], None, first, second, flops=flops)[0]

    def after_all(x, *others):
        before.extend(others)
        return run(pass_kernel, [(x.shape, BF16)], None, x)[0]

    def expert(*blocks):
        number, count = len(blocks), blocks[0].shape[0]
        row_grads, grads, hidden = run(
            expert_kernel,
            [
                ((number * count, columns), BF16),
                ((number, count, 2 * width), BF16),
                ((number, count, width), BF16),
            ],
            place, *blocks, *weights, limit=6, flops=6 * 10**9,
        )
        numbers.append(number)
        saved.extend([*blocks, grads, hidden])
        return row_grads

    def split(kept, got, types, flops=0):
        shape = (kept.shape[0] // 2, columns)
        return run(split_kernel, [(shape, t) for t in types], None, kept, got, flops=flops)

    def collect(total, part):
        return run(add_kernel, [(total.shape, F32)], None, total, part)[0]

    far_two = at_offset(block, 0)
    first_own = join(block, exchange(block, near_a))
    second_own = exchange(first_own, near_b)
    near_1 = at_offset(join(block, far_two, flops=4 * 10**9), 1)
    second_own = after_all(second_own)
    first_two = join(far_two, exchange(far_two, near_a))
    second_two = exchange(first_two, near_b)
    near_1 = after_all(near_1)
    got_near = exchange(near_1, near_a)
    weights[-1] = after_all(weights[-1])
    kept_0 = expert(first_own, first_two)
    first_1 = join(near_1, got_near)
    second_1 = exchange(first_1, near_b)
    give_0 = expert(second_own, second_two)
    kept_1 = expert(first_1)
    got_0 = exchange(after_all(give_0, second_1), near_b)
    got_1 = exchange(expert(second_1), near_b)
    kept_0, give = split(kept_0, got_0, (F32, BF16))
    got_0 = exchange(give, near_a)
    keep_in, keep_down, *gives = run(
        lambda *refs: weight_kernel(tuple(numbers), *refs),
        [
            ((half, 2 * width), F32),
            ((width, half), F32),
            ((half, width), BF16),
            ((half, width), BF16),
            ((width, half), BF16),
        ],
        place, *saved, limit=10, flops=6 * 10**9,
    )
    kept_1, give = split(kept_1, got_1, (F32, BF16))
    got_1 = exchange(give, near_a)
    total, give = split(kept_0, got_0, (F32, BF16))
    back_two = at_offset(give, 0)
    gots = [swap_core(give) for give in gives]
    give_one, give_both = split(kept_1, got_1, (BF16, BF16), flops=6 * 10**9)
    back_one, back_both = at_offset(give_one, 1), at_offset(give_both, 2)
    grad_gate, grad_up, grad_down, _ = run(
        settle_kernel,
        [((half, width), BF16), ((half, width), BF16), ((width, half), BF16), ((8, 128), F32)],
        None, keep_in, keep_down, *gots, leaves=3, limit=6,
    )
    total = collect(total, back_two)
    total = collect(total, back_one)

    parts = (total, back_both)
    if far:
        total = total + back_both.astype(F32)
        for step in reversed(steps[:far]):
            middle = total.shape[0] // 2
            total = total[:middle] + exchange(total[middle:].astype(BF16), step).astype(F32)
        parts = (total,)
    grad_tokens, grad_gates = run(
        finish_kernel,
        [((tok_rows, features), BF16), (expert_ids.shape[::-1], BF16)],
        place, *parts, expert_ids.T, arrives=1, leaves=2,
    )
    return grad_tokens, grad_gates.T, grad_gate[None], grad_up[None], grad_down[None]


def solution(mesh):
    shape = mesh.shape
    devices = mesh.devices.reshape(shape["dom"], shape["expert"], shape["dp"] // 2, 2)
    fine = Mesh(devices, ("dom", "expert", "chip", "core"))
    every = ("dom", "expert", "chip", "core")
    flat, cube = P(every, None), P(every, None, None)
    return jax.shard_map(
        body,
        mesh=fine,
        in_specs=(flat, flat, flat, flat, cube, cube, cube),
        out_specs=(flat, flat, cube, cube, cube),
        check_vma=False,
    )
```

```python
import jax
import jax.numpy as jnp
from jax import lax
from jax.experimental import pallas as pl
from jax.experimental.pallas import tpu as pltpu
from jax.sharding import Mesh, PartitionSpec as P

DEVICES = ("expert", "chip", "core")
F32, BF16 = jnp.float32, jnp.bfloat16
NN = (((1,), (0,)), ((), ()))
NT = (((1,), (1,)), ((), ()))
TN = (((0,), (0,)), ((), ()))
CHUNK = 128


def dot(a, b, dims):
    return lax.dot_general(a, b, dims, preferred_element_type=F32)


def swap_core(x):
    return lax.ppermute(x, "core", [(0, 1), (1, 0)])


def for_chunks(rows, step, chunk):
    if rows <= chunk:
        step(pl.ds(0, rows))
    else:

        @pl.loop(0, rows // chunk)
        def _(i):
            step(pl.ds(pl.multiple_of(i * chunk, chunk), chunk))


def own_other(place_ref, half, start=0):
    member = place_ref[0]
    own = pl.ds(pl.multiple_of(start + member * half, half), half)
    other = pl.ds(pl.multiple_of(start + (1 - member) * half, half), half)
    return own, other


def prepare_kernel(tokens, cotangent, ids, probs, out, ids_here, probs_here, sems):
    features = tokens.shape[1]
    lanes = out.shape[1] - 2 * features
    copies = [
        pltpu.make_async_copy(source, target, sems.at[i])
        for i, (source, target) in enumerate(
            (
                (ids, ids_here),
                (probs, probs_here),
                (tokens, out.at[:, pl.ds(0, features)]),
                (cotangent, out.at[:, pl.ds(features, features)]),
            )
        )
    ]
    for copy in copies:
        copy.start()
    copies[0].wait()
    copies[1].wait()
    names, given = ids_here[...], probs_here[...].astype(F32)
    expert = lax.broadcasted_iota(jnp.int32, (lanes, names.shape[1]), 0)
    weight = jnp.zeros(expert.shape, F32)
    for k in range(names.shape[0]):
        weight = jnp.where(names[k : k + 1, :] == expert, given[k : k + 1, :], weight)
    turned = dot(weight.astype(BF16), unit_matrix(lanes), TN)
    out[:, pl.ds(2 * features, lanes)] = turned.astype(BF16)
    copies[2].wait()
    copies[3].wait()


def unit_matrix(size):
    row = lax.broadcasted_iota(jnp.int32, (size, size), 0)
    column = lax.broadcasted_iota(jnp.int32, (size, size), 1)
    return jnp.where(row == column, 1.0, 0.0).astype(BF16)


def join_kernel(first, second, out):
    rows = first.shape[0]
    out[pl.ds(0, rows), :] = first[...]
    out[pl.ds(rows, rows), :] = second[...]


def split_kernel(kept, got, keep, give):
    rows = keep.shape[0]
    upper, lower = pl.ds(0, rows), pl.ds(rows, rows)
    give[...] = (kept[lower, :].astype(F32) + got[lower, :].astype(F32)).astype(give.dtype)
    keep[...] = (kept[upper, :].astype(F32) + got[upper, :].astype(F32)).astype(keep.dtype)


def add_kernel(kept, got, total):
    total[...] = (kept[...] + got[...].astype(F32)).astype(total.dtype)


def pass_kernel(source, out):
    out[...] = source[...]


def expert_kernel(place, *refs):
    blocks, refs = refs[:-9], refs[-9:]
    gate_own, gate_other, up_own, up_other, down_own, down_other = refs[:6]
    row_grads, grads, scaled_hidden = refs[6:]
    half, width = gate_own.shape
    features = 2 * half
    number, count = len(blocks), blocks[0].shape[0]
    lanes = blocks[0].shape[1] - 2 * features
    own, other = own_other(place, half)
    dys_own, dys_other = own_other(place, half, features)

    def step(at):
        def take(cols):
            return jnp.concatenate([block[at, cols] for block in blocks], 0)

        mine, rest = take(own), take(other)
        pre_gate = dot(mine, gate_own[...], NN) + dot(rest, gate_other[...], NN)
        pre_up = dot(mine, up_own[...], NN) + dot(rest, up_other[...], NN)
        back = dot(take(dys_own), down_own[...], NT) + dot(take(dys_other), down_other[...], NT)
        sig = jax.nn.sigmoid(pre_gate)
        active = pre_gate * sig
        slope = sig * (1.0 + pre_gate * (1.0 - sig))
        hidden = active * pre_up
        lane = lax.broadcasted_iota(jnp.int32, (back.shape[0], lanes), 1)
        is_own = lane == place[1]
        gates = jnp.where(is_own, take(pl.ds(2 * features, lanes)).astype(F32), 0.0)
        gates = jnp.sum(gates, 1, keepdims=True)
        gate_grads = jnp.sum(hidden * back, 1, keepdims=True)
        back = back * gates
        grad_gate = (back * pre_up * slope).astype(BF16)
        grad_up = (back * active).astype(BF16)
        scaled = (hidden * gates).astype(BF16)
        middle = count // 2

        def put(rows, cols):
            for i in range(number):
                part = rows[i * at.size : (i + 1) * at.size]
                if at.size == count:
                    row_grads[pl.ds(i * middle, middle), cols] = part[:middle]
                    row_grads[pl.ds((number + i) * middle, middle), cols] = part[middle:]
                else:
                    start = at.start + at.start // middle * (number - 1) * middle + i * middle
                    row_grads[pl.ds(pl.multiple_of(start, at.size), at.size), cols] = part

        to_own = dot(grad_gate, gate_own[...], NT) + dot(grad_up, up_own[...], NT)
        put(to_own.astype(BF16), pl.ds(0, half))
        to_other = dot(grad_gate, gate_other[...], NT) + dot(grad_up, up_other[...], NT)
        put(to_other.astype(BF16), pl.ds(half, half))
        put(jnp.where(is_own, gate_grads, 0.0).astype(BF16), pl.ds(features, lanes))
        for i in range(number):
            part = slice(i * at.size, (i + 1) * at.size)
            grads[i, at, pl.ds(0, width)] = grad_gate[part]
            grads[i, at, pl.ds(width, width)] = grad_up[part]
            scaled_hidden[i, at, :] = scaled[part]

    for_chunks(count, step, CHUNK // number)


def weight_kernel(numbers, place, *refs):
    keep_in, keep_down, give_gate, give_up, give_down = refs[-5:]
    parts, begin = [], 0
    for number in numbers:
        grads, hidden = refs[begin + number : begin + number + 2]
        parts += [(refs[begin + i], grads.at[i], hidden.at[i]) for i in range(number)]
        begin += number + 2
    half, width = give_gate.shape
    own, other = own_other(place, half)
    dys_own, dys_other = own_other(place, half, 2 * half)
    steps = max(1, min(p[0].shape[0] for p in parts) // CHUNK)

    def products(i, cols, dys_cols):
        def gather(which, cols):
            values = []
            for part in parts:
                size = part[0].shape[0] // steps
                start = i * size
                at = pl.ds(start if steps == 1 else pl.multiple_of(start, size), size)
                values.append(part[which][at, cols])
            return jnp.concatenate(values, 0)

        into = dot(gather(0, cols), gather(1, pl.ds(0, 2 * width)), TN)
        return into, dot(gather(2, pl.ds(0, width)), gather(0, dys_cols), TN)

    def hand_over(into, down):
        give_gate[...] = into[:, :width].astype(BF16)
        give_up[...] = into[:, width:].astype(BF16)
        give_down[...] = down.astype(BF16)

    if steps == 1:
        hand_over(*products(0, other, dys_other))
        keep_in[...], keep_down[...] = products(0, own, dys_own)
    else:
        for cols, dys_cols, is_given in ((other, dys_other, True), (own, dys_own, False)):
            keep_in[...] = jnp.zeros_like(keep_in)
            keep_down[...] = jnp.zeros_like(keep_down)

            @pl.loop(0, steps)
            def _(i):
                into, down = products(i, cols, dys_cols)
                keep_in[...] += into
                keep_down[...] += down

            if is_given:
                hand_over(keep_in[...], keep_down[...])


def settle_kernel(keep_in, keep_down, got_gate, got_up, got_down, gate, up, down, done):
    width = gate.shape[1]
    left, right = pl.ds(0, width), pl.ds(width, width)
    gate[...] = (keep_in[:, left] + got_gate[...].astype(F32)).astype(BF16)
    up[...] = (keep_in[:, right] + got_up[...].astype(F32)).astype(BF16)
    down[...] = (keep_down[...] + got_down[...].astype(F32)).astype(BF16)
    done[...] = jnp.zeros_like(done)


def finish_kernel(place, *refs):
    ids, grad_tokens, grad_gates = refs[-3:]
    total = refs[0][...].astype(F32)
    for part in refs[1:-3]:
        total = total + part[...].astype(F32)
    half = grad_tokens.shape[1] // 2
    lanes = total.shape[1] - 2 * half
    own, other = own_other(place, half)
    grad_tokens[:, own] = total[:, :half].astype(BF16)
    grad_tokens[:, other] = total[:, half : 2 * half].astype(BF16)
    gates = dot(unit_matrix(lanes), total[:, 2 * half :].astype(BF16), NT)
    names = ids[...]
    expert = lax.broadcasted_iota(jnp.int32, gates.shape, 0)
    row = lax.broadcasted_iota(jnp.int32, names.shape, 0)
    out = jnp.zeros(names.shape, F32)
    for k in range(names.shape[0]):
        picked = jnp.sum(jnp.where(names[k : k + 1, :] == expert, gates, 0.0), 0, keepdims=True)
        out = jnp.where(row == k, picked, out)
    grad_gates[...] = out.astype(BF16)


def call(kernel, outs, place, *args, after=(), small=True, arrives=0, leaves=0, flops=0, limit=2):
    used = len(args)
    limit = (limit if small else 56) * 2**20
    if small:
        args = [
            pltpu.with_memory_space_constraint(x, pltpu.VMEM) if i < used - arrives else x
            for i, x in enumerate(args)
        ]
    out_shape = [
        pltpu.VMEM(s, d) if small and i >= leaves else jax.ShapeDtypeStruct(s, d)
        for i, (s, d) in enumerate(outs)
    ]

    scalars = () if place is None else (place,)
    read = len(scalars) + used

    def run(*refs):
        kernel(*refs[:read], *refs[read + len(after) :])

    vmem = pl.BlockSpec(memory_space=pltpu.VMEM)
    return pl.pallas_call(
        run,
        out_shape=out_shape,
        in_specs=[pl.BlockSpec(memory_space=pltpu.SMEM)] * len(scalars)
        + [vmem] * used
        + [pl.BlockSpec(memory_space=pl.ANY)] * len(after),
        out_specs=[vmem] * len(outs),
        compiler_params=pltpu.CompilerParams(vmem_limit_bytes=limit),
        cost_estimate=pl.CostEstimate(flops=flops, bytes_accessed=0, transcendentals=0),
        name=kernel.__name__.replace("<lambda>", "weight_kernel"),
    )(*scalars, *args, *after)


def chip_bits(chip_count):
    bits = []
    bit = chip_count // 2
    while bit:
        bits.append(bit)
        bit //= 2
    return (bits[:-2] + bits[-2:][::-1], bits)


def body(tokens, cotangent, expert_ids, gate_probs, gate_half, up_half, down_half):
    chip_count = lax.axis_size("expert") * lax.axis_size("chip")
    tok_rows, features = tokens.shape
    half = features // 2
    width = gate_half.shape[2]
    lanes = -(-chip_count // 128) * 128
    member = lax.axis_index("core")
    own_expert = lax.axis_index("expert") * lax.axis_size("chip") + lax.axis_index("chip")
    place = jnp.stack([member, own_expert]).astype(jnp.int32)
    bits = chip_bits(chip_count)
    far = len(bits[0]) - 4
    small = far == 0

    def exchange(x, offsets):
        pairs = [
            (2 * chip + core, 2 * (chip ^ offsets[core]) + core)
            for chip in range(chip_count)
            for core in range(2)
        ]
        return lax.ppermute(x, DEVICES, pairs)

    steps = list(zip(*bits))
    near_a, near_b = steps[-2:]
    up_two, up_one = steps[far][0], steps[far + 1][0]

    before = []

    def run(kernel, outs, place, *args, **kwargs):
        results = call(kernel, outs, place, *args, after=tuple(before), small=small, **kwargs)
        before[:] = results[-1:]
        return results

    hbm = pl.BlockSpec(memory_space=pltpu.HBM)
    arguments = (tokens, cotangent, expert_ids.T, gate_probs.T)
    block = pl.pallas_call(
        prepare_kernel,
        out_shape=pltpu.VMEM((tok_rows, 2 * features + lanes), BF16),
        in_specs=[hbm] * 4,
        out_specs=pl.BlockSpec(memory_space=pltpu.VMEM),
        scratch_shapes=[
            pltpu.VMEM(expert_ids.shape[::-1], jnp.int32),
            pltpu.VMEM(gate_probs.shape[::-1], BF16),
            pltpu.SemaphoreType.DMA((4,)),
        ],
        name="prepare_kernel",
    )(*(pltpu.with_memory_space_constraint(x, pltpu.HBM) for x in arguments))

    for step in steps[:far]:
        block = jnp.concatenate([block, exchange(block, step)], 0)

    offsets = (up_two, up_one, up_one ^ up_two)
    rows = block.shape[0]
    columns = features + lanes

    gate_own, up_own, down_own = gate_half[0], up_half[0], down_half[0]
    gate_other, up_other, down_other = swap_core(gate_own), swap_core(up_own), swap_core(down_own)
    weights = [gate_own, gate_other, up_own, up_other, down_own, down_other]
    numbers, saved = [], []

    def at_offset(x, i):
        return exchange(x, (offsets[i], offsets[i]))

    def join(first, second, flops=0):
        shape = (2 * first.shape[0], first.shape[1])
        return run(join_kernel, [(shape, BF16)], None, first, second, flops=flops)[0]

    def after_all(x, *others):
        before.extend(others)
        return run(pass_kernel, [(x.shape, BF16)], None, x)[0]

    def expert(*blocks):
        number, count = len(blocks), blocks[0].shape[0]
        row_grads, grads, hidden = run(
            expert_kernel,
            [
                ((number * count, columns), BF16),
                ((number, count, 2 * width), BF16),
                ((number, count, width), BF16),
            ],
            place, *blocks, *weights, limit=6, flops=6 * 10**9,
        )
        numbers.append(number)
        saved.extend([*blocks, grads, hidden])
        return row_grads

    def split(kept, got, types, flops=0):
        shape = (kept.shape[0] // 2, columns)
        return run(split_kernel, [(shape, t) for t in types], None, kept, got, flops=flops)

    def collect(total, part, flops=0):
        return run(add_kernel, [(total.shape, F32)], None, total, part, flops=flops)[0]

    far_two = at_offset(block, 0)
    first_own = join(block, exchange(block, near_a))
    second_own = exchange(first_own, near_b)
    near_1 = at_offset(join(block, far_two, flops=4 * 10**9), 1)
    second_own = after_all(second_own)
    first_two = join(far_two, exchange(far_two, near_a))
    second_two = exchange(first_two, near_b)
    near_1 = after_all(near_1)
    got_near = exchange(near_1, near_a)
    weights[-1] = after_all(weights[-1])
    kept_0 = expert(first_own, first_two)
    first_1 = join(near_1, got_near)
    second_1 = exchange(first_1, near_b)
    give_0 = expert(second_own, second_two)
    kept_1 = expert(first_1)
    got_0 = exchange(after_all(give_0, second_1), near_b)
    got_1 = exchange(expert(second_1), near_b)
    kept_0, give = split(kept_0, got_0, (F32, BF16))
    got_0 = exchange(give, near_a)
    keep_in, keep_down, *gives = run(
        lambda *refs: weight_kernel(tuple(numbers), *refs),
        [
            ((half, 2 * width), F32),
            ((width, half), F32),
            ((half, width), BF16),
            ((half, width), BF16),
            ((width, half), BF16),
        ],
        place, *saved, limit=10, flops=6 * 10**9,
    )
    total, give = split(kept_0, got_0, (F32, BF16))
    back_two = at_offset(give, 0)
    kept_1, give = split(kept_1, got_1, (F32, BF16))
    got_1 = exchange(give, near_a)
    gots = [swap_core(give) for give in gives]
    total = collect(total, back_two, flops=6 * 10**9)
    give_one, give_both = split(kept_1, got_1, (BF16, BF16), flops=6 * 10**9)
    back_one, back_both = at_offset(give_one, 1), at_offset(give_both, 2)
    grad_gate, grad_up, grad_down, _ = run(
        settle_kernel,
        [((half, width), BF16), ((half, width), BF16), ((width, half), BF16), ((8, 128), F32)],
        None, keep_in, keep_down, *gots, leaves=3, limit=6,
    )
    total = collect(total, back_one)

    parts = (total, back_both)
    if far:
        total = total + back_both.astype(F32)
        for step in reversed(steps[:far]):
            middle = total.shape[0] // 2
            total = total[:middle] + exchange(total[middle:].astype(BF16), step).astype(F32)
        parts = (total,)
    grad_tokens, grad_gates = run(
        finish_kernel,
        [((tok_rows, features), BF16), (expert_ids.shape[::-1], BF16)],
        place, *parts, expert_ids.T, arrives=1, leaves=2,
    )
    return grad_tokens, grad_gates.T, grad_gate[None], grad_up[None], grad_down[None]


def solution(mesh):
    shape = mesh.shape
    devices = mesh.devices.reshape(shape["dom"], shape["expert"], shape["dp"] // 2, 2)
    fine = Mesh(devices, ("dom", "expert", "chip", "core"))
    every = ("dom", "expert", "chip", "core")
    flat, cube = P(every, None), P(every, None, None)
    return jax.shard_map(
        body,
        mesh=fine,
        in_specs=(flat, flat, flat, flat, cube, cube, cube),
        out_specs=(flat, flat, cube, cube, cube),
        check_vma=False,
    )
```

```python
import jax
import jax.numpy as jnp
from jax import lax
from jax.experimental import pallas as pl
from jax.experimental.pallas import tpu as pltpu
from jax.sharding import Mesh, PartitionSpec as P

DEVICES = ("expert", "chip", "core")
F32, BF16 = jnp.float32, jnp.bfloat16
NN = (((1,), (0,)), ((), ()))
NT = (((1,), (1,)), ((), ()))
TN = (((0,), (0,)), ((), ()))
CHUNK = 128


def dot(a, b, dims):
    return lax.dot_general(a, b, dims, preferred_element_type=F32)


def swap_core(x):
    return lax.ppermute(x, "core", [(0, 1), (1, 0)])


def for_chunks(rows, step, chunk):
    if rows <= chunk:
        step(pl.ds(0, rows))
    else:

        @pl.loop(0, rows // chunk)
        def _(i):
            step(pl.ds(pl.multiple_of(i * chunk, chunk), chunk))


def own_other(place_ref, half, start=0):
    member = place_ref[0]
    own = pl.ds(pl.multiple_of(start + member * half, half), half)
    other = pl.ds(pl.multiple_of(start + (1 - member) * half, half), half)
    return own, other


def prepare_kernel(tokens, cotangent, ids, probs, out, ids_here, probs_here, sems):
    features = tokens.shape[1]
    lanes = out.shape[1] - 2 * features
    copies = [
        pltpu.make_async_copy(source, target, sems.at[i])
        for i, (source, target) in enumerate(
            (
                (ids, ids_here),
                (probs, probs_here),
                (tokens, out.at[:, pl.ds(0, features)]),
                (cotangent, out.at[:, pl.ds(features, features)]),
            )
        )
    ]
    for copy in copies:
        copy.start()
    copies[0].wait()
    copies[1].wait()
    names, given = ids_here[...], probs_here[...].astype(F32)
    expert = lax.broadcasted_iota(jnp.int32, (lanes, names.shape[1]), 0)
    weight = jnp.zeros(expert.shape, F32)
    for k in range(names.shape[0]):
        weight = jnp.where(names[k : k + 1, :] == expert, given[k : k + 1, :], weight)
    turned = dot(weight.astype(BF16), unit_matrix(lanes), TN)
    out[:, pl.ds(2 * features, lanes)] = turned.astype(BF16)
    copies[2].wait()
    copies[3].wait()


def unit_matrix(size):
    row = lax.broadcasted_iota(jnp.int32, (size, size), 0)
    column = lax.broadcasted_iota(jnp.int32, (size, size), 1)
    return jnp.where(row == column, 1.0, 0.0).astype(BF16)


def join_kernel(first, second, out):
    rows = first.shape[0]
    out[pl.ds(0, rows), :] = first[...]
    out[pl.ds(rows, rows), :] = second[...]


def split_kernel(kept, got, keep, give):
    rows = keep.shape[0]
    upper, lower = pl.ds(0, rows), pl.ds(rows, rows)
    give[...] = (kept[lower, :].astype(F32) + got[lower, :].astype(F32)).astype(give.dtype)
    keep[...] = (kept[upper, :].astype(F32) + got[upper, :].astype(F32)).astype(keep.dtype)


def add_kernel(kept, got, total):
    total[...] = (kept[...] + got[...].astype(F32)).astype(total.dtype)


def pass_kernel(source, out):
    out[...] = source[...]


def expert_kernel(place, *refs):
    blocks, refs = refs[:-9], refs[-9:]
    gate_own, gate_other, up_own, up_other, down_own, down_other = refs[:6]
    row_grads, grads, scaled_hidden = refs[6:]
    half, width = gate_own.shape
    features = 2 * half
    number, count = len(blocks), blocks[0].shape[0]
    lanes = blocks[0].shape[1] - 2 * features
    own, other = own_other(place, half)
    dys_own, dys_other = own_other(place, half, features)

    def step(at):
        def take(cols):
            return jnp.concatenate([block[at, cols] for block in blocks], 0)

        mine, rest = take(own), take(other)
        pre_gate = dot(mine, gate_own[...], NN) + dot(rest, gate_other[...], NN)
        pre_up = dot(mine, up_own[...], NN) + dot(rest, up_other[...], NN)
        back = dot(take(dys_own), down_own[...], NT) + dot(take(dys_other), down_other[...], NT)
        sig = jax.nn.sigmoid(pre_gate)
        active = pre_gate * sig
        slope = sig * (1.0 + pre_gate * (1.0 - sig))
        hidden = active * pre_up
        lane = lax.broadcasted_iota(jnp.int32, (back.shape[0], lanes), 1)
        is_own = lane == place[1]
        gates = jnp.where(is_own, take(pl.ds(2 * features, lanes)).astype(F32), 0.0)
        gates = jnp.sum(gates, 1, keepdims=True)
        gate_grads = jnp.sum(hidden * back, 1, keepdims=True)
        back = back * gates
        grad_gate = (back * pre_up * slope).astype(BF16)
        grad_up = (back * active).astype(BF16)
        scaled = (hidden * gates).astype(BF16)
        middle = count // 2

        def put(rows, cols):
            for i in range(number):
                part = rows[i * at.size : (i + 1) * at.size]
                if at.size == count:
                    row_grads[pl.ds(i * middle, middle), cols] = part[:middle]
                    row_grads[pl.ds((number + i) * middle, middle), cols] = part[middle:]
                else:
                    start = at.start + at.start // middle * (number - 1) * middle + i * middle
                    row_grads[pl.ds(pl.multiple_of(start, at.size), at.size), cols] = part

        to_own = dot(grad_gate, gate_own[...], NT) + dot(grad_up, up_own[...], NT)
        put(to_own.astype(BF16), pl.ds(0, half))
        to_other = dot(grad_gate, gate_other[...], NT) + dot(grad_up, up_other[...], NT)
        put(to_other.astype(BF16), pl.ds(half, half))
        put(jnp.where(is_own, gate_grads, 0.0).astype(BF16), pl.ds(features, lanes))
        for i in range(number):
            part = slice(i * at.size, (i + 1) * at.size)
            grads[i, at, pl.ds(0, width)] = grad_gate[part]
            grads[i, at, pl.ds(width, width)] = grad_up[part]
            scaled_hidden[i, at, :] = scaled[part]

    for_chunks(count, step, CHUNK // number)


def weight_kernel(numbers, place, *refs):
    keep_in, keep_down, give_gate, give_up, give_down = refs[-5:]
    parts, begin = [], 0
    for number in numbers:
        grads, hidden = refs[begin + number : begin + number + 2]
        parts += [(refs[begin + i], grads.at[i], hidden.at[i]) for i in range(number)]
        begin += number + 2
    half, width = give_gate.shape
    own, other = own_other(place, half)
    dys_own, dys_other = own_other(place, half, 2 * half)
    steps = max(1, min(p[0].shape[0] for p in parts) // CHUNK)

    def products(i, cols, dys_cols):
        def gather(which, cols):
            values = []
            for part in parts:
                size = part[0].shape[0] // steps
                start = i * size
                at = pl.ds(start if steps == 1 else pl.multiple_of(start, size), size)
                values.append(part[which][at, cols])
            return jnp.concatenate(values, 0)

        into = dot(gather(0, cols), gather(1, pl.ds(0, 2 * width)), TN)
        return into, dot(gather(2, pl.ds(0, width)), gather(0, dys_cols), TN)

    def hand_over(into, down):
        give_gate[...] = into[:, :width].astype(BF16)
        give_up[...] = into[:, width:].astype(BF16)
        give_down[...] = down.astype(BF16)

    if steps == 1:
        hand_over(*products(0, other, dys_other))
        keep_in[...], keep_down[...] = products(0, own, dys_own)
    else:
        for cols, dys_cols, is_given in ((other, dys_other, True), (own, dys_own, False)):
            keep_in[...] = jnp.zeros_like(keep_in)
            keep_down[...] = jnp.zeros_like(keep_down)

            @pl.loop(0, steps)
            def _(i):
                into, down = products(i, cols, dys_cols)
                keep_in[...] += into
                keep_down[...] += down

            if is_given:
                hand_over(keep_in[...], keep_down[...])


def settle_kernel(keep_in, keep_down, got_gate, got_up, got_down, gate, up, down, done):
    width = gate.shape[1]
    left, right = pl.ds(0, width), pl.ds(width, width)
    gate[...] = (keep_in[:, left] + got_gate[...].astype(F32)).astype(BF16)
    up[...] = (keep_in[:, right] + got_up[...].astype(F32)).astype(BF16)
    down[...] = (keep_down[...] + got_down[...].astype(F32)).astype(BF16)
    done[...] = jnp.zeros_like(done)


def finish_kernel(place, *refs):
    ids, grad_tokens, grad_gates = refs[-3:]
    total = refs[0][...].astype(F32)
    for part in refs[1:-3]:
        total = total + part[...].astype(F32)
    half = grad_tokens.shape[1] // 2
    lanes = total.shape[1] - 2 * half
    own, other = own_other(place, half)
    grad_tokens[:, own] = total[:, :half].astype(BF16)
    grad_tokens[:, other] = total[:, half : 2 * half].astype(BF16)
    gates = dot(unit_matrix(lanes), total[:, 2 * half :].astype(BF16), NT)
    names = ids[...]
    expert = lax.broadcasted_iota(jnp.int32, gates.shape, 0)
    row = lax.broadcasted_iota(jnp.int32, names.shape, 0)
    out = jnp.zeros(names.shape, F32)
    for k in range(names.shape[0]):
        picked = jnp.sum(jnp.where(names[k : k + 1, :] == expert, gates, 0.0), 0, keepdims=True)
        out = jnp.where(row == k, picked, out)
    grad_gates[...] = out.astype(BF16)


def call(kernel, outs, place, *args, after=(), small=True, arrives=0, leaves=0, flops=0, limit=2):
    used = len(args)
    limit = (limit if small else 56) * 2**20
    if small:
        args = [
            pltpu.with_memory_space_constraint(x, pltpu.VMEM) if i < used - arrives else x
            for i, x in enumerate(args)
        ]
    out_shape = [
        pltpu.VMEM(s, d) if small and i >= leaves else jax.ShapeDtypeStruct(s, d)
        for i, (s, d) in enumerate(outs)
    ]

    scalars = () if place is None else (place,)
    read = len(scalars) + used

    def run(*refs):
        kernel(*refs[:read], *refs[read + len(after) :])

    vmem = pl.BlockSpec(memory_space=pltpu.VMEM)
    return pl.pallas_call(
        run,
        out_shape=out_shape,
        in_specs=[pl.BlockSpec(memory_space=pltpu.SMEM)] * len(scalars)
        + [vmem] * used
        + [pl.BlockSpec(memory_space=pl.ANY)] * len(after),
        out_specs=[vmem] * len(outs),
        compiler_params=pltpu.CompilerParams(vmem_limit_bytes=limit),
        cost_estimate=pl.CostEstimate(flops=flops, bytes_accessed=0, transcendentals=0),
        name=kernel.__name__.replace("<lambda>", "weight_kernel"),
    )(*scalars, *args, *after)


def chip_bits(chip_count):
    bits = []
    bit = chip_count // 2
    while bit:
        bits.append(bit)
        bit //= 2
    return (bits[:-2] + bits[-2:][::-1], bits)


def body(tokens, cotangent, expert_ids, gate_probs, gate_half, up_half, down_half):
    chip_count = lax.axis_size("expert") * lax.axis_size("chip")
    tok_rows, features = tokens.shape
    half = features // 2
    width = gate_half.shape[2]
    lanes = -(-chip_count // 128) * 128
    member = lax.axis_index("core")
    own_expert = lax.axis_index("expert") * lax.axis_size("chip") + lax.axis_index("chip")
    place = jnp.stack([member, own_expert]).astype(jnp.int32)
    bits = chip_bits(chip_count)
    far = len(bits[0]) - 4
    small = far == 0

    def exchange(x, offsets):
        pairs = [
            (2 * chip + core, 2 * (chip ^ offsets[core]) + core)
            for chip in range(chip_count)
            for core in range(2)
        ]
        return lax.ppermute(x, DEVICES, pairs)

    steps = list(zip(*bits))
    near_a, near_b = steps[-2:]
    up_two, up_one = steps[far][0], steps[far + 1][0]

    before = []

    def run(kernel, outs, place, *args, **kwargs):
        results = call(kernel, outs, place, *args, after=tuple(before), small=small, **kwargs)
        before[:] = results[-1:]
        return results

    hbm = pl.BlockSpec(memory_space=pltpu.HBM)
    arguments = (tokens, cotangent, expert_ids.T, gate_probs.T)
    block = pl.pallas_call(
        prepare_kernel,
        out_shape=pltpu.VMEM((tok_rows, 2 * features + lanes), BF16),
        in_specs=[hbm] * 4,
        out_specs=pl.BlockSpec(memory_space=pltpu.VMEM),
        scratch_shapes=[
            pltpu.VMEM(expert_ids.shape[::-1], jnp.int32),
            pltpu.VMEM(gate_probs.shape[::-1], BF16),
            pltpu.SemaphoreType.DMA((4,)),
        ],
        name="prepare_kernel",
    )(*(pltpu.with_memory_space_constraint(x, pltpu.HBM) for x in arguments))

    for step in steps[:far]:
        block = jnp.concatenate([block, exchange(block, step)], 0)

    offsets = (up_two, up_one, up_one ^ up_two)
    rows = block.shape[0]
    columns = features + lanes

    gate_own, up_own, down_own = gate_half[0], up_half[0], down_half[0]
    gate_other, up_other, down_other = swap_core(gate_own), swap_core(up_own), swap_core(down_own)
    weights = [gate_own, gate_other, up_own, up_other, down_own, down_other]
    numbers, saved = [], []

    def at_offset(x, i):
        return exchange(x, (offsets[i], offsets[i]))

    def join(first, second, flops=0):
        shape = (2 * first.shape[0], first.shape[1])
        return run(join_kernel, [(shape, BF16)], None, first, second, flops=flops)[0]

    def after_all(x, *others):
        before.extend(others)
        return run(pass_kernel, [(x.shape, BF16)], None, x)[0]

    def expert(*blocks):
        number, count = len(blocks), blocks[0].shape[0]
        row_grads, grads, hidden = run(
            expert_kernel,
            [
                ((number * count, columns), BF16),
                ((number, count, 2 * width), BF16),
                ((number, count, width), BF16),
            ],
            place, *blocks, *weights, limit=6, flops=6 * 10**9,
        )
        numbers.append(number)
        saved.extend([*blocks, grads, hidden])
        return row_grads

    def split(kept, got, types, flops=0):
        shape = (kept.shape[0] // 2, columns)
        return run(split_kernel, [(shape, t) for t in types], None, kept, got, flops=flops)

    def collect(total, part):
        return run(add_kernel, [(total.shape, F32)], None, total, part)[0]

    far_two = at_offset(block, 0)
    first_own = join(block, exchange(block, near_a))
    second_own = exchange(first_own, near_b)
    near_1 = at_offset(join(block, far_two, flops=4 * 10**9), 1)
    second_own = after_all(second_own)
    first_two = join(far_two, exchange(far_two, near_a))
    second_two = exchange(first_two, near_b)
    near_1 = after_all(near_1)
    got_near = exchange(near_1, near_a)
    weights[-1] = after_all(weights[-1])
    kept_0 = expert(first_own, first_two)
    first_1 = join(near_1, got_near)
    second_1 = exchange(first_1, near_b)
    give_0 = expert(second_own, second_two)
    kept_1 = expert(first_1)
    got_1 = exchange(expert(second_1), near_b)
    got_0 = exchange(after_all(give_0), near_b)
    keep_in, keep_down, *gives = run(
        lambda *refs: weight_kernel(tuple(numbers), *refs),
        [
            ((half, 2 * width), F32),
            ((width, half), F32),
            ((half, width), BF16),
            ((half, width), BF16),
            ((width, half), BF16),
        ],
        place, *saved, limit=10, flops=6 * 10**9,
    )
    kept_1, give = split(kept_1, got_1, (F32, BF16))
    got_1 = exchange(give, near_a)
    kept_0, give = split(kept_0, got_0, (F32, BF16))
    got_0 = exchange(give, near_a)
    gots = [swap_core(give) for give in gives]
    give_one, give_both = split(kept_1, got_1, (BF16, BF16), flops=6 * 10**9)
    back_one, back_both = at_offset(give_one, 1), at_offset(give_both, 2)
    grad_gate, grad_up, grad_down, _ = run(
        settle_kernel,
        [((half, width), BF16), ((half, width), BF16), ((width, half), BF16), ((8, 128), F32)],
        None, keep_in, keep_down, *gots, leaves=3, limit=6,
    )
    total, give = split(kept_0, got_0, (F32, BF16))
    back_two = at_offset(give, 0)
    total = collect(total, back_one)
    total = collect(total, back_both)

    parts = (total, back_two)
    if far:
        total = total + back_two.astype(F32)
        for step in reversed(steps[:far]):
            middle = total.shape[0] // 2
            total = total[:middle] + exchange(total[middle:].astype(BF16), step).astype(F32)
        parts = (total,)
    grad_tokens, grad_gates = run(
        finish_kernel,
        [((tok_rows, features), BF16), (expert_ids.shape[::-1], BF16)],
        place, *parts, expert_ids.T, arrives=1, leaves=2,
    )
    return grad_tokens, grad_gates.T, grad_gate[None], grad_up[None], grad_down[None]


def solution(mesh):
    shape = mesh.shape
    devices = mesh.devices.reshape(shape["dom"], shape["expert"], shape["dp"] // 2, 2)
    fine = Mesh(devices, ("dom", "expert", "chip", "core"))
    every = ("dom", "expert", "chip", "core")
    flat, cube = P(every, None), P(every, None, None)
    return jax.shard_map(
        body,
        mesh=fine,
        in_specs=(flat, flat, flat, flat, cube, cube, cube),
        out_specs=(flat, flat, cube, cube, cube),
        check_vma=False,
    )
```

```python
import jax
import jax.numpy as jnp
from jax import lax
from jax.experimental import pallas as pl
from jax.experimental.pallas import tpu as pltpu
from jax.sharding import Mesh, PartitionSpec as P

DEVICES = ("expert", "chip", "core")
F32, BF16 = jnp.float32, jnp.bfloat16
NN = (((1,), (0,)), ((), ()))
NT = (((1,), (1,)), ((), ()))
TN = (((0,), (0,)), ((), ()))
CHUNK = 128


def dot(a, b, dims):
    return lax.dot_general(a, b, dims, preferred_element_type=F32)


def swap_core(x):
    return lax.ppermute(x, "core", [(0, 1), (1, 0)])


def for_chunks(rows, step, chunk):
    if rows <= chunk:
        step(pl.ds(0, rows))
    else:

        @pl.loop(0, rows // chunk)
        def _(i):
            step(pl.ds(pl.multiple_of(i * chunk, chunk), chunk))


def own_other(place_ref, half, start=0):
    member = place_ref[0]
    own = pl.ds(pl.multiple_of(start + member * half, half), half)
    other = pl.ds(pl.multiple_of(start + (1 - member) * half, half), half)
    return own, other


def prepare_kernel(tokens, cotangent, ids, probs, out, ids_here, probs_here, sems):
    features = tokens.shape[1]
    lanes = out.shape[1] - 2 * features
    copies = [
        pltpu.make_async_copy(source, target, sems.at[i])
        for i, (source, target) in enumerate(
            (
                (ids, ids_here),
                (probs, probs_here),
                (tokens, out.at[:, pl.ds(0, features)]),
                (cotangent, out.at[:, pl.ds(features, features)]),
            )
        )
    ]
    for copy in copies:
        copy.start()
    copies[0].wait()
    copies[1].wait()
    names, given = ids_here[...], probs_here[...].astype(F32)
    expert = lax.broadcasted_iota(jnp.int32, (lanes, names.shape[1]), 0)
    weight = jnp.zeros(expert.shape, F32)
    for k in range(names.shape[0]):
        weight = jnp.where(names[k : k + 1, :] == expert, given[k : k + 1, :], weight)
    turned = dot(weight.astype(BF16), unit_matrix(lanes), TN)
    out[:, pl.ds(2 * features, lanes)] = turned.astype(BF16)
    copies[2].wait()
    copies[3].wait()


def unit_matrix(size):
    row = lax.broadcasted_iota(jnp.int32, (size, size), 0)
    column = lax.broadcasted_iota(jnp.int32, (size, size), 1)
    return jnp.where(row == column, 1.0, 0.0).astype(BF16)


def join_kernel(first, second, out):
    rows = first.shape[0]
    out[pl.ds(0, rows), :] = first[...]
    out[pl.ds(rows, rows), :] = second[...]


def split_kernel(kept, got, keep, give):
    rows = keep.shape[0]
    upper, lower = pl.ds(0, rows), pl.ds(rows, rows)
    give[...] = (kept[lower, :].astype(F32) + got[lower, :].astype(F32)).astype(give.dtype)
    keep[...] = (kept[upper, :].astype(F32) + got[upper, :].astype(F32)).astype(keep.dtype)


def add_kernel(kept, got, total):
    total[...] = (kept[...] + got[...].astype(F32)).astype(total.dtype)


def pass_kernel(source, out):
    out[...] = source[...]


def expert_kernel(place, *refs):
    blocks, refs = refs[:-9], refs[-9:]
    gate_own, gate_other, up_own, up_other, down_own, down_other = refs[:6]
    row_grads, grads, scaled_hidden = refs[6:]
    half, width = gate_own.shape
    features = 2 * half
    number, count = len(blocks), blocks[0].shape[0]
    lanes = blocks[0].shape[1] - 2 * features
    own, other = own_other(place, half)
    dys_own, dys_other = own_other(place, half, features)

    def step(at):
        def take(cols):
            return jnp.concatenate([block[at, cols] for block in blocks], 0)

        mine, rest = take(own), take(other)
        pre_gate = dot(mine, gate_own[...], NN) + dot(rest, gate_other[...], NN)
        pre_up = dot(mine, up_own[...], NN) + dot(rest, up_other[...], NN)
        back = dot(take(dys_own), down_own[...], NT) + dot(take(dys_other), down_other[...], NT)
        sig = jax.nn.sigmoid(pre_gate)
        active = pre_gate * sig
        slope = sig * (1.0 + pre_gate * (1.0 - sig))
        hidden = active * pre_up
        lane = lax.broadcasted_iota(jnp.int32, (back.shape[0], lanes), 1)
        is_own = lane == place[1]
        gates = jnp.where(is_own, take(pl.ds(2 * features, lanes)).astype(F32), 0.0)
        gates = jnp.sum(gates, 1, keepdims=True)
        gate_grads = jnp.sum(hidden * back, 1, keepdims=True)
        back = back * gates
        grad_gate = (back * pre_up * slope).astype(BF16)
        grad_up = (back * active).astype(BF16)
        scaled = (hidden * gates).astype(BF16)
        middle = count // 2

        def put(rows, cols):
            for i in range(number):
                part = rows[i * at.size : (i + 1) * at.size]
                if at.size == count:
                    row_grads[pl.ds(i * middle, middle), cols] = part[:middle]
                    row_grads[pl.ds((number + i) * middle, middle), cols] = part[middle:]
                else:
                    start = at.start + at.start // middle * (number - 1) * middle + i * middle
                    row_grads[pl.ds(pl.multiple_of(start, at.size), at.size), cols] = part

        to_own = dot(grad_gate, gate_own[...], NT) + dot(grad_up, up_own[...], NT)
        put(to_own.astype(BF16), pl.ds(0, half))
        to_other = dot(grad_gate, gate_other[...], NT) + dot(grad_up, up_other[...], NT)
        put(to_other.astype(BF16), pl.ds(half, half))
        put(jnp.where(is_own, gate_grads, 0.0).astype(BF16), pl.ds(features, lanes))
        for i in range(number):
            part = slice(i * at.size, (i + 1) * at.size)
            grads[i, at, pl.ds(0, width)] = grad_gate[part]
            grads[i, at, pl.ds(width, width)] = grad_up[part]
            scaled_hidden[i, at, :] = scaled[part]

    for_chunks(count, step, CHUNK // number)


def weight_kernel(numbers, place, *refs):
    keep_in, keep_down, give_gate, give_up, give_down = refs[-5:]
    parts, begin = [], 0
    for number in numbers:
        grads, hidden = refs[begin + number : begin + number + 2]
        parts += [(refs[begin + i], grads.at[i], hidden.at[i]) for i in range(number)]
        begin += number + 2
    half, width = give_gate.shape
    own, other = own_other(place, half)
    dys_own, dys_other = own_other(place, half, 2 * half)
    steps = max(1, min(p[0].shape[0] for p in parts) // CHUNK)

    def products(i, cols, dys_cols):
        def gather(which, cols):
            values = []
            for part in parts:
                size = part[0].shape[0] // steps
                start = i * size
                at = pl.ds(start if steps == 1 else pl.multiple_of(start, size), size)
                values.append(part[which][at, cols])
            return jnp.concatenate(values, 0)

        into = dot(gather(0, cols), gather(1, pl.ds(0, 2 * width)), TN)
        return into, dot(gather(2, pl.ds(0, width)), gather(0, dys_cols), TN)

    def hand_over(into, down):
        give_gate[...] = into[:, :width].astype(BF16)
        give_up[...] = into[:, width:].astype(BF16)
        give_down[...] = down.astype(BF16)

    if steps == 1:
        hand_over(*products(0, other, dys_other))
        keep_in[...], keep_down[...] = products(0, own, dys_own)
    else:
        for cols, dys_cols, is_given in ((other, dys_other, True), (own, dys_own, False)):
            keep_in[...] = jnp.zeros_like(keep_in)
            keep_down[...] = jnp.zeros_like(keep_down)

            @pl.loop(0, steps)
            def _(i):
                into, down = products(i, cols, dys_cols)
                keep_in[...] += into
                keep_down[...] += down

            if is_given:
                hand_over(keep_in[...], keep_down[...])


def settle_kernel(keep_in, keep_down, got_gate, got_up, got_down, gate, up, down, done):
    width = gate.shape[1]
    left, right = pl.ds(0, width), pl.ds(width, width)
    gate[...] = (keep_in[:, left] + got_gate[...].astype(F32)).astype(BF16)
    up[...] = (keep_in[:, right] + got_up[...].astype(F32)).astype(BF16)
    down[...] = (keep_down[...] + got_down[...].astype(F32)).astype(BF16)
    done[...] = jnp.zeros_like(done)


def finish_kernel(place, *refs):
    ids, grad_tokens, grad_gates = refs[-3:]
    total = refs[0][...].astype(F32)
    for part in refs[1:-3]:
        total = total + part[...].astype(F32)
    half = grad_tokens.shape[1] // 2
    lanes = total.shape[1] - 2 * half
    own, other = own_other(place, half)
    grad_tokens[:, own] = total[:, :half].astype(BF16)
    grad_tokens[:, other] = total[:, half : 2 * half].astype(BF16)
    gates = dot(unit_matrix(lanes), total[:, 2 * half :].astype(BF16), NT)
    names = ids[...]
    expert = lax.broadcasted_iota(jnp.int32, gates.shape, 0)
    row = lax.broadcasted_iota(jnp.int32, names.shape, 0)
    out = jnp.zeros(names.shape, F32)
    for k in range(names.shape[0]):
        picked = jnp.sum(jnp.where(names[k : k + 1, :] == expert, gates, 0.0), 0, keepdims=True)
        out = jnp.where(row == k, picked, out)
    grad_gates[...] = out.astype(BF16)


def call(kernel, outs, place, *args, after=(), small=True, arrives=0, leaves=0, flops=0, limit=2):
    used = len(args)
    limit = (limit if small else 56) * 2**20
    if small:
        args = [
            pltpu.with_memory_space_constraint(x, pltpu.VMEM) if i < used - arrives else x
            for i, x in enumerate(args)
        ]
    out_shape = [
        pltpu.VMEM(s, d) if small and i >= leaves else jax.ShapeDtypeStruct(s, d)
        for i, (s, d) in enumerate(outs)
    ]

    scalars = () if place is None else (place,)
    read = len(scalars) + used

    def run(*refs):
        kernel(*refs[:read], *refs[read + len(after) :])

    vmem = pl.BlockSpec(memory_space=pltpu.VMEM)
    return pl.pallas_call(
        run,
        out_shape=out_shape,
        in_specs=[pl.BlockSpec(memory_space=pltpu.SMEM)] * len(scalars)
        + [vmem] * used
        + [pl.BlockSpec(memory_space=pl.ANY)] * len(after),
        out_specs=[vmem] * len(outs),
        compiler_params=pltpu.CompilerParams(vmem_limit_bytes=limit),
        cost_estimate=pl.CostEstimate(flops=flops, bytes_accessed=0, transcendentals=0),
        name=kernel.__name__.replace("<lambda>", "weight_kernel"),
    )(*scalars, *args, *after)


def chip_bits(chip_count):
    bits = []
    bit = chip_count // 2
    while bit:
        bits.append(bit)
        bit //= 2
    return (bits[:-2] + bits[-2:][::-1], bits)


def body(tokens, cotangent, expert_ids, gate_probs, gate_half, up_half, down_half):
    chip_count = lax.axis_size("expert") * lax.axis_size("chip")
    tok_rows, features = tokens.shape
    half = features // 2
    width = gate_half.shape[2]
    lanes = -(-chip_count // 128) * 128
    member = lax.axis_index("core")
    own_expert = lax.axis_index("expert") * lax.axis_size("chip") + lax.axis_index("chip")
    place = jnp.stack([member, own_expert]).astype(jnp.int32)
    bits = chip_bits(chip_count)
    far = len(bits[0]) - 4
    small = far == 0

    def exchange(x, offsets):
        pairs = [
            (2 * chip + core, 2 * (chip ^ offsets[core]) + core)
            for chip in range(chip_count)
            for core in range(2)
        ]
        return lax.ppermute(x, DEVICES, pairs)

    steps = list(zip(*bits))
    near_a, near_b = steps[-2:]
    up_two, up_one = steps[far][0], steps[far + 1][0]

    before = []

    def run(kernel, outs, place, *args, **kwargs):
        results = call(kernel, outs, place, *args, after=tuple(before), small=small, **kwargs)
        before[:] = results[-1:]
        return results

    hbm = pl.BlockSpec(memory_space=pltpu.HBM)
    arguments = (tokens, cotangent, expert_ids.T, gate_probs.T)
    block = pl.pallas_call(
        prepare_kernel,
        out_shape=pltpu.VMEM((tok_rows, 2 * features + lanes), BF16),
        in_specs=[hbm] * 4,
        out_specs=pl.BlockSpec(memory_space=pltpu.VMEM),
        scratch_shapes=[
            pltpu.VMEM(expert_ids.shape[::-1], jnp.int32),
            pltpu.VMEM(gate_probs.shape[::-1], BF16),
            pltpu.SemaphoreType.DMA((4,)),
        ],
        name="prepare_kernel",
    )(*(pltpu.with_memory_space_constraint(x, pltpu.HBM) for x in arguments))

    for step in steps[:far]:
        block = jnp.concatenate([block, exchange(block, step)], 0)

    offsets = (up_two, up_one, up_one ^ up_two)
    rows = block.shape[0]
    columns = features + lanes

    gate_own, up_own, down_own = gate_half[0], up_half[0], down_half[0]
    gate_other, up_other, down_other = swap_core(gate_own), swap_core(up_own), swap_core(down_own)
    weights = [gate_own, gate_other, up_own, up_other, down_own, down_other]
    numbers, saved = [], []

    def at_offset(x, i):
        return exchange(x, (offsets[i], offsets[i]))

    def join(first, second, flops=0):
        shape = (2 * first.shape[0], first.shape[1])
        return run(join_kernel, [(shape, BF16)], None, first, second, flops=flops)[0]

    def after_all(x, *others):
        before.extend(others)
        return run(pass_kernel, [(x.shape, BF16)], None, x)[0]

    def expert(*blocks):
        number, count = len(blocks), blocks[0].shape[0]
        row_grads, grads, hidden = run(
            expert_kernel,
            [
                ((number * count, columns), BF16),
                ((number, count, 2 * width), BF16),
                ((number, count, width), BF16),
            ],
            place, *blocks, *weights, limit=6, flops=6 * 10**9,
        )
        numbers.append(number)
        saved.extend([*blocks, grads, hidden])
        return row_grads

    def split(kept, got, types, flops=0):
        shape = (kept.shape[0] // 2, columns)
        return run(split_kernel, [(shape, t) for t in types], None, kept, got, flops=flops)

    def collect(total, part):
        return run(add_kernel, [(total.shape, F32)], None, total, part)[0]

    far_two = at_offset(block, 0)
    first_own = join(block, exchange(block, near_a))
    second_own = exchange(first_own, near_b)
    near_1 = at_offset(join(block, far_two, flops=1 * 10**9), 1)
    second_own = after_all(second_own)
    first_two = join(far_two, exchange(far_two, near_a))
    second_two = exchange(first_two, near_b)
    near_1 = after_all(near_1)
    got_near = exchange(near_1, near_a)
    weights[-1] = after_all(weights[-1])
    kept_0 = expert(first_own, first_two)
    first_1 = join(near_1, got_near)
    second_1 = exchange(first_1, near_b)
    give_0 = expert(second_own, second_two)
    kept_1 = expert(first_1)
    got_0 = exchange(after_all(give_0, second_1), near_b)
    got_1 = exchange(expert(second_1), near_b)
    kept_0, give = split(kept_0, got_0, (F32, BF16))
    got_0 = exchange(give, near_a)
    keep_in, keep_down, *gives = run(
        lambda *refs: weight_kernel(tuple(numbers), *refs),
        [
            ((half, 2 * width), F32),
            ((width, half), F32),
            ((half, width), BF16),
            ((half, width), BF16),
            ((width, half), BF16),
        ],
        place, *saved, limit=10, flops=6 * 10**9,
    )
    kept_1, give = split(kept_1, got_1, (F32, BF16))
    got_1 = exchange(give, near_a)
    total, give = split(kept_0, got_0, (F32, BF16))
    back_two = at_offset(give, 0)
    gots = [swap_core(give) for give in gives]
    give_one, give_both = split(kept_1, got_1, (BF16, BF16), flops=6 * 10**9)
    back_one, back_both = at_offset(give_one, 1), at_offset(give_both, 2)
    grad_gate, grad_up, grad_down, _ = run(
        settle_kernel,
        [((half, width), BF16), ((half, width), BF16), ((width, half), BF16), ((8, 128), F32)],
        None, keep_in, keep_down, *gots, leaves=3, limit=6,
    )
    total = collect(total, back_two)
    total = collect(total, back_one)

    parts = (total, back_both)
    if far:
        total = total + back_both.astype(F32)
        for step in reversed(steps[:far]):
            middle = total.shape[0] // 2
            total = total[:middle] + exchange(total[middle:].astype(BF16), step).astype(F32)
        parts = (total,)
    grad_tokens, grad_gates = run(
        finish_kernel,
        [((tok_rows, features), BF16), (expert_ids.shape[::-1], BF16)],
        place, *parts, expert_ids.T, arrives=1, leaves=2,
    )
    return grad_tokens, grad_gates.T, grad_gate[None], grad_up[None], grad_down[None]


def solution(mesh):
    shape = mesh.shape
    devices = mesh.devices.reshape(shape["dom"], shape["expert"], shape["dp"] // 2, 2)
    fine = Mesh(devices, ("dom", "expert", "chip", "core"))
    every = ("dom", "expert", "chip", "core")
    flat, cube = P(every, None), P(every, None, None)
    return jax.shard_map(
        body,
        mesh=fine,
        in_specs=(flat, flat, flat, flat, cube, cube, cube),
        out_specs=(flat, flat, cube, cube, cube),
        check_vma=False,
    )
```

```python
import jax
import jax.numpy as jnp
from jax import lax
from jax.experimental import pallas as pl
from jax.experimental.pallas import tpu as pltpu
from jax.sharding import Mesh, PartitionSpec as P

DEVICES = ("expert", "chip", "core")
F32, BF16 = jnp.float32, jnp.bfloat16
NN = (((1,), (0,)), ((), ()))
NT = (((1,), (1,)), ((), ()))
TN = (((0,), (0,)), ((), ()))
CHUNK = 128


def dot(a, b, dims):
    return lax.dot_general(a, b, dims, preferred_element_type=F32)


def swap_core(x):
    return lax.ppermute(x, "core", [(0, 1), (1, 0)])


def for_chunks(rows, step, chunk):
    if rows <= chunk:
        step(pl.ds(0, rows))
    else:

        @pl.loop(0, rows // chunk)
        def _(i):
            step(pl.ds(pl.multiple_of(i * chunk, chunk), chunk))


def own_other(place_ref, half, start=0):
    member = place_ref[0]
    own = pl.ds(pl.multiple_of(start + member * half, half), half)
    other = pl.ds(pl.multiple_of(start + (1 - member) * half, half), half)
    return own, other


def prepare_kernel(tokens, cotangent, ids, probs, out, ids_here, probs_here, sems):
    features = tokens.shape[1]
    lanes = out.shape[1] - 2 * features
    copies = [
        pltpu.make_async_copy(source, target, sems.at[i])
        for i, (source, target) in enumerate(
            (
                (ids, ids_here),
                (probs, probs_here),
                (tokens, out.at[:, pl.ds(0, features)]),
                (cotangent, out.at[:, pl.ds(features, features)]),
            )
        )
    ]
    for copy in copies:
        copy.start()
    copies[0].wait()
    copies[1].wait()
    names, given = ids_here[...], probs_here[...].astype(F32)
    expert = lax.broadcasted_iota(jnp.int32, (lanes, names.shape[1]), 0)
    weight = jnp.zeros(expert.shape, F32)
    for k in range(names.shape[0]):
        weight = jnp.where(names[k : k + 1, :] == expert, given[k : k + 1, :], weight)
    turned = dot(weight.astype(BF16), unit_matrix(lanes), TN)
    out[:, pl.ds(2 * features, lanes)] = turned.astype(BF16)
    copies[2].wait()
    copies[3].wait()


def unit_matrix(size):
    row = lax.broadcasted_iota(jnp.int32, (size, size), 0)
    column = lax.broadcasted_iota(jnp.int32, (size, size), 1)
    return jnp.where(row == column, 1.0, 0.0).astype(BF16)


def join_kernel(first, second, out):
    rows = first.shape[0]
    out[pl.ds(0, rows), :] = first[...]
    out[pl.ds(rows, rows), :] = second[...]


def split_kernel(kept, got, keep, give):
    rows = keep.shape[0]
    upper, lower = pl.ds(0, rows), pl.ds(rows, rows)
    give[...] = (kept[lower, :].astype(F32) + got[lower, :].astype(F32)).astype(give.dtype)
    keep[...] = (kept[upper, :].astype(F32) + got[upper, :].astype(F32)).astype(keep.dtype)


def add_kernel(kept, got, total):
    total[...] = (kept[...] + got[...].astype(F32)).astype(total.dtype)


def pass_kernel(source, out):
    out[...] = source[...]


def expert_kernel(place, *refs):
    blocks, refs = refs[:-9], refs[-9:]
    gate_own, gate_other, up_own, up_other, down_own, down_other = refs[:6]
    row_grads, grads, scaled_hidden = refs[6:]
    half, width = gate_own.shape
    features = 2 * half
    number, count = len(blocks), blocks[0].shape[0]
    lanes = blocks[0].shape[1] - 2 * features
    own, other = own_other(place, half)
    dys_own, dys_other = own_other(place, half, features)

    def step(at):
        def take(cols):
            return jnp.concatenate([block[at, cols] for block in blocks], 0)

        mine, rest = take(own), take(other)
        pre_gate = dot(mine, gate_own[...], NN) + dot(rest, gate_other[...], NN)
        pre_up = dot(mine, up_own[...], NN) + dot(rest, up_other[...], NN)
        back = dot(take(dys_own), down_own[...], NT) + dot(take(dys_other), down_other[...], NT)
        sig = jax.nn.sigmoid(pre_gate)
        active = pre_gate * sig
        slope = sig * (1.0 + pre_gate * (1.0 - sig))
        hidden = active * pre_up
        lane = lax.broadcasted_iota(jnp.int32, (back.shape[0], lanes), 1)
        is_own = lane == place[1]
        gates = jnp.where(is_own, take(pl.ds(2 * features, lanes)).astype(F32), 0.0)
        gates = jnp.sum(gates, 1, keepdims=True)
        gate_grads = jnp.sum(hidden * back, 1, keepdims=True)
        back = back * gates
        grad_gate = (back * pre_up * slope).astype(BF16)
        grad_up = (back * active).astype(BF16)
        scaled = (hidden * gates).astype(BF16)
        middle = count // 2

        def put(rows, cols):
            for i in range(number):
                part = rows[i * at.size : (i + 1) * at.size]
                if at.size == count:
                    row_grads[pl.ds(i * middle, middle), cols] = part[:middle]
                    row_grads[pl.ds((number + i) * middle, middle), cols] = part[middle:]
                else:
                    start = at.start + at.start // middle * (number - 1) * middle + i * middle
                    row_grads[pl.ds(pl.multiple_of(start, at.size), at.size), cols] = part

        to_own = dot(grad_gate, gate_own[...], NT) + dot(grad_up, up_own[...], NT)
        put(to_own.astype(BF16), pl.ds(0, half))
        to_other = dot(grad_gate, gate_other[...], NT) + dot(grad_up, up_other[...], NT)
        put(to_other.astype(BF16), pl.ds(half, half))
        put(jnp.where(is_own, gate_grads, 0.0).astype(BF16), pl.ds(features, lanes))
        for i in range(number):
            part = slice(i * at.size, (i + 1) * at.size)
            grads[i, at, pl.ds(0, width)] = grad_gate[part]
            grads[i, at, pl.ds(width, width)] = grad_up[part]
            scaled_hidden[i, at, :] = scaled[part]

    for_chunks(count, step, CHUNK // number)


def weight_kernel(numbers, place, *refs):
    keep_in, keep_down, give_gate, give_up, give_down = refs[-5:]
    parts, begin = [], 0
    for number in numbers:
        grads, hidden = refs[begin + number : begin + number + 2]
        parts += [(refs[begin + i], grads.at[i], hidden.at[i]) for i in range(number)]
        begin += number + 2
    half, width = give_gate.shape
    own, other = own_other(place, half)
    dys_own, dys_other = own_other(place, half, 2 * half)
    steps = max(1, min(p[0].shape[0] for p in parts) // CHUNK)

    def products(i, cols, dys_cols):
        def gather(which, cols):
            values = []
            for part in parts:
                size = part[0].shape[0] // steps
                start = i * size
                at = pl.ds(start if steps == 1 else pl.multiple_of(start, size), size)
                values.append(part[which][at, cols])
            return jnp.concatenate(values, 0)

        into = dot(gather(0, cols), gather(1, pl.ds(0, 2 * width)), TN)
        return into, dot(gather(2, pl.ds(0, width)), gather(0, dys_cols), TN)

    def hand_over(into, down):
        give_gate[...] = into[:, :width].astype(BF16)
        give_up[...] = into[:, width:].astype(BF16)
        give_down[...] = down.astype(BF16)

    if steps == 1:
        hand_over(*products(0, other, dys_other))
        keep_in[...], keep_down[...] = products(0, own, dys_own)
    else:
        for cols, dys_cols, is_given in ((other, dys_other, True), (own, dys_own, False)):
            keep_in[...] = jnp.zeros_like(keep_in)
            keep_down[...] = jnp.zeros_like(keep_down)

            @pl.loop(0, steps)
            def _(i):
                into, down = products(i, cols, dys_cols)
                keep_in[...] += into
                keep_down[...] += down

            if is_given:
                hand_over(keep_in[...], keep_down[...])


def settle_kernel(keep_in, keep_down, got_gate, got_up, got_down, gate, up, down, done):
    width = gate.shape[1]
    left, right = pl.ds(0, width), pl.ds(width, width)
    gate[...] = (keep_in[:, left] + got_gate[...].astype(F32)).astype(BF16)
    up[...] = (keep_in[:, right] + got_up[...].astype(F32)).astype(BF16)
    down[...] = (keep_down[...] + got_down[...].astype(F32)).astype(BF16)
    done[...] = jnp.zeros_like(done)


def finish_kernel(place, *refs):
    ids, grad_tokens, grad_gates = refs[-3:]
    total = refs[0][...].astype(F32)
    for part in refs[1:-3]:
        total = total + part[...].astype(F32)
    half = grad_tokens.shape[1] // 2
    lanes = total.shape[1] - 2 * half
    own, other = own_other(place, half)
    grad_tokens[:, own] = total[:, :half].astype(BF16)
    grad_tokens[:, other] = total[:, half : 2 * half].astype(BF16)
    gates = dot(unit_matrix(lanes), total[:, 2 * half :].astype(BF16), NT)
    names = ids[...]
    expert = lax.broadcasted_iota(jnp.int32, gates.shape, 0)
    row = lax.broadcasted_iota(jnp.int32, names.shape, 0)
    out = jnp.zeros(names.shape, F32)
    for k in range(names.shape[0]):
        picked = jnp.sum(jnp.where(names[k : k + 1, :] == expert, gates, 0.0), 0, keepdims=True)
        out = jnp.where(row == k, picked, out)
    grad_gates[...] = out.astype(BF16)


def call(kernel, outs, place, *args, after=(), small=True, arrives=0, leaves=0, flops=0, limit=2):
    used = len(args)
    limit = (limit if small else 56) * 2**20
    if small:
        args = [
            pltpu.with_memory_space_constraint(x, pltpu.VMEM) if i < used - arrives else x
            for i, x in enumerate(args)
        ]
    out_shape = [
        pltpu.VMEM(s, d) if small and i >= leaves else jax.ShapeDtypeStruct(s, d)
        for i, (s, d) in enumerate(outs)
    ]

    scalars = () if place is None else (place,)
    read = len(scalars) + used

    def run(*refs):
        kernel(*refs[:read], *refs[read + len(after) :])

    vmem = pl.BlockSpec(memory_space=pltpu.VMEM)
    return pl.pallas_call(
        run,
        out_shape=out_shape,
        in_specs=[pl.BlockSpec(memory_space=pltpu.SMEM)] * len(scalars)
        + [vmem] * used
        + [pl.BlockSpec(memory_space=pl.ANY)] * len(after),
        out_specs=[vmem] * len(outs),
        compiler_params=pltpu.CompilerParams(vmem_limit_bytes=limit),
        cost_estimate=pl.CostEstimate(flops=flops, bytes_accessed=0, transcendentals=0),
        name=kernel.__name__.replace("<lambda>", "weight_kernel"),
    )(*scalars, *args, *after)


def chip_bits(chip_count):
    bits = []
    bit = chip_count // 2
    while bit:
        bits.append(bit)
        bit //= 2
    return (bits, bits[:-2] + bits[-2:][::-1])


def body(tokens, cotangent, expert_ids, gate_probs, gate_half, up_half, down_half):
    chip_count = lax.axis_size("expert") * lax.axis_size("chip")
    tok_rows, features = tokens.shape
    half = features // 2
    width = gate_half.shape[2]
    lanes = -(-chip_count // 128) * 128
    member = lax.axis_index("core")
    own_expert = lax.axis_index("expert") * lax.axis_size("chip") + lax.axis_index("chip")
    place = jnp.stack([member, own_expert]).astype(jnp.int32)
    bits = chip_bits(chip_count)
    far = len(bits[0]) - 4
    small = far == 0

    def exchange(x, offsets):
        pairs = [
            (2 * chip + core, 2 * (chip ^ offsets[core]) + core)
            for chip in range(chip_count)
            for core in range(2)
        ]
        return lax.ppermute(x, DEVICES, pairs)

    steps = list(zip(*bits))
    near_a, near_b = steps[-2:]
    up_two, up_one = steps[far][0], steps[far + 1][0]

    before = []

    def run(kernel, outs, place, *args, **kwargs):
        results = call(kernel, outs, place, *args, after=tuple(before), small=small, **kwargs)
        before[:] = results[-1:]
        return results

    hbm = pl.BlockSpec(memory_space=pltpu.HBM)
    arguments = (tokens, cotangent, expert_ids.T, gate_probs.T)
    block = pl.pallas_call(
        prepare_kernel,
        out_shape=pltpu.VMEM((tok_rows, 2 * features + lanes), BF16),
        in_specs=[hbm] * 4,
        out_specs=pl.BlockSpec(memory_space=pltpu.VMEM),
        scratch_shapes=[
            pltpu.VMEM(expert_ids.shape[::-1], jnp.int32),
            pltpu.VMEM(gate_probs.shape[::-1], BF16),
            pltpu.SemaphoreType.DMA((4,)),
        ],
        name="prepare_kernel",
    )(*(pltpu.with_memory_space_constraint(x, pltpu.HBM) for x in arguments))

    for step in steps[:far]:
        block = jnp.concatenate([block, exchange(block, step)], 0)

    offsets = (up_two, up_one, up_one ^ up_two)
    rows = block.shape[0]
    columns = features + lanes

    gate_own, up_own, down_own = gate_half[0], up_half[0], down_half[0]
    gate_other, up_other, down_other = swap_core(gate_own), swap_core(up_own), swap_core(down_own)
    weights = [gate_own, gate_other, up_own, up_other, down_own, down_other]
    numbers, saved = [], []

    def at_offset(x, i):
        return exchange(x, (offsets[i], offsets[i]))

    def join(first, second, flops=0):
        shape = (2 * first.shape[0], first.shape[1])
        return run(join_kernel, [(shape, BF16)], None, first, second, flops=flops)[0]

    def after_all(x, *others):
        before.extend(others)
        return run(pass_kernel, [(x.shape, BF16)], None, x)[0]

    def expert(*blocks):
        number, count = len(blocks), blocks[0].shape[0]
        row_grads, grads, hidden = run(
            expert_kernel,
            [
                ((number * count, columns), BF16),
                ((number, count, 2 * width), BF16),
                ((number, count, width), BF16),
            ],
            place, *blocks, *weights, limit=6, flops=6 * 10**9,
        )
        numbers.append(number)
        saved.extend([*blocks, grads, hidden])
        return row_grads

    def split(kept, got, types, flops=0):
        shape = (kept.shape[0] // 2, columns)
        return run(split_kernel, [(shape, t) for t in types], None, kept, got, flops=flops)

    def collect(total, part):
        return run(add_kernel, [(total.shape, F32)], None, total, part)[0]

    far_two = at_offset(block, 0)
    first_own = join(block, exchange(block, near_a))
    second_own = exchange(first_own, near_b)
    near_1 = at_offset(join(block, far_two, flops=1 * 10**9), 1)
    second_own = after_all(second_own)
    first_two = join(far_two, exchange(far_two, near_a))
    second_two = exchange(first_two, near_b)
    near_1 = after_all(near_1)
    got_near = exchange(near_1, near_a)
    weights[-1] = after_all(weights[-1])
    kept_0 = expert(first_own, first_two)
    first_1 = join(near_1, got_near)
    second_1 = exchange(first_1, near_b)
    give_0 = expert(second_own, second_two)
    kept_1 = expert(first_1)
    got_0 = exchange(after_all(give_0, second_1), near_b)
    got_1 = exchange(expert(second_1), near_b)
    kept_0, give = split(kept_0, got_0, (F32, BF16))
    got_0 = exchange(give, near_a)
    keep_in, keep_down, *gives = run(
        lambda *refs: weight_kernel(tuple(numbers), *refs),
        [
            ((half, 2 * width), F32),
            ((width, half), F32),
            ((half, width), BF16),
            ((half, width), BF16),
            ((width, half), BF16),
        ],
        place, *saved, limit=10, flops=6 * 10**9,
    )
    kept_1, give = split(kept_1, got_1, (F32, BF16))
    got_1 = exchange(give, near_a)
    total, give = split(kept_0, got_0, (F32, BF16))
    back_two = at_offset(give, 0)
    gots = [swap_core(give) for give in gives]
    give_one, give_both = split(kept_1, got_1, (BF16, BF16), flops=6 * 10**9)
    back_one, back_both = at_offset(give_one, 1), at_offset(give_both, 2)
    grad_gate, grad_up, grad_down, _ = run(
        settle_kernel,
        [((half, width), BF16), ((half, width), BF16), ((width, half), BF16), ((8, 128), F32)],
        None, keep_in, keep_down, *gots, leaves=3, limit=6,
    )
    total = collect(total, back_two)
    total = collect(total, back_one)

    parts = (total, back_both)
    if far:
        total = total + back_both.astype(F32)
        for step in reversed(steps[:far]):
            middle = total.shape[0] // 2
            total = total[:middle] + exchange(total[middle:].astype(BF16), step).astype(F32)
        parts = (total,)
    grad_tokens, grad_gates = run(
        finish_kernel,
        [((tok_rows, features), BF16), (expert_ids.shape[::-1], BF16)],
        place, *parts, expert_ids.T, arrives=1, leaves=2,
    )
    return grad_tokens, grad_gates.T, grad_gate[None], grad_up[None], grad_down[None]


def solution(mesh):
    shape = mesh.shape
    devices = mesh.devices.reshape(shape["dom"], shape["expert"], shape["dp"] // 2, 2)
    fine = Mesh(devices, ("dom", "expert", "chip", "core"))
    every = ("dom", "expert", "chip", "core")
    flat, cube = P(every, None), P(every, None, None)
    return jax.shard_map(
        body,
        mesh=fine,
        in_specs=(flat, flat, flat, flat, cube, cube, cube),
        out_specs=(flat, flat, cube, cube, cube),
        check_vma=False,
    )
```

```python
import jax
import jax.numpy as jnp
from jax import lax
from jax.experimental import pallas as pl
from jax.experimental.pallas import tpu as pltpu
from jax.sharding import Mesh, PartitionSpec as P

DEVICES = ("expert", "chip", "core")
F32, BF16 = jnp.float32, jnp.bfloat16
NN = (((1,), (0,)), ((), ()))
NT = (((1,), (1,)), ((), ()))
TN = (((0,), (0,)), ((), ()))
CHUNK = 128


def dot(a, b, dims):
    return lax.dot_general(a, b, dims, preferred_element_type=F32)


def swap_core(x):
    return lax.ppermute(x, "core", [(0, 1), (1, 0)])


def for_chunks(rows, step, chunk):
    if rows <= chunk:
        step(pl.ds(0, rows))
    else:

        @pl.loop(0, rows // chunk)
        def _(i):
            step(pl.ds(pl.multiple_of(i * chunk, chunk), chunk))


def own_other(place_ref, half, start=0):
    member = place_ref[0]
    own = pl.ds(pl.multiple_of(start + member * half, half), half)
    other = pl.ds(pl.multiple_of(start + (1 - member) * half, half), half)
    return own, other


def prepare_kernel(tokens, cotangent, ids, probs, out, ids_here, probs_here, sems):
    features = tokens.shape[1]
    lanes = out.shape[1] - 2 * features
    copies = [
        pltpu.make_async_copy(source, target, sems.at[i])
        for i, (source, target) in enumerate(
            (
                (ids, ids_here),
                (probs, probs_here),
                (tokens, out.at[:, pl.ds(0, features)]),
                (cotangent, out.at[:, pl.ds(features, features)]),
            )
        )
    ]
    for copy in copies:
        copy.start()
    copies[0].wait()
    copies[1].wait()
    names, given = ids_here[...], probs_here[...].astype(F32)
    expert = lax.broadcasted_iota(jnp.int32, (lanes, names.shape[1]), 0)
    weight = jnp.zeros(expert.shape, F32)
    for k in range(names.shape[0]):
        weight = jnp.where(names[k : k + 1, :] == expert, given[k : k + 1, :], weight)
    turned = dot(weight.astype(BF16), unit_matrix(lanes), TN)
    out[:, pl.ds(2 * features, lanes)] = turned.astype(BF16)
    copies[2].wait()
    copies[3].wait()


def unit_matrix(size):
    row = lax.broadcasted_iota(jnp.int32, (size, size), 0)
    column = lax.broadcasted_iota(jnp.int32, (size, size), 1)
    return jnp.where(row == column, 1.0, 0.0).astype(BF16)


def join_kernel(first, second, out):
    rows = first.shape[0]
    out[pl.ds(0, rows), :] = first[...]
    out[pl.ds(rows, rows), :] = second[...]


def split_kernel(kept, got, keep, give):
    rows = keep.shape[0]
    upper, lower = pl.ds(0, rows), pl.ds(rows, rows)
    give[...] = (kept[lower, :].astype(F32) + got[lower, :].astype(F32)).astype(give.dtype)
    keep[...] = (kept[upper, :].astype(F32) + got[upper, :].astype(F32)).astype(keep.dtype)


def add_kernel(kept, got, total):
    total[...] = (kept[...] + got[...].astype(F32)).astype(total.dtype)


def pass_kernel(source, out):
    out[...] = source[...]


def expert_kernel(place, *refs):
    blocks, refs = refs[:-9], refs[-9:]
    gate_own, gate_other, up_own, up_other, down_own, down_other = refs[:6]
    row_grads, grads, scaled_hidden = refs[6:]
    half, width = gate_own.shape
    features = 2 * half
    number, count = len(blocks), blocks[0].shape[0]
    lanes = blocks[0].shape[1] - 2 * features
    own, other = own_other(place, half)
    dys_own, dys_other = own_other(place, half, features)

    def step(at):
        def take(cols):
            return jnp.concatenate([block[at, cols] for block in blocks], 0)

        mine, rest = take(own), take(other)
        pre_gate = dot(mine, gate_own[...], NN) + dot(rest, gate_other[...], NN)
        pre_up = dot(mine, up_own[...], NN) + dot(rest, up_other[...], NN)
        back = dot(take(dys_own), down_own[...], NT) + dot(take(dys_other), down_other[...], NT)
        sig = jax.nn.sigmoid(pre_gate)
        active = pre_gate * sig
        slope = sig * (1.0 + pre_gate * (1.0 - sig))
        hidden = active * pre_up
        lane = lax.broadcasted_iota(jnp.int32, (back.shape[0], lanes), 1)
        is_own = lane == place[1]
        gates = jnp.where(is_own, take(pl.ds(2 * features, lanes)).astype(F32), 0.0)
        gates = jnp.sum(gates, 1, keepdims=True)
        gate_grads = jnp.sum(hidden * back, 1, keepdims=True)
        back = back * gates
        grad_gate = (back * pre_up * slope).astype(BF16)
        grad_up = (back * active).astype(BF16)
        scaled = (hidden * gates).astype(BF16)
        middle = count // 2

        def put(rows, cols):
            for i in range(number):
                part = rows[i * at.size : (i + 1) * at.size]
                if at.size == count:
                    row_grads[pl.ds(i * middle, middle), cols] = part[:middle]
                    row_grads[pl.ds((number + i) * middle, middle), cols] = part[middle:]
                else:
                    start = at.start + at.start // middle * (number - 1) * middle + i * middle
                    row_grads[pl.ds(pl.multiple_of(start, at.size), at.size), cols] = part

        to_own = dot(grad_gate, gate_own[...], NT) + dot(grad_up, up_own[...], NT)
        put(to_own.astype(BF16), pl.ds(0, half))
        to_other = dot(grad_gate, gate_other[...], NT) + dot(grad_up, up_other[...], NT)
        put(to_other.astype(BF16), pl.ds(half, half))
        put(jnp.where(is_own, gate_grads, 0.0).astype(BF16), pl.ds(features, lanes))
        for i in range(number):
            part = slice(i * at.size, (i + 1) * at.size)
            grads[i, at, pl.ds(0, width)] = grad_gate[part]
            grads[i, at, pl.ds(width, width)] = grad_up[part]
            scaled_hidden[i, at, :] = scaled[part]

    for_chunks(count, step, CHUNK // number)


def weight_kernel(numbers, place, *refs):
    keep_in, keep_down, give_gate, give_up, give_down = refs[-5:]
    parts, begin = [], 0
    for number in numbers:
        grads, hidden = refs[begin + number : begin + number + 2]
        parts += [(refs[begin + i], grads.at[i], hidden.at[i]) for i in range(number)]
        begin += number + 2
    half, width = give_gate.shape
    own, other = own_other(place, half)
    dys_own, dys_other = own_other(place, half, 2 * half)
    steps = max(1, min(p[0].shape[0] for p in parts) // CHUNK)

    def products(i, cols, dys_cols):
        def gather(which, cols):
            values = []
            for part in parts:
                size = part[0].shape[0] // steps
                start = i * size
                at = pl.ds(start if steps == 1 else pl.multiple_of(start, size), size)
                values.append(part[which][at, cols])
            return jnp.concatenate(values, 0)

        into = dot(gather(0, cols), gather(1, pl.ds(0, 2 * width)), TN)
        return into, dot(gather(2, pl.ds(0, width)), gather(0, dys_cols), TN)

    def hand_over(into, down):
        give_gate[...] = into[:, :width].astype(BF16)
        give_up[...] = into[:, width:].astype(BF16)
        give_down[...] = down.astype(BF16)

    if steps == 1:
        hand_over(*products(0, other, dys_other))
        keep_in[...], keep_down[...] = products(0, own, dys_own)
    else:
        for cols, dys_cols, is_given in ((other, dys_other, True), (own, dys_own, False)):
            keep_in[...] = jnp.zeros_like(keep_in)
            keep_down[...] = jnp.zeros_like(keep_down)

            @pl.loop(0, steps)
            def _(i):
                into, down = products(i, cols, dys_cols)
                keep_in[...] += into
                keep_down[...] += down

            if is_given:
                hand_over(keep_in[...], keep_down[...])


def settle_kernel(keep_in, keep_down, got_gate, got_up, got_down, gate, up, down, done):
    width = gate.shape[1]
    left, right = pl.ds(0, width), pl.ds(width, width)
    gate[...] = (keep_in[:, left] + got_gate[...].astype(F32)).astype(BF16)
    up[...] = (keep_in[:, right] + got_up[...].astype(F32)).astype(BF16)
    down[...] = (keep_down[...] + got_down[...].astype(F32)).astype(BF16)
    done[...] = jnp.zeros_like(done)


def finish_kernel(place, *refs):
    ids, grad_tokens, grad_gates = refs[-3:]
    total = refs[0][...].astype(F32)
    for part in refs[1:-3]:
        total = total + part[...].astype(F32)
    half = grad_tokens.shape[1] // 2
    lanes = total.shape[1] - 2 * half
    own, other = own_other(place, half)
    grad_tokens[:, own] = total[:, :half].astype(BF16)
    grad_tokens[:, other] = total[:, half : 2 * half].astype(BF16)
    gates = dot(unit_matrix(lanes), total[:, 2 * half :].astype(BF16), NT)
    names = ids[...]
    expert = lax.broadcasted_iota(jnp.int32, gates.shape, 0)
    row = lax.broadcasted_iota(jnp.int32, names.shape, 0)
    out = jnp.zeros(names.shape, F32)
    for k in range(names.shape[0]):
        picked = jnp.sum(jnp.where(names[k : k + 1, :] == expert, gates, 0.0), 0, keepdims=True)
        out = jnp.where(row == k, picked, out)
    grad_gates[...] = out.astype(BF16)


def call(kernel, outs, place, *args, after=(), small=True, arrives=0, leaves=0, flops=0, limit=2):
    used = len(args)
    limit = (limit if small else 56) * 2**20
    if small:
        args = [
            pltpu.with_memory_space_constraint(x, pltpu.VMEM) if i < used - arrives else x
            for i, x in enumerate(args)
        ]
    out_shape = [
        pltpu.VMEM(s, d) if small and i >= leaves else jax.ShapeDtypeStruct(s, d)
        for i, (s, d) in enumerate(outs)
    ]

    scalars = () if place is None else (place,)
    read = len(scalars) + used

    def run(*refs):
        kernel(*refs[:read], *refs[read + len(after) :])

    vmem = pl.BlockSpec(memory_space=pltpu.VMEM)
    return pl.pallas_call(
        run,
        out_shape=out_shape,
        in_specs=[pl.BlockSpec(memory_space=pltpu.SMEM)] * len(scalars)
        + [vmem] * used
        + [pl.BlockSpec(memory_space=pl.ANY)] * len(after),
        out_specs=[vmem] * len(outs),
        compiler_params=pltpu.CompilerParams(vmem_limit_bytes=limit),
        cost_estimate=pl.CostEstimate(flops=flops, bytes_accessed=0, transcendentals=0),
        name=kernel.__name__.replace("<lambda>", "weight_kernel"),
    )(*scalars, *args, *after)


def chip_bits(chip_count):
    bits = []
    bit = chip_count // 2
    while bit:
        bits.append(bit)
        bit //= 2
    return (bits, bits[:-2] + bits[-2:][::-1])


def body(tokens, cotangent, expert_ids, gate_probs, gate_half, up_half, down_half):
    chip_count = lax.axis_size("expert") * lax.axis_size("chip")
    tok_rows, features = tokens.shape
    half = features // 2
    width = gate_half.shape[2]
    lanes = -(-chip_count // 128) * 128
    member = lax.axis_index("core")
    own_expert = lax.axis_index("expert") * lax.axis_size("chip") + lax.axis_index("chip")
    place = jnp.stack([member, own_expert]).astype(jnp.int32)
    bits = chip_bits(chip_count)
    far = len(bits[0]) - 4
    small = far == 0

    def exchange(x, offsets):
        pairs = [
            (2 * chip + core, 2 * (chip ^ offsets[core]) + core)
            for chip in range(chip_count)
            for core in range(2)
        ]
        return lax.ppermute(x, DEVICES, pairs)

    steps = list(zip(*bits))
    near_a, near_b = steps[-2:]
    up_two, up_one = steps[far][0], steps[far + 1][0]

    before = []

    def run(kernel, outs, place, *args, **kwargs):
        results = call(kernel, outs, place, *args, after=tuple(before), small=small, **kwargs)
        before[:] = results[-1:]
        return results

    hbm = pl.BlockSpec(memory_space=pltpu.HBM)
    arguments = (tokens, cotangent, expert_ids.T, gate_probs.T)
    block = pl.pallas_call(
        prepare_kernel,
        out_shape=pltpu.VMEM((tok_rows, 2 * features + lanes), BF16),
        in_specs=[hbm] * 4,
        out_specs=pl.BlockSpec(memory_space=pltpu.VMEM),
        scratch_shapes=[
            pltpu.VMEM(expert_ids.shape[::-1], jnp.int32),
            pltpu.VMEM(gate_probs.shape[::-1], BF16),
            pltpu.SemaphoreType.DMA((4,)),
        ],
        name="prepare_kernel",
    )(*(pltpu.with_memory_space_constraint(x, pltpu.HBM) for x in arguments))

    for step in steps[:far]:
        block = jnp.concatenate([block, exchange(block, step)], 0)

    offsets = (up_two, up_one, up_one ^ up_two)
    rows = block.shape[0]
    columns = features + lanes

    gate_own, up_own, down_own = gate_half[0], up_half[0], down_half[0]
    gate_other, up_other, down_other = swap_core(gate_own), swap_core(up_own), swap_core(down_own)
    weights = [gate_own, gate_other, up_own, up_other, down_own, down_other]
    numbers, saved = [], []

    def at_offset(x, i):
        return exchange(x, (offsets[i], offsets[i]))

    def join(first, second, flops=0):
        shape = (2 * first.shape[0], first.shape[1])
        return run(join_kernel, [(shape, BF16)], None, first, second, flops=flops)[0]

    def after_all(x, *others):
        before.extend(others)
        return run(pass_kernel, [(x.shape, BF16)], None, x)[0]

    def expert(*blocks):
        number, count = len(blocks), blocks[0].shape[0]
        row_grads, grads, hidden = run(
            expert_kernel,
            [
                ((number * count, columns), BF16),
                ((number, count, 2 * width), BF16),
                ((number, count, width), BF16),
            ],
            place, *blocks, *weights, limit=6, flops=6 * 10**9,
        )
        numbers.append(number)
        saved.extend([*blocks, grads, hidden])
        return row_grads

    def split(kept, got, types, flops=0):
        shape = (kept.shape[0] // 2, columns)
        return run(split_kernel, [(shape, t) for t in types], None, kept, got, flops=flops)

    def collect(total, part):
        return run(add_kernel, [(total.shape, F32)], None, total, part)[0]

    far_two = at_offset(block, 0)
    first_own = join(block, exchange(block, near_a))
    second_own = exchange(first_own, near_b)
    near_1 = at_offset(join(block, far_two, flops=1 * 10**9), 1)
    second_own = after_all(second_own)
    first_two = join(far_two, exchange(far_two, near_a))
    second_two = exchange(first_two, near_b)
    near_1 = after_all(near_1)
    got_near = exchange(near_1, near_a)
    weights[-1] = after_all(weights[-1])
    kept_0 = expert(first_own, first_two)
    first_1 = join(near_1, got_near)
    second_1 = exchange(first_1, near_b)
    give_0 = expert(second_own, second_two)
    kept_1 = expert(first_1)
    got_0 = exchange(after_all(give_0, second_1), near_b)
    got_1 = exchange(expert(second_1), near_b)
    kept_0, give = split(kept_0, got_0, (F32, BF16))
    got_0 = exchange(give, near_a)
    keep_in, keep_down, *gives = run(
        lambda *refs: weight_kernel(tuple(numbers), *refs),
        [
            ((half, 2 * width), F32),
            ((width, half), F32),
            ((half, width), BF16),
            ((half, width), BF16),
            ((width, half), BF16),
        ],
        place, *saved, limit=10, flops=6 * 10**9,
    )
    kept_1, give = split(kept_1, got_1, (F32, BF16))
    got_1 = exchange(give, near_a)
    total, give = split(kept_0, got_0, (F32, BF16))
    back_two = at_offset(give, 0)
    gots = [swap_core(give) for give in gives]
    give_one, give_both = split(kept_1, got_1, (BF16, BF16), flops=6 * 10**9)
    back_one, back_both = at_offset(give_one, 1), at_offset(give_both, 2)
    grad_gate, grad_up, grad_down, _ = run(
        settle_kernel,
        [((half, width), BF16), ((half, width), BF16), ((width, half), BF16), ((8, 128), F32)],
        None, keep_in, keep_down, *gots, leaves=3, limit=6,
    )
    total = collect(total, back_two)
    total = collect(total, back_both)

    parts = (total, back_one)
    if far:
        total = total + back_one.astype(F32)
        for step in reversed(steps[:far]):
            middle = total.shape[0] // 2
            total = total[:middle] + exchange(total[middle:].astype(BF16), step).astype(F32)
        parts = (total,)
    grad_tokens, grad_gates = run(
        finish_kernel,
        [((tok_rows, features), BF16), (expert_ids.shape[::-1], BF16)],
        place, *parts, expert_ids.T, arrives=1, leaves=2,
    )
    return grad_tokens, grad_gates.T, grad_gate[None], grad_up[None], grad_down[None]


def solution(mesh):
    shape = mesh.shape
    devices = mesh.devices.reshape(shape["dom"], shape["expert"], shape["dp"] // 2, 2)
    fine = Mesh(devices, ("dom", "expert", "chip", "core"))
    every = ("dom", "expert", "chip", "core")
    flat, cube = P(every, None), P(every, None, None)
    return jax.shard_map(
        body,
        mesh=fine,
        in_specs=(flat, flat, flat, flat, cube, cube, cube),
        out_specs=(flat, flat, cube, cube, cube),
        check_vma=False,
    )
```
